32 devices in a mesh: section: 2 (over x), batch: 16 (over z, y, core).
Axes of the slice: x: 2, y: 2, z: 4, core: 2. Of those that a mesh axis runs over, the one named last changes fastest.
Arguments:
- latents: bfloat16 [12288, 512], P('batch'), may hold values from 0 to 0.25
- actions: bfloat16 [2, 12288, 6], P('section', 'batch'), may hold values from -1 to 1
- tasks: int32 [12288], P('batch'), may hold values from 0 to 79
- masks: int32 [2, 12288], P('section', 'batch'), may hold values 0 or 1
- reward_bins: int32 [2, 12288], P('section', 'batch'), may hold values from 0 to 99
- reward_frac: float32 [2, 12288], P('section', 'batch'), may hold values from 0 to 1
- value_bins: int32 [2, 12288], P('section', 'batch'), may hold values from 0 to 99
- value_frac: float32 [2, 12288], P('section', 'batch'), may hold values from 0 to 1
- targets: bfloat16 [2, 12288, 512], P('section', 'batch'), may hold values from 0 to 0.25
- task_table: bfloat16 [80, 96], replicated, may hold values from -6 to 6
- w_latent: bfloat16 [2, 512, 7168], P('section'), may hold values from -2 to 2
- w_action: bfloat16 [2, 6, 7168], P('section'), may hold values from -4 to 4
- w_task: bfloat16 [2, 96, 7168], P('section'), may hold values from -0.625 to 0.625
- gain_one: float32 [2, 7168], P('section'), may hold values from 0.5 to 1.5
- shift_one: float32 [2, 7168], P('section'), may hold values from -1.8 to 1.8
- w_hidden: bfloat16 [2, 7, 1024, 1024], P('section'), may hold values from -0.1875 to 0.1875
- gain_two: float32 [2, 7, 1024], P('section'), may hold values from 0.5 to 1.5
- shift_two: float32 [2, 7, 1024], P('section'), may hold values from -1.8 to 1.8
- w_next: bfloat16 [2, 1024, 512], P('section'), may hold values from -0.1875 to 0.1875
- bias_next: float32 [2, 512], P('section'), may hold values from -3 to 3
- gain_three: float32 [2, 512], P('section'), may hold values from 0.5 to 1.5
- shift_three: float32 [2, 512], P('section'), may hold values from -1.8 to 1.8
- w_head: bfloat16 [2, 6, 1024, 101], P('section'), may hold values from -0.375 to 0.375
- bias_head: float32 [2, 6, 101], P('section'), may hold values from -3 to 3
Outputs:
- latents_out: bfloat16 [2, 12288, 512], P('section', 'batch')
- latent_grads: bfloat16 [2, 12288, 512], P('section', 'batch')
- step_loss: float32 [2], P('section')
- w_latent_grad: float32 [2, 512, 7168], P('section', None, 'batch')
- w_action_grad: float32 [2, 6, 7168], P('section', None, 'batch')
- w_task_grad: float32 [2, 96, 7168], P('section', None, 'batch')
- gain_one_grad: float32 [2, 7168], P('section', 'batch')
- shift_one_grad: float32 [2, 7168], P('section', 'batch')
- w_hidden_grad: float32 [2, 7, 1024, 1024], P('section', None, None, 'batch')
- gain_two_grad: float32 [2, 7, 1024], P('section', None, 'batch')
- shift_two_grad: float32 [2, 7, 1024], P('section', None, 'batch')
- w_next_grad: float32 [2, 1024, 512], P('section', 'batch')
- bias_next_grad: float32 [2, 512], P('section', 'batch')
- gain_three_grad: float32 [2, 512], P('section', 'batch')
- shift_three_grad: float32 [2, 512], P('section', 'batch')
- w_head_grad: float32 [2, 6, 1024, 101], P('section', None, 'batch')
- bias_head_grad: float32 [2, 6, 101], P('section')
- table_grad: float32 [80, 96], replicated
The draws below stay inside these ranges and needn't reach their ends.
All inputs are finite; a program needn't handle non-finite values. No bound on the sum of `masks` on one device may be relied on, other than what follows from the above.
Results may differ from the reference program's by a relative error of at most 0.009.
Values may be sent and summed in bfloat16 or wider, within the bound.
A program may use at most 384 MiB of HBM per device.

```python
import math
import jax
import jax.numpy as jnp
from jax import lax

LATENT = 512
HIDDEN_SIZE = 1024
TASK_DIM = 96
BINS = 101
TASKS = 80
ACT = 6
HEADS = 5
GROUP = 8
SECTIONS = 2
TRANS = 12288


def plant(result, own_key, smallest, top_value):
    longest = result.shape.index(max(result.shape))
    spots = []
    for shift in (0, 1):
        where = [jax.random.randint(jax.random.fold_in(own_key, axis), (), 0, length) for axis, length in enumerate(result.shape)]
        where[longest] = (where[longest] + shift) % result.shape[longest]
        spots.append(tuple(where))
    return result.at[spots[0]].set(smallest).at[spots[1]].set(top_value)


def levels(own_key, shape, shards, smallest, top_value):
    level = 1.0
    for dim, blocks in shards:
        draws = jax.random.uniform(jax.random.fold_in(jax.random.fold_in(own_key, 6), dim), (blocks,), jnp.float32, smallest / len(shards), top_value / len(shards))
        level = level * jnp.repeat(jnp.exp(draws), shape[dim] // blocks).reshape((-1,) + (1,) * (len(shape) - 1 - dim))
    return level


def gaussian(key, shape, deviation, most, split=(), kind=jnp.bfloat16):
    level = levels(key, shape, split, -0.22, 0.18) if split else 1.0
    values = jax.random.normal(key, shape, jnp.float32) * deviation * level
    return jnp.minimum(jnp.maximum(values, -most), most).astype(kind)


def setup_inputs(seed: int = 0) -> dict:
    arg_keys = jax.random.split(jax.random.key(seed), 25)
    return {
        "latents": jnp.clip(0.25 * jax.random.uniform(arg_keys[0], (TRANS, LATENT), jnp.float32) ** levels(arg_keys[0], (TRANS, LATENT), ((0, 16),), -0.2, 0.2), 0.0, 0.25).astype(jnp.bfloat16),
        "actions": jnp.clip(jax.random.uniform(arg_keys[1], (SECTIONS, TRANS, ACT), jnp.float32, -1.0, 1.0) * levels(arg_keys[1], (SECTIONS, TRANS, ACT), ((0, 2), (1, 16)), -0.4, 0.0), -1.0, 1.0).astype(jnp.bfloat16),
        "tasks": plant(jax.random.randint(arg_keys[2], (TRANS,), 0, TASKS), jax.random.fold_in(arg_keys[2], 1), 0, TASKS - 1).astype(jnp.int32),
        "masks": plant((jax.random.randint(arg_keys[3], (SECTIONS, TRANS), 0, 4) < 3).astype(jnp.int32), jax.random.fold_in(arg_keys[3], 1), 0, 1),
        "reward_bins": plant(jax.random.randint(arg_keys[4], (SECTIONS, TRANS), 0, BINS - 1), jax.random.fold_in(arg_keys[4], 1), 0, (BINS - 1) - 1).astype(jnp.int32),
        "reward_frac": jnp.clip(1.0 * jax.random.uniform(arg_keys[5], (SECTIONS, TRANS), jnp.float32) ** levels(arg_keys[5], (SECTIONS, TRANS), ((0, 2), (1, 16)), -0.2, 0.2), 0.0, 1.0),
        "value_bins": plant(jax.random.randint(arg_keys[6], (SECTIONS, TRANS), 0, BINS - 1), jax.random.fold_in(arg_keys[6], 1), 0, (BINS - 1) - 1).astype(jnp.int32),
        "value_frac": jnp.clip(1.0 * jax.random.uniform(arg_keys[7], (SECTIONS, TRANS), jnp.float32) ** levels(arg_keys[7], (SECTIONS, TRANS), ((0, 2), (1, 16)), -0.2, 0.2), 0.0, 1.0),
        "targets": jnp.clip(0.25 * jax.random.uniform(arg_keys[8], (SECTIONS, TRANS, LATENT), jnp.float32) ** levels(arg_keys[8], (SECTIONS, TRANS, LATENT), ((0, 2), (1, 16)), -0.2, 0.2), 0.0, 0.25).astype(jnp.bfloat16),
        "task_table": gaussian(arg_keys[9], (TASKS, TASK_DIM), 1.0, 6.0),
        "w_latent": gaussian(arg_keys[10], (SECTIONS, LATENT, (HEADS + 2) * HIDDEN_SIZE), 8 ** -0.5, 2.0, ((0, 2),)),
        "w_action": gaussian(arg_keys[11], (SECTIONS, ACT, (HEADS + 2) * HIDDEN_SIZE), 2 ** -0.5, 4.0, ((0, 2),)),
        "w_task": gaussian(arg_keys[12], (SECTIONS, TASK_DIM, (HEADS + 2) * HIDDEN_SIZE), TASK_DIM ** -0.5, 0.625, ((0, 2),)),
        "gain_one": jnp.clip(1.0 + 0.1 * jax.random.normal(arg_keys[13], (SECTIONS, (HEADS + 2) * HIDDEN_SIZE), jnp.float32), 0.5, 1.5),
        "shift_one": gaussian(arg_keys[14], (SECTIONS, (HEADS + 2) * HIDDEN_SIZE), 0.3, 1.8, ((0, 2),), jnp.float32),
        "w_hidden": gaussian(arg_keys[15], (SECTIONS, HEADS + 2, HIDDEN_SIZE, HIDDEN_SIZE), HIDDEN_SIZE ** -0.5, 0.1875, ((0, 2),)),
        "gain_two": jnp.clip(1.0 + 0.1 * jax.random.normal(arg_keys[16], (SECTIONS, HEADS + 2, HIDDEN_SIZE), jnp.float32), 0.5, 1.5),
        "shift_two": gaussian(arg_keys[17], (SECTIONS, HEADS + 2, HIDDEN_SIZE), 0.3, 1.8, ((0, 2),), jnp.float32),
        "w_next": gaussian(arg_keys[18], (SECTIONS, HIDDEN_SIZE, LATENT), HIDDEN_SIZE ** -0.5, 0.1875, ((0, 2),)),
        "bias_next": gaussian(arg_keys[19], (SECTIONS, LATENT), 0.5, 3.0, ((0, 2),), jnp.float32),
        "gain_three": jnp.clip(1.0 + 0.1 * jax.random.normal(arg_keys[20], (SECTIONS, LATENT), jnp.float32), 0.5, 1.5),
        "shift_three": gaussian(arg_keys[21], (SECTIONS, LATENT), 0.3, 1.8, ((0, 2),), jnp.float32),
        "w_head": gaussian(arg_keys[22], (SECTIONS, HEADS + 1, HIDDEN_SIZE, BINS), (HIDDEN_SIZE // 4) ** -0.5, 0.375, ((0, 2),)),
        "bias_head": gaussian(arg_keys[23], (SECTIONS, HEADS + 1, BINS), 0.5, 3.0, ((0, 2),), jnp.float32),
    }


RHO = 0.5
CONSISTENCY = 20.0
EPSILON = 1e-05
HIGH = lax.Precision.HIGHEST

@jax.custom_vjp
def low(v):
    return lax.optimization_barrier(v.astype(jnp.bfloat16)).astype(jnp.float32)

@jax.custom_vjp
def low_back(v):
    return v

def low_keep(v):
    return (low(v), None)

def low_pass(kept, grad):
    return (grad,)

def back_keep(v):
    return (v, None)

def back_low(kept, grad):
    return (low(grad),)
low.defvjp(low_keep, low_pass)
low_back.defvjp(back_keep, back_low)

def mish(values):
    return values * jnp.tanh(jax.nn.softplus(values))

def layer_norm(pre, gain, shift):
    centre = pre - lax.optimization_barrier(jnp.mean(pre, axis=-1, keepdims=True))
    spread = lax.optimization_barrier(jnp.mean(centre * centre, axis=-1, keepdims=True))
    return centre * lax.rsqrt(spread + EPSILON) * gain + shift

def norm_mish(pre, gain, shift):
    return mish(layer_norm(pre, gain, shift))

def simplex(pre):
    grouped = pre.reshape(pre.shape[0], pre.shape[1] // GROUP, GROUP)
    return jax.nn.softmax(grouped, axis=-1).reshape(pre.shape)

def tail(pre_next, logits, gain_three, shift_three, bins, fraction, value_bin, value_fraction, goal, weight):
    latent_next = simplex(layer_norm(pre_next, gain_three, shift_three))
    log_probs = jax.nn.log_softmax(logits, axis=-1)
    head_count = logits.shape[0]
    row_count = bins.shape[0]
    lower = jnp.concatenate([bins[None], jnp.broadcast_to(value_bin[None], (head_count - 1, row_count))], axis=0)
    upper = jnp.concatenate([fraction[None], jnp.broadcast_to(value_fraction[None], (head_count - 1, row_count))], axis=0)
    columns = lax.broadcasted_iota(jnp.int32, logits.shape, 2)
    two_hot = jnp.where(columns == lower[:, :, None], 1.0 - upper[:, :, None], 0.0)
    two_hot = two_hot + jnp.where(columns == lower[:, :, None] + 1, upper[:, :, None], 0.0)
    cross = -lax.optimization_barrier(jnp.sum(two_hot * log_probs, axis=-1))
    head_index = lax.broadcasted_iota(jnp.int32, (head_count, 1), 0)
    head_weight = jnp.where(head_index == 0, 1.0, 1.0 / (head_count - 1))
    cross_total = lax.optimization_barrier(jnp.sum(cross * head_weight, axis=0))
    differ = latent_next - goal
    consist = CONSISTENCY * lax.optimization_barrier(jnp.mean(differ * differ, axis=-1))
    return (latent_next, jnp.sum(weight * (cross_total + consist)))

def section_block(params, index, latent_in, acts, embedded, weight, bins, fraction, value_bin, value_fraction, goal):
    latent_w, action_w, task_w, gains_one, shifts_one, hidden_w, gains_two, shifts_two, next_w, next_b, gains_three, shifts_three, head_w, head_b = params
    row_count = latent_in.shape[0]
    branches = HEADS + 2
    pre_one = low_back(jnp.dot(latent_in, latent_w[index], precision=HIGH) + jnp.dot(acts, action_w[index], precision=HIGH) + jnp.dot(embedded, task_w[index], precision=HIGH))
    hidden_one = low(norm_mish(pre_one.reshape(row_count, branches, HIDDEN_SIZE), gains_one[index].reshape(branches, HIDDEN_SIZE), shifts_one[index].reshape(branches, HIDDEN_SIZE)))
    pre_two = low_back(jnp.einsum('rkh,khj->krj', hidden_one, hidden_w[index], precision=HIGH))
    hidden_two = low(norm_mish(pre_two, gains_two[index][:, None, :], shifts_two[index][:, None, :]))
    pre_next = low_back(jnp.dot(hidden_two[0], next_w[index], precision=HIGH) + next_b[index])
    logits = low_back(jnp.einsum('krh,khb->krb', hidden_two[1:], head_w[index], precision=HIGH) + head_b[index][:, None, :])
    return tail(pre_next, logits, gains_three[index], shifts_three[index], bins, fraction, value_bin, value_fraction, goal, weight)

def reference(latents, actions, tasks, masks, reward_bins, reward_frac, value_bins, value_frac, targets, task_table, w_latent, w_action, w_task, gain_one, shift_one, w_hidden, gain_two, shift_two, w_next, bias_next, gain_three, shift_three, w_head, bias_head):
    params = tuple((p.astype(jnp.float32) for p in (w_latent, w_action, w_task, gain_one, shift_one, w_hidden, gain_two, shift_two, w_next, bias_next, gain_three, shift_three, w_head, bias_head)))
    table_full = task_table.astype(jnp.float32)
    start_latent = latents.astype(jnp.float32)
    probes = jnp.zeros((SECTIONS, TRANS, LATENT), jnp.float32)
    block_rows = math.gcd(TRANS, 4096)
    blocks = TRANS // block_rows

    def by_block(array):
        moved = array.reshape((SECTIONS, blocks, block_rows) + array.shape[2:])
        return jnp.swapaxes(moved, 0, 1)
    action_blocks = by_block(actions.astype(jnp.float32))
    mask_blocks = by_block(masks)
    bin_blocks = by_block(reward_bins)
    frac_blocks = by_block(reward_frac.astype(jnp.float32))
    vbin_blocks = by_block(value_bins)
    vfrac_blocks = by_block(value_frac.astype(jnp.float32))
    goal_blocks = by_block(targets.astype(jnp.float32))
    task_blocks = tasks.reshape(blocks, block_rows)
    task_ids = jnp.arange(TASKS, dtype=jnp.int32)

    def objective(params, table_full, start_latent, probes):
        probe_blocks = by_block(probes)
        latent_blocks = start_latent.reshape(blocks, block_rows, LATENT)

        def advance(totals, pieces):
            latent_b, probe_b, action_b, task_b, mask_b, bin_b, frac_b, vbin_b, vfrac_b, goal_b = pieces
            one_hot = (task_b[:, None] == task_ids[None, :]).astype(jnp.float32)
            embedded = jnp.dot(one_hot, table_full, precision=HIGH)
            current = latent_b
            outputs = []
            losses = []
            for index in range(SECTIONS):
                latent_in = low_back(current + probe_b[index])
                weight = RHO ** index * mask_b[index].astype(jnp.float32)
                latent_next, loss_part = section_block(params, index, latent_in, action_b[index], embedded, weight, bin_b[index], frac_b[index], vbin_b[index], vfrac_b[index], goal_b[index])
                current = low(latent_next)
                outputs.append(current)
                losses.append(loss_part)
            return (totals + jnp.stack(losses), jnp.stack(outputs))
        totals, outputs = lax.scan(jax.checkpoint(advance), jnp.zeros((SECTIONS,), jnp.float32), (latent_blocks, probe_blocks, action_blocks, task_blocks, mask_blocks, bin_blocks, frac_blocks, vbin_blocks, vfrac_blocks, goal_blocks))
        return (jnp.sum(totals), (totals, outputs))
    unused, backward, extras = jax.vjp(objective, params, table_full, start_latent, probes, has_aux=True)
    totals, outputs = extras
    param_grads, table_grads, unused_latent, probe_grads = backward(jnp.float32(1.0))
    scale = 1.0 / TRANS
    latents_out = jnp.swapaxes(outputs, 0, 1).reshape(SECTIONS, TRANS, LATENT).astype(jnp.bfloat16)
    latent_grads = probe_grads.astype(jnp.bfloat16)
    step_loss = totals * scale
    scaled = tuple((g * scale for g in param_grads))
    return (latents_out, latent_grads, step_loss, scaled[0], scaled[1], scaled[2], scaled[3], scaled[4], scaled[5], scaled[6], scaled[7], scaled[8], scaled[9], scaled[10], scaled[11], scaled[12], scaled[13], table_grads * scale)
```

```python
import functools

import jax
import jax.numpy as jnp
from jax import lax
from jax.experimental import pallas as pl
from jax.experimental.pallas import tpu as pltpu
from jax.sharding import PartitionSpec as P

F32 = jnp.float32
BF16 = jnp.bfloat16
GROUP = 8
RHO = 0.5
CONSISTENCY = 20.0
EPSILON = 1e-05
HIGH = lax.Precision.HIGHEST
LANES = 128
TILE = 256
CHUNK = 16
CAP = 20.0
VMEM_BYTES = 58 * 2**20


def dot(left, right, contract):
    return lax.dot_general(
        left, right, ((contract[:1], contract[1:]), ((), ())), preferred_element_type=F32
    )


def nn(left, right):
    return dot(left, right, (1, 0))


def nt(left, right):
    return dot(left, right, (1, 1))


def tn(left, right):
    return dot(left, right, (0, 0))


def norm_forward(pre, gain, shift, hidden, slope, unit, inverse, row):
    width = pre.shape[1]
    for start in range(0, TILE, CHUNK):
        out = slice(row + start, row + start + CHUNK)
        x = pre[start : start + CHUNK, :]
        x = x - jnp.sum(x, axis=-1, keepdims=True) * (1.0 / width)
        r = lax.rsqrt(jnp.sum(x * x, axis=-1, keepdims=True) * (1.0 / width) + EPSILON)
        if inverse is not None:
            inverse[out, :] = r
        for q in range(0, width, 256):
            cols = slice(q, q + 256)
            y = x[:, cols] * r
            v = y * gain[:, cols] + shift[:, cols]
            e = jnp.exp(jnp.minimum(v, CAP))
            k = e * (e + 2.0)
            d = 1.0 / (k + 2.0)
            t = k * d
            hidden[out, cols] = (v * t).astype(BF16)
            if slope is not None:
                slope[out, cols] = (t + (4.0 * v * d) * ((k - e) * d)).astype(BF16)
                unit[out, cols] = y.astype(BF16)


def norm_backward(grad, gain, slope, unit, inverse, result, gain_sum, shift_sum, row):
    width = grad.shape[1]
    gains = shifts = None
    for start in range(0, TILE, CHUNK):
        out = slice(row + start, row + start + CHUNK)
        y = unit[out, :].astype(F32)
        dv = grad[start : start + CHUNK, :] * slope[out, :].astype(F32)
        dvy = dv * y
        g = dvy[:8] + dvy[8:]
        s = dv[:8] + dv[8:]
        gains = g if gains is None else gains + g
        shifts = s if shifts is None else shifts + s
        row_gain = gain[...]
        dx = dv * row_gain
        mean = jnp.sum(dx, axis=-1, keepdims=True) * (1.0 / width)
        along = jnp.sum(dvy * row_gain, axis=-1, keepdims=True) * (1.0 / width)
        result[out, :] = ((dx - mean - y * along) * inverse[out, :]).astype(BF16)
    gain_sum[...] += gains
    shift_sum[...] += shifts


def group_matrix():
    i = lax.broadcasted_iota(jnp.int32, (256, 256), 0) // GROUP
    j = lax.broadcasted_iota(jnp.int32, (256, 256), 1) // GROUP
    return jnp.where(i == j, 1.0, 0.0).astype(BF16)


def group_sum(values, ones):
    parts = []
    for q in range(0, values.shape[1], 256):
        v = values[:, q : q + 256]
        high = v.astype(BF16)
        low = (v - high.astype(F32)).astype(BF16)
        parts.append(nn(high, ones) + nn(low, ones))
    return jnp.concatenate(parts, axis=1)


def simplex_forward(pre, gain, shift, ones):
    width = pre.shape[1]
    x = pre - jnp.sum(pre, axis=-1, keepdims=True) * (1.0 / width)
    r = lax.rsqrt(jnp.sum(x * x, axis=-1, keepdims=True) * (1.0 / width) + EPSILON)
    y = x * r
    e = jnp.exp(y * gain + shift)
    return y, r, e / group_sum(e, ones)


def tile_rows(i):
    return slice(i * TILE, (i + 1) * TILE)


def staged(count, first, then):
    first(0)
    for i in range(count):
        if i + 1 < count:
            first(i + 1)
        then(i)


def forward_pair(x, wl, wta, g1, s1, w2, g2, s2, pre, h1, m1, x1, r1, h2, m2, x2, r2):
    count = x.shape[0] // TILE
    latent = wl.shape[0]

    def one(i):
        r = tile_rows(i)
        pre[i][...] = nn(x[r, :latent], wl[...]) + nn(x[r, latent:], wta[...])

    def two(i):
        pre[i][...] = nn(h1[tile_rows(i), :], w2[...])

    staged(count, one, lambda i: norm_forward(pre[i], g1, s1, h1, m1, x1, r1, i * TILE))
    staged(count, two, lambda i: norm_forward(pre[i], g2, s2, h2, m2, x2, r2, i * TILE))


def backward_pair(
    x, wl, wta, g1, w2, g2, pre, m1, x1, r1, m2, x2, r2, d1, d2, back_in,
    dx, add_dx, dg1, ds1, dg2, ds2,
):
    count = x.shape[0] // TILE
    latent = wl.shape[0]

    def one(i):
        pre[i][...] = nt(d2[tile_rows(i), :], w2[...])

    staged(
        count, back_in, lambda i: norm_backward(pre[i], g2, m2, x2, r2, d2, dg2, ds2, i * TILE)
    )
    staged(count, one, lambda i: norm_backward(pre[i], g1, m1, x1, r1, d1, dg1, ds1, i * TILE))
    for i in range(count):
        r = tile_rows(i)
        main, side = nt(d1[r, :], wl[...]), nt(d1[r, :], wta[...])
        if add_dx:
            dx[r, :latent] += main
            dx[r, latent:] += side
        else:
            dx[r, :latent] = main
            dx[r, latent:] = side


def weight_grads(x, h1, d1, d2, tail_left, tail_right, u):
    hidden = h1.shape[1]
    width = x.shape[1]
    for n in range(0, hidden, 256):
        cols = slice(n, n + 256)
        u[cols, :hidden] = tn(d2[:, cols], h1[...]).astype(BF16)
        u[cols, hidden : hidden + width] = tn(d1[:, cols], x[...]).astype(BF16)
        u[cols, hidden + width :] = tn(tail_left[:, cols], tail_right[...]).astype(BF16)


def heads_kernel(
    x, wl, wta, g1, s1, w2, g2, s2, wh, bh, cond,
    u, dx, head_bias, loss, small,
    p0, p1, p2, logits, h1, h2, m1, m2, x1, x2, r1, r2, d1, d2, dl,
):
    pre = (p0, p1, p2)
    w2, wh, g1, s1, g2, s2, bh, cond, u = (
        ref.at[0] for ref in (w2, wh, g1, s1, g2, s2, bh, cond, u)
    )
    sums = [small.at[0, pl.ds(8 * i, 8)] for i in range(4)]
    small[...] = jnp.zeros_like(small)
    head_bias[...] = jnp.zeros_like(head_bias)

    @pl.when(pl.program_id(0) == 0)
    def _():
        dx[...] = jnp.zeros_like(dx)
        loss[...] = jnp.zeros_like(loss)

    forward_pair(x, wl, wta, g1, s1, w2, g2, s2, pre, h1, m1, x1, r1, h2, m2, x2, r2)

    def tail(i):
        r = tile_rows(i)
        v = nn(h2[r, :], wh[...]) + bh[...]
        given = cond[r, :]
        lower, upper, weight = given[:, 0:1], given[:, 1:2], given[:, 2:3]
        v = v - jnp.max(v, axis=-1, keepdims=True)
        e = jnp.exp(v)
        total = jnp.sum(e, axis=-1, keepdims=True)
        at = lax.broadcasted_iota(jnp.int32, v.shape, 1).astype(F32)
        hot = jnp.where(at == lower, 1.0 - upper, 0.0) + jnp.where(at == lower + 1.0, upper, 0.0)
        loss[r, :] += weight * (jnp.log(total) - jnp.sum(hot * v, axis=-1, keepdims=True))
        grad = (weight * (e / total - hot)).astype(BF16)
        dl[r, :] = grad
        head_bias[0, 0:1, :] += jnp.sum(grad.astype(F32), axis=0, keepdims=True)

    for i in range(x.shape[0] // TILE):
        tail(i)

    def back_in(i):
        pre[i][...] = nt(dl[tile_rows(i), :], wh[...])

    backward_pair(
        x, wl, wta, g1, w2, g2, pre, m1, x1, r1, m2, x2, r2, d1, d2, back_in, dx, True, *sums
    )
    weight_grads(x, h1, d1, d2, h2, dl, u)


def scratch(rows, hidden, forward=False):
    def hold():
        return pltpu.VMEM((rows, hidden), BF16)

    if forward:
        return [pltpu.VMEM((TILE, hidden), F32)] * 3 + [hold(), hold()]
    return (
        [pltpu.VMEM((TILE, hidden), F32)] * 3
        + [hold() for _ in range(6)]
        + [pltpu.VMEM((rows, 1), F32)] * 2
        + [hold(), hold()]
    )


def heads(x, w_latent, wta, g1, s1, w_hidden, g2, s2, wh, bh, cond):
    rows, width = x.shape
    latent = w_latent.shape[0]
    count, hidden = wh.shape[0], w_hidden.shape[-1]
    held = scratch(rows, hidden)
    row = pl.BlockSpec((1, 1, hidden), lambda k: (k + 1, 0, 0))
    return pl.pallas_call(
        heads_kernel,
        grid=(count,),
        in_specs=[
            pl.BlockSpec((rows, width), lambda k: (0, 0)),
            pl.BlockSpec((latent, hidden), lambda k: (0, k + 1)),
            pl.BlockSpec((LANES, hidden), lambda k: (0, k + 1)),
            row,
            row,
            pl.BlockSpec((1, hidden, hidden), lambda k: (k + 1, 0, 0)),
            row,
            row,
            pl.BlockSpec((1, hidden, LANES), lambda k: (k, 0, 0)),
            pl.BlockSpec((1, 1, LANES), lambda k: (k, 0, 0)),
            pl.BlockSpec((1, rows, 8), lambda k: (jnp.minimum(k, 1), 0, 0)),
        ],
        out_shape=[
            jax.ShapeDtypeStruct((count, hidden, hidden + width + LANES), BF16),
            jax.ShapeDtypeStruct((rows, width), F32),
            jax.ShapeDtypeStruct((count, 8, LANES), F32),
            jax.ShapeDtypeStruct((rows, 1), F32),
            jax.ShapeDtypeStruct((count, 32, hidden), F32),
        ],
        out_specs=[
            pl.BlockSpec((1, hidden, hidden + width + LANES), lambda k: (k, 0, 0)),
            pl.BlockSpec((rows, width), lambda k: (0, 0)),
            pl.BlockSpec((1, 8, LANES), lambda k: (k, 0, 0)),
            pl.BlockSpec((rows, 1), lambda k: (0, 0)),
            pl.BlockSpec((1, 32, hidden), lambda k: (k, 0, 0)),
        ],
        scratch_shapes=held[:3]
        + [pltpu.VMEM((rows, LANES), F32)]
        + held[3:]
        + [pltpu.VMEM((rows, LANES), BF16)],
        compiler_params=pltpu.CompilerParams(vmem_limit_bytes=VMEM_BYTES),
    )(x, w_latent, wta, g1, s1, w_hidden, g2, s2, wh, bh, cond)


def dynamics_specs(rows, width, latent, hidden):
    row = pl.BlockSpec((1, 1, hidden), lambda k: (0, 0, 0))
    short = pl.BlockSpec((1, latent), lambda k: (0, 0))
    return [
        pl.BlockSpec((rows, width), lambda k: (0, 0)),
        pl.BlockSpec((latent, hidden), lambda k: (0, 0)),
        pl.BlockSpec((LANES, hidden), lambda k: (0, 0)),
        row,
        row,
        pl.BlockSpec((1, hidden, hidden), lambda k: (0, 0, 0)),
        row,
        row,
        pl.BlockSpec((hidden, latent), lambda k: (0, 0)),
        short,
        short,
        short,
    ]


def rollout_kernel(
    x, wl, wta, g1, s1, w2, g2, s2, wn, bn, g3, s3, z_out, p0, p1, p2, h1, h2
):
    pre = (p0, p1, p2)
    w2, g1, s1, g2, s2 = (ref.at[0] for ref in (w2, g1, s1, g2, s2))
    ones = group_matrix()
    none = (None, None, None)
    forward_pair(x, wl, wta, g1, s1, w2, g2, s2, pre, h1, *none, h2, *none)
    for i in range(x.shape[0] // TILE):
        for start in range(i * TILE, (i + 1) * TILE, 64):
            r = slice(start, start + 64)
            v = nn(h2[r, :], wn[...]) + bn[...]
            z_out[r, :] = simplex_forward(v, g3[...], s3[...], ones)[2].astype(BF16)


def rollout(x, w_latent, wta, g1, s1, w_hidden, g2, s2, wn, bn, g3, s3):
    rows, width = x.shape
    latent, hidden = w_latent.shape[0], w_hidden.shape[-1]
    return pl.pallas_call(
        rollout_kernel,
        grid=(1,),
        in_specs=dynamics_specs(rows, width, latent, hidden),
        out_shape=jax.ShapeDtypeStruct((rows, latent), BF16),
        out_specs=pl.BlockSpec((rows, latent), lambda k: (0, 0)),
        scratch_shapes=scratch(rows, hidden, True),
        compiler_params=pltpu.CompilerParams(vmem_limit_bytes=VMEM_BYTES),
    )(x, w_latent, wta, g1, s1, w_hidden, g2, s2, wn, bn, g3, s3)


def dynamics_kernel(
    x, wl, wta, g1, s1, w2, g2, s2, wn, bn, g3, s3, goal, weights, upstream,
    u, dx, z_out, loss, small, small3,
    p0, p1, p2, pre3, h1, h2, m1, m2, x1, x2, r1, r2, d1, d2, d3,
):
    pre = (p0, p1, p2)
    w2, g1, s1, g2, s2 = (ref.at[0] for ref in (w2, g1, s1, g2, s2))
    sums = [small.at[pl.ds(8 * i, 8)] for i in range(4)]
    small[...] = jnp.zeros_like(small)
    ones = group_matrix()
    width = wn.shape[1]
    forward_pair(x, wl, wta, g1, s1, w2, g2, s2, pre, h1, m1, x1, r1, h2, m2, x2, r2)
    totals = [None, None, None]
    count = x.shape[0] // TILE
    for i in range(count):
        r = tile_rows(i)
        pre3[r, :] = nn(h2[r, :], wn[...]) + bn[...]
    for start in range(0, x.shape[0], 64):
        r = slice(start, start + 64)
        y, inverse, z = simplex_forward(pre3[r, :], g3[...], s3[...], ones)
        z_out[r, :] = z.astype(BF16)
        differ = z - goal[r, :].astype(F32)
        weight = weights[r, :]
        loss[r, :] = weight * (
            CONSISTENCY / width * jnp.sum(differ * differ, axis=-1, keepdims=True)
        )
        grad = upstream[r, :].astype(F32) + weight * (2.0 * CONSISTENCY / width) * differ
        grad = grad * z
        dv = grad - z * group_sum(grad, ones)
        dvy = dv * y
        dy = dv * g3[...]
        mean = jnp.sum(dy, axis=-1, keepdims=True) * (1.0 / width)
        along = jnp.sum(dy * y, axis=-1, keepdims=True) * (1.0 / width)
        result = ((dy - mean - y * along) * inverse).astype(BF16)
        d3[r, :] = result
        for q, part in enumerate((dvy, dv, result.astype(F32))):
            part = functools.reduce(jnp.add, [part[s : s + 8] for s in range(0, 64, 8)])
            totals[q] = part if totals[q] is None else totals[q] + part
    for q in range(3):
        small3[8 * q : 8 * q + 8, :] = totals[q]

    def back_in(i):
        pre[i][...] = nt(d3[tile_rows(i), :], wn[...])

    backward_pair(
        x, wl, wta, g1, w2, g2, pre, m1, x1, r1, m2, x2, r2, d1, d2, back_in, dx, False, *sums
    )
    weight_grads(x, h1, d1, d2, h2, d3, u)


def dynamics(
    x, w_latent, wta, g1, s1, w_hidden, g2, s2, wn, bn, g3, s3, goal, weights, upstream
):
    rows, width = x.shape
    latent, hidden = w_latent.shape[0], w_hidden.shape[-1]
    held = scratch(rows, hidden)

    def whole(shape):
        return pl.BlockSpec(shape, lambda k: (0, 0))

    shapes = [
        ((hidden, hidden + width + latent), BF16),
        ((rows, width), F32),
        ((rows, latent), BF16),
        ((rows, 1), F32),
        ((32, hidden), F32),
        ((24, latent), F32),
    ]
    return pl.pallas_call(
        dynamics_kernel,
        grid=(1,),
        in_specs=dynamics_specs(rows, width, latent, hidden)
        + [whole((rows, latent)), whole((rows, 1)), whole((rows, latent))],
        out_shape=[jax.ShapeDtypeStruct(*s) for s in shapes],
        out_specs=[whole(s[0]) for s in shapes],
        scratch_shapes=held[:3]
        + [pltpu.VMEM((rows, latent), F32)]
        + held[3:]
        + [pltpu.VMEM((rows, latent), BF16)],
        compiler_params=pltpu.CompilerParams(vmem_limit_bytes=VMEM_BYTES),
    )(x, w_latent, wta, g1, s1, w_hidden, g2, s2, wn, bn, g3, s3, goal, weights, upstream)


def on_device(
    latents, actions, tasks, masks, reward_bins, reward_frac, value_bins, value_frac, targets,
    task_table, w_latent, w_action, w_task, gain_one, shift_one, w_hidden, gain_two, shift_two,
    w_next, bias_next, gain_three, shift_three, w_head, bias_head,
):
    section = lax.axis_index("section")
    device = lax.axis_index("batch")
    devices = lax.axis_size("batch")
    sections = lax.axis_size("section")
    rows, latent = latents.shape
    branches, hidden = w_hidden.shape[1], w_hidden.shape[-1]
    heads_count, bins = w_head.shape[1], w_head.shape[-1]
    tasks_count, task_dim = task_table.shape
    act = actions.shape[-1]
    scale = 1.0 / (rows * devices)
    rho = jnp.where(section == 0, 1.0, RHO).astype(F32)
    spare = LANES - task_dim - act

    ids = lax.broadcasted_iota(jnp.int32, (1, tasks_count), 1)
    one_hot = (tasks[:, None] == ids).astype(BF16)
    embedded = nn(one_hot, task_table).astype(BF16)
    extra = jnp.concatenate([embedded, actions[0], jnp.zeros((rows, spare), BF16)], axis=1)
    wta = jnp.concatenate(
        [w_task[0], w_action[0], jnp.zeros((spare, branches * hidden), BF16)], axis=0
    )
    weight = rho * masks[0].astype(F32)
    wide = LANES - bins
    wh = jnp.pad(w_head[0], ((0, 0), (0, 0), (0, wide)))
    bh = jnp.pad(bias_head[0], ((0, 0), (0, wide)), constant_values=-1e30)[:, None, :]
    none = jnp.zeros((2, rows), F32)
    cond = jnp.stack(
        [
            jnp.stack([reward_bins[0], value_bins[0]]).astype(F32),
            jnp.stack([reward_frac[0], value_frac[0]]),
            jnp.stack([weight, weight / (heads_count - 1)]),
        ]
        + [none] * 5,
        axis=-1,
    )
    g1 = gain_one[0].reshape(branches, 1, hidden)
    s1 = shift_one[0].reshape(branches, 1, hidden)
    g2 = gain_two[0][:, None, :]
    s2 = shift_two[0][:, None, :]
    shared = (w_latent[0], wta, g1, s1, w_hidden[0], g2, s2)
    last = (w_next[0], bias_next, gain_three, shift_three)

    first = rollout(jnp.concatenate([latents, extra], axis=1), *shared, *last)
    received = lax.ppermute(first, "section", [(i, i + 1) for i in range(sections - 1)])
    x = jnp.concatenate([jnp.where(section == 0, latents, received), extra], axis=1)
    u_heads, dx_heads, head_bias, loss, small = heads(x, *shared, wh, bh, cond)

    def run(upstream):
        return tuple(
            dynamics(x, *shared, *last, targets[0], weight[:, None], upstream)
        )

    empty = jnp.zeros((rows, latent), BF16)
    shapes = jax.eval_shape(run, empty)
    done = lax.cond(
        section == sections - 1,
        lambda: run(empty),
        lambda: tuple(jnp.zeros(s.shape, s.dtype) for s in shapes),
    )
    back = (dx_heads[:, :latent] + done[1][:, :latent]).astype(BF16)
    upstream = lax.ppermute(back, "section", [(i + 1, i) for i in range(sections - 1)])
    u_next, dx_next, z_out, loss_next, small_next, small3 = lax.cond(
        section == sections - 1, lambda: done, lambda: run(upstream)
    )

    dx = dx_heads + dx_next
    grads = dx[:, :latent].astype(BF16)
    table = jnp.einsum(
        "rt,re->te", one_hot.astype(F32), dx[:, latent : latent + task_dim], precision=HIGH
    )
    loss_sum = jnp.sum(loss) + jnp.sum(loss_next)

    width = x.shape[1]
    sum_heads = lax.psum_scatter(u_heads, "batch", scatter_dimension=1, tiled=True).astype(F32)
    sum_next = lax.psum_scatter(u_next, "batch", scatter_dimension=0, tiled=True).astype(F32)
    part = hidden // devices
    layer_one = jnp.concatenate(
        [sum_next[None, :, hidden : hidden + width], sum_heads[:, :, hidden : hidden + width]]
    )
    blocks = []
    inverse = pow(branches, -1, devices)
    for slot in range(branches):
        owner = lax.rem((device - slot + devices * branches) * inverse, devices)
        chosen = (branches * owner + slot) // devices
        piece = lax.dynamic_index_in_dim(layer_one, chosen, 0, keepdims=False)
        route = [((branches * e + slot) % devices, e) for e in range(devices)]
        blocks.append(lax.ppermute(piece.astype(BF16), "batch", route).astype(F32))
    w_one = jnp.concatenate(blocks, axis=0).T * scale

    small = jnp.concatenate([small_next[None], small]).reshape(branches, 4, 8, hidden).sum(2)
    small3 = small3.reshape(3, 8, latent).sum(1)
    packed = jnp.concatenate(
        [
            small[:, 0].reshape(devices, -1),
            small[:, 1].reshape(devices, -1),
            small[:, 2].reshape(branches, devices, part).swapaxes(0, 1).reshape(devices, -1),
            small[:, 3].reshape(branches, devices, part).swapaxes(0, 1).reshape(devices, -1),
            small3.reshape(3, devices, -1).swapaxes(0, 1).reshape(devices, -1),
        ],
        axis=1,
    )
    packed = lax.psum_scatter(packed, "batch", scatter_dimension=0, tiled=True)[0] * scale
    one = branches * hidden // devices
    two = branches * part
    three = latent // devices
    parts = jnp.split(packed, [one, 2 * one, 2 * one + two, 2 * one + 2 * two])
    third = parts[4].reshape(3, three)

    head_bias_total, loss_total = lax.psum((head_bias[:, 0, :bins], loss_sum), "batch")
    table_total = lax.psum(table, ("section", "batch"))
    w_two = jnp.concatenate([sum_next[None, :, :hidden], sum_heads[:, :, :hidden]])
    return (
        z_out[None],
        grads[None],
        (loss_total * scale).reshape(1),
        w_one[None, :latent],
        w_one[None, latent + task_dim : latent + task_dim + act],
        w_one[None, latent : latent + task_dim],
        parts[0][None],
        parts[1][None],
        (w_two.swapaxes(1, 2) * scale)[None],
        parts[2].reshape(1, branches, part),
        parts[3].reshape(1, branches, part),
        (sum_next[:, hidden + width :] * scale)[None],
        third[2][None],
        third[0][None],
        third[1][None],
        (sum_heads[:, :, hidden + width : hidden + width + bins] * scale)[None],
        (head_bias_total * scale)[None],
        table_total * scale,
    )


def solution(mesh):
    rows = P("section", "batch")
    wide = P("section", "batch", None)
    matrix = P("section", None, None)
    vector = P("section", None)
    in_specs = (
        P("batch", None), wide, P("batch"), rows, rows, rows, rows, rows, wide, P(),
        matrix, matrix, matrix, vector, vector, P("section", None, None, None), matrix, matrix,
        matrix, vector, vector, vector, P("section", None, None, None), matrix,
    )
    columns = P("section", None, "batch")
    out_specs = (
        wide, wide, P("section"), columns, columns, columns, rows, rows,
        P("section", None, None, "batch"), columns, columns, wide, rows, rows, rows,
        P("section", None, "batch", None), matrix, P(),
    )
    return jax.shard_map(
        on_device, mesh=mesh, in_specs=in_specs, out_specs=out_specs, check_vma=False
    )
```

```python
import functools

import jax
import jax.numpy as jnp
from jax import lax
from jax.experimental import pallas as pl
from jax.experimental.pallas import tpu as pltpu
from jax.sharding import PartitionSpec as P

F32 = jnp.float32
BF16 = jnp.bfloat16
GROUP = 8
RHO = 0.5
CONSISTENCY = 20.0
EPSILON = 1e-05
HIGH = lax.Precision.HIGHEST
LANES = 128
TILE = 256
CHUNK = 16
CAP = 20.0
VMEM_BYTES = 58 * 2**20
WINDOW_BYTES = 62 * 2**20


def dot(left, right, contract):
    return lax.dot_general(
        left, right, ((contract[:1], contract[1:]), ((), ())), preferred_element_type=F32
    )


def nn(left, right):
    return dot(left, right, (1, 0))


def nt(left, right):
    return dot(left, right, (1, 1))


def tn(left, right):
    return dot(left, right, (0, 0))


def norm_forward(pre, gain, shift, hidden, slope, unit, inverse, row):
    width = pre.shape[1]
    for start in range(0, TILE, CHUNK):
        out = slice(row + start, row + start + CHUNK)
        x = pre[start : start + CHUNK, :]
        x = x - jnp.sum(x, axis=-1, keepdims=True) * (1.0 / width)
        r = lax.rsqrt(jnp.sum(x * x, axis=-1, keepdims=True) * (1.0 / width) + EPSILON)
        if inverse is not None:
            inverse[out, :] = r
        for q in range(0, width, 256):
            cols = slice(q, q + 256)
            y = x[:, cols] * r
            v = y * gain[:, cols] + shift[:, cols]
            e = jnp.exp(jnp.minimum(v, CAP))
            k = e * (e + 2.0)
            d = 1.0 / (k + 2.0)
            t = k * d
            hidden[out, cols] = (v * t).astype(BF16)
            if slope is not None:
                slope[out, cols] = (t + (4.0 * v * d) * ((k - e) * d)).astype(BF16)
                unit[out, cols] = y.astype(BF16)


def norm_backward(grad, gain, slope, unit, inverse, result, gain_sum, shift_sum, row):
    width = grad.shape[1]
    gains = shifts = None
    for start in range(0, TILE, CHUNK):
        out = slice(row + start, row + start + CHUNK)
        y = unit[out, :].astype(F32)
        dv = grad[start : start + CHUNK, :] * slope[out, :].astype(F32)
        dvy = dv * y
        g = dvy[:8] + dvy[8:]
        s = dv[:8] + dv[8:]
        gains = g if gains is None else gains + g
        shifts = s if shifts is None else shifts + s
        row_gain = gain[...]
        dx = dv * row_gain
        mean = jnp.sum(dx, axis=-1, keepdims=True) * (1.0 / width)
        along = jnp.sum(dvy * row_gain, axis=-1, keepdims=True) * (1.0 / width)
        result[out, :] = ((dx - mean - y * along) * inverse[out, :]).astype(BF16)
    gain_sum[...] += gains
    shift_sum[...] += shifts


def group_matrix():
    i = lax.broadcasted_iota(jnp.int32, (256, 256), 0) // GROUP
    j = lax.broadcasted_iota(jnp.int32, (256, 256), 1) // GROUP
    return jnp.where(i == j, 1.0, 0.0).astype(BF16)


def group_sum(values, ones):
    parts = []
    for q in range(0, values.shape[1], 256):
        v = values[:, q : q + 256]
        high = v.astype(BF16)
        low = (v - high.astype(F32)).astype(BF16)
        parts.append(nn(high, ones) + nn(low, ones))
    return jnp.concatenate(parts, axis=1)


def simplex_forward(pre, gain, shift, ones):
    width = pre.shape[1]
    x = pre - jnp.sum(pre, axis=-1, keepdims=True) * (1.0 / width)
    r = lax.rsqrt(jnp.sum(x * x, axis=-1, keepdims=True) * (1.0 / width) + EPSILON)
    y = x * r
    e = jnp.exp(y * gain + shift)
    return y, r, e / group_sum(e, ones)


def tile_rows(i):
    return slice(i * TILE, (i + 1) * TILE)


def staged(count, first, then):
    first(0)
    for i in range(count):
        if i + 1 < count:
            first(i + 1)
        then(i)


def forward_pair(x, wl, wta, g1, s1, w2, g2, s2, pre, h1, m1, x1, r1, h2, m2, x2, r2):
    count = x.shape[0] // TILE
    latent = wl.shape[0]

    def one(i):
        r = tile_rows(i)
        pre[i][...] = nn(x[r, :latent], wl[...]) + nn(x[r, latent:], wta[...])

    def two(i):
        pre[i][...] = nn(h1[tile_rows(i), :], w2[...])

    staged(count, one, lambda i: norm_forward(pre[i], g1, s1, h1, m1, x1, r1, i * TILE))
    staged(count, two, lambda i: norm_forward(pre[i], g2, s2, h2, m2, x2, r2, i * TILE))


def backward_pair(
    x, wl, wta, g1, w2, g2, pre, m1, x1, r1, m2, x2, r2, d1, d2, back_in,
    dx, add_dx, dg1, ds1, dg2, ds2,
):
    count = x.shape[0] // TILE
    latent = wl.shape[0]

    def one(i):
        pre[i][...] = nt(d2[tile_rows(i), :], w2[...])

    staged(
        count, back_in, lambda i: norm_backward(pre[i], g2, m2, x2, r2, d2, dg2, ds2, i * TILE)
    )
    staged(count, one, lambda i: norm_backward(pre[i], g1, m1, x1, r1, d1, dg1, ds1, i * TILE))
    for i in range(count):
        r = tile_rows(i)
        main, side = nt(d1[r, :], wl[...]), nt(d1[r, :], wta[...])
        if add_dx:
            dx[r, :latent] += main
            dx[r, latent:] += side
        else:
            dx[r, :latent] = main
            dx[r, latent:] = side


def weight_grads(x, h1, d1, d2, tail_left, tail_right, u):
    hidden = h1.shape[1]
    width = x.shape[1]
    for n in range(0, hidden, 256):
        cols = slice(n, n + 256)
        u[cols, :hidden] = tn(d2[:, cols], h1[...]).astype(BF16)
        u[cols, hidden : hidden + width] = tn(d1[:, cols], x[...]).astype(BF16)
        u[cols, hidden + width :] = tn(tail_left[:, cols], tail_right[...]).astype(BF16)


def heads_kernel(
    x, wl, wta, g1, s1, w2, g2, s2, wh, bh, cond,
    u, dx, head_bias, loss, small,
    p0, p1, p2, logits, h1, h2, m1, m2, x1, x2, r1, r2, d1, d2, dl,
):
    pre = (p0, p1, p2)
    w2, wh, g1, s1, g2, s2, bh, cond, u = (
        ref.at[0] for ref in (w2, wh, g1, s1, g2, s2, bh, cond, u)
    )
    sums = [small.at[0, pl.ds(8 * i, 8)] for i in range(4)]
    small[...] = jnp.zeros_like(small)
    head_bias[...] = jnp.zeros_like(head_bias)

    @pl.when(pl.program_id(0) == 0)
    def _():
        dx[...] = jnp.zeros_like(dx)
        loss[...] = jnp.zeros_like(loss)

    forward_pair(x, wl, wta, g1, s1, w2, g2, s2, pre, h1, m1, x1, r1, h2, m2, x2, r2)

    def tail(i):
        r = tile_rows(i)
        v = nn(h2[r, :], wh[...]) + bh[...]
        given = cond[r, :]
        lower, upper, weight = given[:, 0:1], given[:, 1:2], given[:, 2:3]
        v = v - jnp.max(v, axis=-1, keepdims=True)
        e = jnp.exp(v)
        total = jnp.sum(e, axis=-1, keepdims=True)
        at = lax.broadcasted_iota(jnp.int32, v.shape, 1).astype(F32)
        hot = jnp.where(at == lower, 1.0 - upper, 0.0) + jnp.where(at == lower + 1.0, upper, 0.0)
        loss[r, :] += weight * (jnp.log(total) - jnp.sum(hot * v, axis=-1, keepdims=True))
        grad = (weight * (e / total - hot)).astype(BF16)
        dl[r, :] = grad
        head_bias[0, 0:1, :] += jnp.sum(grad.astype(F32), axis=0, keepdims=True)

    for i in range(x.shape[0] // TILE):
        tail(i)

    def back_in(i):
        pre[i][...] = nt(dl[tile_rows(i), :], wh[...])

    backward_pair(
        x, wl, wta, g1, w2, g2, pre, m1, x1, r1, m2, x2, r2, d1, d2, back_in, dx, True, *sums
    )
    weight_grads(x, h1, d1, d2, h2, dl, u)


def scratch(rows, hidden, forward=False):
    def hold():
        return pltpu.VMEM((rows, hidden), BF16)

    if forward:
        return [pltpu.VMEM((TILE, hidden), F32)] * 3 + [hold(), hold()]
    return (
        [pltpu.VMEM((TILE, hidden), F32)] * 3
        + [hold() for _ in range(6)]
        + [pltpu.VMEM((rows, 1), F32)] * 2
        + [hold(), hold()]
    )


def heads(x, w_latent, wta, g1, s1, w_hidden, g2, s2, wh, bh, cond):
    rows, width = x.shape
    latent = w_latent.shape[0]
    count, hidden = wh.shape[0], w_hidden.shape[-1]
    held = scratch(rows, hidden)
    row = pl.BlockSpec((1, 1, hidden), lambda k: (k + 1, 0, 0))
    return pl.pallas_call(
        heads_kernel,
        grid=(count,),
        in_specs=[
            pl.BlockSpec((rows, width), lambda k: (0, 0)),
            pl.BlockSpec((latent, hidden), lambda k: (0, k + 1)),
            pl.BlockSpec((LANES, hidden), lambda k: (0, k + 1)),
            row,
            row,
            pl.BlockSpec((1, hidden, hidden), lambda k: (k + 1, 0, 0)),
            row,
            row,
            pl.BlockSpec((1, hidden, LANES), lambda k: (k, 0, 0)),
            pl.BlockSpec((1, 1, LANES), lambda k: (k, 0, 0)),
            pl.BlockSpec((1, rows, 8), lambda k: (jnp.minimum(k, 1), 0, 0)),
        ],
        out_shape=[
            jax.ShapeDtypeStruct((count, hidden, hidden + width + LANES), BF16),
            jax.ShapeDtypeStruct((rows, width), F32),
            jax.ShapeDtypeStruct((count, 8, LANES), F32),
            jax.ShapeDtypeStruct((rows, 1), F32),
            jax.ShapeDtypeStruct((count, 32, hidden), F32),
        ],
        out_specs=[
            pl.BlockSpec((1, hidden, hidden + width + LANES), lambda k: (k, 0, 0)),
            pl.BlockSpec((rows, width), lambda k: (0, 0)),
            pl.BlockSpec((1, 8, LANES), lambda k: (k, 0, 0)),
            pl.BlockSpec((rows, 1), lambda k: (0, 0)),
            pl.BlockSpec((1, 32, hidden), lambda k: (k, 0, 0)),
        ],
        scratch_shapes=held[:3]
        + [pltpu.VMEM((rows, LANES), F32)]
        + held[3:]
        + [pltpu.VMEM((rows, LANES), BF16)],
        compiler_params=pltpu.CompilerParams(vmem_limit_bytes=VMEM_BYTES),
    )(x, w_latent, wta, g1, s1, w_hidden, g2, s2, wh, bh, cond)


def dynamics_specs(rows, width, latent, hidden):
    row = pl.BlockSpec((1, 1, hidden), lambda k: (0, 0, 0))
    short = pl.BlockSpec((1, latent), lambda k: (0, 0))
    return [
        pl.BlockSpec((rows, width), lambda k: (0, 0)),
        pl.BlockSpec((latent, hidden), lambda k: (0, 0)),
        pl.BlockSpec((LANES, hidden), lambda k: (0, 0)),
        row,
        row,
        pl.BlockSpec((1, hidden, hidden), lambda k: (0, 0, 0)),
        row,
        row,
        pl.BlockSpec((hidden, latent), lambda k: (0, 0)),
        short,
        short,
        short,
    ]


def rollout_kernel(
    x, wl, wta, g1, s1, w2, g2, s2, wn, bn, g3, s3, z_out, p0, p1, p2, h1, h2
):
    pre = (p0, p1, p2)
    w2, g1, s1, g2, s2 = (ref.at[0] for ref in (w2, g1, s1, g2, s2))
    ones = group_matrix()
    none = (None, None, None)
    forward_pair(x, wl, wta, g1, s1, w2, g2, s2, pre, h1, *none, h2, *none)
    for i in range(x.shape[0] // TILE):
        for start in range(i * TILE, (i + 1) * TILE, 64):
            r = slice(start, start + 64)
            v = nn(h2[r, :], wn[...]) + bn[...]
            z_out[r, :] = simplex_forward(v, g3[...], s3[...], ones)[2].astype(BF16)


def rollout(x, w_latent, wta, g1, s1, w_hidden, g2, s2, wn, bn, g3, s3):
    rows, width = x.shape
    latent, hidden = w_latent.shape[0], w_hidden.shape[-1]
    return pl.pallas_call(
        rollout_kernel,
        grid=(1,),
        in_specs=dynamics_specs(rows, width, latent, hidden),
        out_shape=jax.ShapeDtypeStruct((rows, latent), BF16),
        out_specs=pl.BlockSpec((rows, latent), lambda k: (0, 0)),
        scratch_shapes=scratch(rows, hidden, True),
        compiler_params=pltpu.CompilerParams(vmem_limit_bytes=VMEM_BYTES),
    )(x, w_latent, wta, g1, s1, w_hidden, g2, s2, wn, bn, g3, s3)


def dynamics_kernel(
    x, wl, wta, g1, s1, w2, g2, s2, wn, bn, g3, s3, goal, weights, upstream,
    u, dx, z_out, loss, small, small3,
    p0, p1, p2, pre3, h1, h2, m1, m2, x1, x2, r1, r2, d1, d2, d3,
):
    pre = (p0, p1, p2)
    w2, g1, s1, g2, s2 = (ref.at[0] for ref in (w2, g1, s1, g2, s2))
    sums = [small.at[pl.ds(8 * i, 8)] for i in range(4)]
    small[...] = jnp.zeros_like(small)
    ones = group_matrix()
    width = wn.shape[1]
    forward_pair(x, wl, wta, g1, s1, w2, g2, s2, pre, h1, m1, x1, r1, h2, m2, x2, r2)
    totals = [None, None, None]
    count = x.shape[0] // TILE
    for i in range(count):
        r = tile_rows(i)
        pre3[r, :] = nn(h2[r, :], wn[...]) + bn[...]
    for start in range(0, x.shape[0], 64):
        r = slice(start, start + 64)
        y, inverse, z = simplex_forward(pre3[r, :], g3[...], s3[...], ones)
        z_out[r, :] = z.astype(BF16)
        differ = z - goal[r, :].astype(F32)
        weight = weights[r, :]
        loss[r, :] = weight * (
            CONSISTENCY / width * jnp.sum(differ * differ, axis=-1, keepdims=True)
        )
        grad = upstream[r, :].astype(F32) + weight * (2.0 * CONSISTENCY / width) * differ
        grad = grad * z
        dv = grad - z * group_sum(grad, ones)
        dvy = dv * y
        dy = dv * g3[...]
        mean = jnp.sum(dy, axis=-1, keepdims=True) * (1.0 / width)
        along = jnp.sum(dy * y, axis=-1, keepdims=True) * (1.0 / width)
        result = ((dy - mean - y * along) * inverse).astype(BF16)
        d3[r, :] = result
        for q, part in enumerate((dvy, dv, result.astype(F32))):
            part = functools.reduce(jnp.add, [part[s : s + 8] for s in range(0, 64, 8)])
            totals[q] = part if totals[q] is None else totals[q] + part
    for q in range(3):
        small3[8 * q : 8 * q + 8, :] = totals[q]

    def back_in(i):
        pre[i][...] = nt(d3[tile_rows(i), :], wn[...])

    backward_pair(
        x, wl, wta, g1, w2, g2, pre, m1, x1, r1, m2, x2, r2, d1, d2, back_in, dx, False, *sums
    )
    weight_grads(x, h1, d1, d2, h2, d3, u)


def dynamics(
    x, w_latent, wta, g1, s1, w_hidden, g2, s2, wn, bn, g3, s3, goal, weights, upstream
):
    rows, width = x.shape
    latent, hidden = w_latent.shape[0], w_hidden.shape[-1]
    held = scratch(rows, hidden)

    def whole(shape):
        return pl.BlockSpec(shape, lambda k: (0, 0))

    shapes = [
        ((hidden, hidden + width + latent), BF16),
        ((rows, width), F32),
        ((rows, latent), BF16),
        ((rows, 1), F32),
        ((32, hidden), F32),
        ((24, latent), F32),
    ]
    return pl.pallas_call(
        dynamics_kernel,
        grid=(1,),
        in_specs=dynamics_specs(rows, width, latent, hidden)
        + [whole((rows, latent)), whole((rows, 1)), whole((rows, latent))],
        out_shape=[jax.ShapeDtypeStruct(*s) for s in shapes],
        out_specs=[whole(s[0]) for s in shapes],
        scratch_shapes=held[:3]
        + [pltpu.VMEM((rows, latent), F32)]
        + held[3:]
        + [pltpu.VMEM((rows, latent), BF16)],
        compiler_params=pltpu.CompilerParams(vmem_limit_bytes=VMEM_BYTES),
    )(x, w_latent, wta, g1, s1, w_hidden, g2, s2, wn, bn, g3, s3, goal, weights, upstream)


def on_device(
    latents, actions, tasks, masks, reward_bins, reward_frac, value_bins, value_frac, targets,
    task_table, w_latent, w_action, w_task, gain_one, shift_one, w_hidden, gain_two, shift_two,
    w_next, bias_next, gain_three, shift_three, w_head, bias_head,
):
    section = lax.axis_index("section")
    device = lax.axis_index("batch")
    devices = lax.axis_size("batch")
    sections = lax.axis_size("section")
    rows, latent = latents.shape
    branches, hidden = w_hidden.shape[1], w_hidden.shape[-1]
    heads_count, bins = w_head.shape[1], w_head.shape[-1]
    tasks_count, task_dim = task_table.shape
    act = actions.shape[-1]
    scale = 1.0 / (rows * devices)
    rho = jnp.where(section == 0, 1.0, RHO).astype(F32)
    spare = LANES - task_dim - act

    ids = lax.broadcasted_iota(jnp.int32, (1, tasks_count), 1)
    one_hot = (tasks[:, None] == ids).astype(BF16)
    embedded = nn(one_hot, task_table).astype(BF16)
    extra = jnp.concatenate([embedded, actions[0], jnp.zeros((rows, spare), BF16)], axis=1)
    wta = jnp.concatenate(
        [w_task[0], w_action[0], jnp.zeros((spare, branches * hidden), BF16)], axis=0
    )
    weight = rho * masks[0].astype(F32)
    wide = LANES - bins
    wh = jnp.pad(w_head[0], ((0, 0), (0, 0), (0, wide)))
    bh = jnp.pad(bias_head[0], ((0, 0), (0, wide)), constant_values=-1e30)[:, None, :]
    none = jnp.zeros((2, rows), F32)
    cond = jnp.stack(
        [
            jnp.stack([reward_bins[0], value_bins[0]]).astype(F32),
            jnp.stack([reward_frac[0], value_frac[0]]),
            jnp.stack([weight, weight / (heads_count - 1)]),
        ]
        + [none] * 5,
        axis=-1,
    )
    g1 = gain_one[0].reshape(branches, 1, hidden)
    s1 = shift_one[0].reshape(branches, 1, hidden)
    g2 = gain_two[0][:, None, :]
    s2 = shift_two[0][:, None, :]
    shared = (w_latent[0], wta, g1, s1, w_hidden[0], g2, s2)
    last = (w_next[0], bias_next, gain_three, shift_three)

    first = rollout(jnp.concatenate([latents, extra], axis=1), *shared, *last)
    received = lax.ppermute(first, "section", [(i, i + 1) for i in range(sections - 1)])
    x = jnp.concatenate([jnp.where(section == 0, latents, received), extra], axis=1)
    u_heads, dx_heads, head_bias, loss, small = heads(x, *shared, wh, bh, cond)

    def run(upstream):
        return tuple(
            dynamics(x, *shared, *last, targets[0], weight[:, None], upstream)
        )

    empty = jnp.zeros((rows, latent), BF16)
    shapes = jax.eval_shape(run, empty)
    done = lax.cond(
        section == sections - 1,
        lambda: run(empty),
        lambda: tuple(jnp.zeros(s.shape, s.dtype) for s in shapes),
    )
    back = (dx_heads[:, :latent] + done[1][:, :latent]).astype(BF16)
    upstream = lax.ppermute(back, "section", [(i + 1, i) for i in range(sections - 1)])
    u_next, dx_next, z_out, loss_next, small_next, small3 = lax.cond(
        section == sections - 1, lambda: done, lambda: run(upstream)
    )

    dx = dx_heads + dx_next
    grads = dx[:, :latent].astype(BF16)
    table = jnp.einsum(
        "rt,re->te", one_hot.astype(F32), dx[:, latent : latent + task_dim], precision=HIGH
    )
    loss_sum = jnp.sum(loss) + jnp.sum(loss_next)

    width = x.shape[1]
    sum_heads = lax.psum_scatter(u_heads, "batch", scatter_dimension=1, tiled=True).astype(F32)
    sum_next = lax.psum_scatter(u_next, "batch", scatter_dimension=0, tiled=True).astype(F32)
    part = hidden // devices
    layer_one = jnp.concatenate(
        [sum_next[None, :, hidden : hidden + width], sum_heads[:, :, hidden : hidden + width]]
    )
    blocks = []
    inverse = pow(branches, -1, devices)
    for slot in range(branches):
        owner = lax.rem((device - slot + devices * branches) * inverse, devices)
        chosen = (branches * owner + slot) // devices
        piece = lax.dynamic_index_in_dim(layer_one, chosen, 0, keepdims=False)
        route = [((branches * e + slot) % devices, e) for e in range(devices)]
        blocks.append(lax.ppermute(piece.astype(BF16), "batch", route).astype(F32))
    w_one = jnp.concatenate(blocks, axis=0).T * scale

    small = jnp.concatenate([small_next[None], small]).reshape(branches, 4, 8, hidden).sum(2)
    small3 = small3.reshape(3, 8, latent).sum(1)
    packed = jnp.concatenate(
        [
            small[:, 0].reshape(devices, -1),
            small[:, 1].reshape(devices, -1),
            small[:, 2].reshape(branches, devices, part).swapaxes(0, 1).reshape(devices, -1),
            small[:, 3].reshape(branches, devices, part).swapaxes(0, 1).reshape(devices, -1),
            small3.reshape(3, devices, -1).swapaxes(0, 1).reshape(devices, -1),
        ],
        axis=1,
    )
    packed = lax.psum_scatter(packed, "batch", scatter_dimension=0, tiled=True)[0] * scale
    one = branches * hidden // devices
    two = branches * part
    three = latent // devices
    parts = jnp.split(packed, [one, 2 * one, 2 * one + two, 2 * one + 2 * two])
    third = parts[4].reshape(3, three)

    head_bias_total, loss_total = lax.psum((head_bias[:, 0, :bins], loss_sum), "batch")
    table_total = lax.psum(table, ("section", "batch"))
    w_two = jnp.concatenate([sum_next[None, :, :hidden], sum_heads[:, :, :hidden]])
    return (
        z_out[None],
        grads[None],
        (loss_total * scale).reshape(1),
        w_one[None, :latent],
        w_one[None, latent + task_dim : latent + task_dim + act],
        w_one[None, latent : latent + task_dim],
        parts[0][None],
        parts[1][None],
        (w_two.swapaxes(1, 2) * scale)[None],
        parts[2].reshape(1, branches, part),
        parts[3].reshape(1, branches, part),
        (sum_next[:, hidden + width :] * scale)[None],
        third[2][None],
        third[0][None],
        third[1][None],
        (sum_heads[:, :, hidden + width : hidden + width + bins] * scale)[None],
        (head_bias_total * scale)[None],
        table_total * scale,
    )


PIECE = 256
HEAD_PIECES = 7
NEXT_PIECES = 9
SMALL_AT = 104
POINTS = ((0, 1, 2), (3, 4), (5, 6))
LAGS = (7, 10, 12, 14)
MESH = pl.DeviceIdType.MESH


def halving(piece, bits):
    return tuple(range(bits))


def window_kernel(
    devices, bins,
    z_in, ea, info, wl_in, wt_in, wa_in, g1, s1, w2_in, g2, s2, wh_in, bh, wn_in, bn, g3, s3, goal_in,
    z_out, d_out, heads_out, next_out, one_out, all_out,
    z, wl, wta, w2, wh_raw, wh, wn, goal, upstream, cond, info_t,
    p0, p1, p2, h1, h2, m1, m2, x1, x2, r1, r2, dl, d3, dx, loss, head_bias, small, small3,
    u, one_send, one_recv, every, every_recv, rb,
    load_sem, once_sem, send_sem, recv_sem, zs_sem, zr_sem, ds_sem, dr_sem, os_sem, or_sem, es_sem, er_sem,
):
    section = lax.axis_index("section")
    device = lax.axis_index("batch")
    rows, latent = z.shape
    hidden = w2.shape[-1]
    heads_count = bh.shape[0]
    branches = heads_count + 1
    count = rows // TILE
    part = hidden // devices
    bits = devices.bit_length() - 1
    pre = (p0, p1, p2)
    bit = [lax.rem(lax.div(device, 1 << b), 2) for b in range(bits)]
    other = (1 - section, device)

    def partner(b):
        return (section, device + (1 - 2 * bit[b]) * (1 << b))

    barrier = pltpu.get_barrier_semaphore()
    for step in range(1, devices):
        to = (section, lax.rem(device + step, devices))
        pl.semaphore_signal(barrier, inc=1, device_id=to, device_id_type=MESH)
    pl.semaphore_signal(barrier, inc=1, device_id=other, device_id_type=MESH)

    def loads(branch, slot):
        cols = pl.ds(pl.multiple_of(branch * hidden, hidden), hidden)
        pairs = [
            (wl_in.at[:, cols], wl.at[slot]),
            (wt_in.at[:, cols], wta.at[slot, pl.ds(0, wt_in.shape[0])]),
            (wa_in.at[:, cols], wta.at[slot, pl.ds(wt_in.shape[0], wa_in.shape[0])]),
            (w2_in.at[branch], w2.at[slot]),
        ]
        return [
            pltpu.make_async_copy(a, b, load_sem.at[slot, i]) for i, (a, b) in enumerate(pairs)
        ]

    def load_head(head, slot):
        return pltpu.make_async_copy(wh_in.at[head], wh_raw.at[slot], load_sem.at[slot, 4])

    for copy in loads(0, 1):
        copy.start()
    first_z = pltpu.make_async_copy(z_in, z, once_sem.at[0])
    load_wn = pltpu.make_async_copy(wn_in, wn, once_sem.at[1])
    load_goal = pltpu.make_async_copy(goal_in, goal, once_sem.at[2])

    @pl.when(section == 0)
    def _():
        first_z.start()

    load_wn.start()
    load_goal.start()
    for copy in loads(1, 0):
        copy.start()
    load_head(0, 0).start()

    info_t[...] = jnp.zeros_like(info_t)
    info_t[0:8, :] = info[...]
    cond[...] = info_t[...].T
    wh[...] = jnp.zeros_like(wh)
    dx[...] = jnp.zeros_like(dx)
    loss[...] = jnp.zeros_like(loss)
    head_bias[...] = jnp.zeros_like(head_bias)

    @pl.when(section == 1)
    def _():
        upstream[...] = jnp.zeros_like(upstream)

    pl.semaphore_wait(barrier, devices)

    def pass_on(i):
        r = pl.ds(i * TILE, TILE)
        return pltpu.make_async_remote_copy(
            src_ref=z_out.at[r], dst_ref=z.at[r], send_sem=zs_sem.at[i], recv_sem=zr_sem.at[i],
            device_id=other, device_id_type=MESH,
        )

    def pass_back(i):
        r = pl.ds(i * TILE, TILE)
        return pltpu.make_async_remote_copy(
            src_ref=d_out.at[r], dst_ref=upstream.at[r], send_sem=ds_sem.at[i], recv_sem=dr_sem.at[i],
            device_id=other, device_id_type=MESH,
        )

    ones = group_matrix()
    for copy in loads(0, 1):
        copy.wait()
    load_wn.wait()
    load_goal.wait()

    def layer_one(i, slot):
        r = tile_rows(i)
        pre[i][...] = nn(z[r, :], wl[slot]) + nn(ea[r, :], wta[slot])

    def layer_two(i, slot):
        pre[i][...] = nn(h1[tile_rows(i), :], w2[slot])

    @pl.when(section == 0)
    def _():
        first_z.wait()
        for i in range(count):
            r = tile_rows(i)
            layer_one(i, 1)
            norm_forward(pre[i], g1.at[0], s1.at[0], h1, None, None, None, i * TILE)
            layer_two(i, 1)
            norm_forward(pre[i], g2.at[0], s2.at[0], h2, None, None, None, i * TILE)
            pre[i][:, :latent] = nn(h2[r, :], wn[...]) + bn[...]
            for start in range(0, TILE, 64):
                v = pre[i][start : start + 64, :latent]
                result = simplex_forward(v, g3[...], s3[...], ones)[2]
                z_out[i * TILE + start : i * TILE + start + 64, :] = result.astype(BF16)
            pass_on(i).start()

    def span(order, stage, take):
        half = hidden >> (stage + 1)
        at = sum(bit[order[i]] * (hidden >> (i + 1)) for i in range(stage)) + take * half
        return pl.ds(pl.multiple_of(at, half), half)

    def copy_of(slot, piece, stage):
        order = halving(piece, bits)
        return pltpu.make_async_remote_copy(
            src_ref=u.at[slot, piece, span(order, stage, 1 - bit[order[stage]])],
            dst_ref=rb[stage].at[slot, piece],
            send_sem=send_sem.at[stage, slot, piece],
            recv_sem=recv_sem.at[stage, slot, piece],
            device_id=partner(order[stage]),
            device_id_type=MESH,
        )

    def take(slot, piece, stage, result):
        copy = copy_of(slot, piece, stage)
        copy.wait_recv()
        copy.wait_send()
        order = halving(piece, bits)
        keep = span(order, stage, bit[order[stage]])
        if stage + 1 < bits:
            u[slot, piece, keep, :] = u[slot, piece, keep, :] + rb[stage][slot, piece]
            copy_of(slot, piece, stage + 1).start()
        else:
            result[...] = u[slot, piece, keep, :].astype(F32) + rb[stage][slot, piece].astype(F32)

    def owner_of(branch):
        block = branch * devices + device
        return lax.div(block, branches), lax.rem(block, branches)

    def send_one(branch):
        to, slot = owner_of(branch)
        return to, pltpu.make_async_remote_copy(
            src_ref=one_send.at[branch], dst_ref=one_recv.at[slot],
            send_sem=os_sem.at[branch], recv_sem=or_sem.at[slot],
            device_id=(section, to), device_id_type=MESH,
        )

    def first_layer_done(branch, result):
        one_send[branch, :, :PIECE] = result[4].astype(BF16)
        one_send[branch, :, PIECE:latent] = result[5].astype(BF16)
        one_send[branch, :, latent:] = result[6, :, :LANES].astype(BF16)
        to, copy = send_one(branch)

        @pl.when(to != device)
        def _():
            copy.start()

        @pl.when(to == device)
        def _():
            one_recv[owner_of(branch)[1]] = one_send[branch]

    def service(step, piece):
        for stage in range(bits):
            behind = step_lag[stage] - piece
            back = -(-behind // HEAD_PIECES)
            mine = back * HEAD_PIECES - behind
            unit = step - back

            def act(unit=unit, mine=mine, stage=stage):
                slot = lax.rem(unit, 2)
                take(slot, mine, stage, heads_out.at[unit, mine])
                if stage == bits - 1 and mine == HEAD_PIECES - 1:
                    first_layer_done(unit + 1, heads_out.at[unit])

            pl.when((unit >= 0) & (unit < heads_count))(act)

    step_lag = LAGS if bits == len(LAGS) else tuple(7 + 2 * i for i in range(bits))

    def put(slot, order, n, piece, col, value):
        each = PIECE // part
        for q in range(each):
            block = n // part + q
            at = sum(((block >> order[i]) & 1) << (bits - 1 - i) for i in range(bits)) * part
            u[slot, piece, at : at + part, col : col + value.shape[1]] = value[
                q * part : (q + 1) * part
            ].astype(BF16)

    select = jnp.where(
        lax.broadcasted_iota(jnp.int32, (16, LANES), 1)
        == lax.broadcasted_iota(jnp.int32, (16, LANES), 0) + SMALL_AT,
        1.0,
        0.0,
    ).astype(BF16)

    def put_hidden(slot):
        for n in range(0, hidden, PIECE):
            value = tn(m2[:, n : n + PIECE], h1[...])
            for piece in range(hidden // PIECE):
                put(slot, halving(piece, bits), n, piece, 0, value[:, piece * PIECE : (piece + 1) * PIECE])

    def put_first(slot):
        for n in range(0, hidden, PIECE):
            cols = slice(n, n + PIECE)
            value = tn(m1[:, cols], z[...])
            for q in range(latent // PIECE):
                piece = hidden // PIECE + q
                put(slot, halving(piece, bits), n, piece, 0, value[:, q * PIECE : (q + 1) * PIECE])
            side = tn(m1[:, cols], ea[...]) + tn(small[0:16, cols].astype(BF16), select)
            piece = HEAD_PIECES - 1
            put(slot, halving(piece, bits), n, piece, 0, side)

    def send_pieces(slot, pieces):
        for piece in pieces:
            copy_of(slot, piece, 0).start()

    sums = [small.at[pl.ds(8 * i, 8)] for i in range(4)]

    def forward_stages(slot, branch):
        one, two = (g1.at[branch], s1.at[branch]), (g2.at[branch], s2.at[branch])
        staged(
            count,
            lambda i: layer_one(i, slot),
            lambda i: norm_forward(pre[i], *one, h1, m1, x1, r1, i * TILE),
        )
        staged(
            count,
            lambda i: layer_two(i, slot),
            lambda i: norm_forward(pre[i], *two, h2, m2, x2, r2, i * TILE),
        )

    def backward_two(branch, back_in):
        gain = g2.at[branch]
        staged(
            count,
            back_in,
            lambda i: norm_backward(pre[i], gain, m2, x2, r2, m2, sums[2], sums[3], i * TILE),
        )

    def backward_one(slot, branch):
        gain = g1.at[branch]

        def back(i):
            pre[i][...] = nt(m2[tile_rows(i), :], w2[slot])

        staged(
            count,
            back,
            lambda i: norm_backward(pre[i], gain, m1, x1, r1, m1, sums[0], sums[1], i * TILE),
        )

    def backward_inputs(i, slot):
        r = tile_rows(i)
        dx[r, :latent] += nt(m1[r, :], wl[slot])
        dx[r, latent:] += nt(m1[r, :], wta[slot])

    def head_tail(i, step, slot):
        r = tile_rows(i)
        v = nn(h2[r, :], wh[...]) + bh[step]
        given = cond[r, :]
        is_first = (step == 0).astype(F32)
        pick = lambda a, b: a * is_first + b * (1.0 - is_first)
        lower, upper = pick(given[:, 0:1], given[:, 2:3]), pick(given[:, 1:2], given[:, 3:4])
        weight = given[:, 4:5] * pick(1.0, 1.0 / (heads_count - 1))
        v = v - jnp.max(v, axis=-1, keepdims=True)
        e = jnp.exp(v)
        total = jnp.sum(e, axis=-1, keepdims=True)
        at = lax.broadcasted_iota(jnp.int32, v.shape, 1).astype(F32)
        hot = jnp.where(at == lower, 1.0 - upper, 0.0) + jnp.where(at == lower + 1.0, upper, 0.0)
        loss[r, :] += weight * (jnp.log(total) - jnp.sum(hot * v, axis=-1, keepdims=True))
        grad = (weight * (e / total - hot)).astype(BF16)
        dl[r, :] = grad
        return jnp.sum(grad.astype(F32), axis=0, keepdims=True)

    @pl.when(section == 1)
    def _():
        for i in range(count):
            pass_on(i).wait_recv()

    def head(step, carry):
        slot = lax.rem(step, 2)
        branch = step + 1
        for copy in loads(branch, slot):
            copy.wait()
        load_head(step, slot).wait()
        wh[:, :bins] = wh_raw[slot]
        for copy in loads(lax.rem(branch + 1, branches), 1 - slot):
            copy.start()

        @pl.when(step + 1 < heads_count)
        def _():
            load_head(step + 1, 1 - slot).start()

        small[...] = jnp.zeros_like(small)
        forward_stages(slot, branch)
        for piece in POINTS[0]:
            service(step, piece)
        biases = [head_tail(i, step, slot) for i in range(count)]
        head_bias[pl.ds(step, 1), :] = functools.reduce(jnp.add, biases)

        def back_in(i):
            pre[i][...] = nt(dl[tile_rows(i), :], wh[...])

        backward_two(branch, back_in)
        for piece in POINTS[1]:
            service(step, piece)
        backward_one(slot, branch)
        for i in range(count):
            backward_inputs(i, slot)
        for piece in POINTS[2]:
            service(step, piece)
        put_hidden(slot)
        put_first(slot)
        for n in range(0, hidden, PIECE):
            cols = slice(n, n + PIECE)
            side = tn(h2[:, cols], dl[...]) + tn(small[16:32, cols].astype(BF16), select)
            piece = HEAD_PIECES - 1
            put(slot, halving(piece, bits), n, piece, LANES, side)
        send_pieces(slot, range(HEAD_PIECES))
        return carry

    lax.fori_loop(0, heads_count, head, 0)

    def rest(start, stop):
        def body(step, carry):
            for piece in range(HEAD_PIECES):
                service(step, piece)
            return carry

        lax.fori_loop(start, stop, body, 0)

    @pl.when(section == 0)
    def _():
        for i in range(count):
            pass_on(i).wait_send()
        rest(heads_count, heads_count + 2)

    slot_next = heads_count % 2

    def dynamics_branch():
        for copy in loads(0, slot_next):
            copy.wait()
        small[...] = jnp.zeros_like(small)
        forward_stages(slot_next, 0)

        def serve(point):
            @pl.when(section == 1)
            def _():
                for piece in POINTS[point]:
                    service(heads_count, piece)

        serve(0)
        width = latent
        for i in range(count):
            pre[i][:, :latent] = nn(h2[tile_rows(i), :], wn[...]) + bn[...]
        small3[...] = jnp.zeros_like(small3)
        for i in range(count):

            @pl.when(section == 0)
            def _(i=i):
                pass_back(i).wait_recv()

            totals = [None, None, None]
            for start in range(0, TILE, 64):
                r = slice(i * TILE + start, i * TILE + start + 64)
                v = pre[i][start : start + 64, :latent]
                y, inverse, zz = simplex_forward(v, g3[...], s3[...], ones)
                z_out[r, :] = zz.astype(BF16)
                differ = zz - goal[r, :].astype(F32)
                weight = cond[r, 4:5]
                loss[r, :] += weight * (
                    CONSISTENCY / width * jnp.sum(differ * differ, axis=-1, keepdims=True)
                )
                grad = upstream[r, :].astype(F32) + weight * (2.0 * CONSISTENCY / width) * differ
                grad = grad * zz
                dv = grad - zz * group_sum(grad, ones)
                dvy = dv * y
                dy = dv * g3[...]
                mean = jnp.sum(dy, axis=-1, keepdims=True) * (1.0 / width)
                along = jnp.sum(dy * y, axis=-1, keepdims=True) * (1.0 / width)
                result = ((dy - mean - y * along) * inverse).astype(BF16)
                d3[r, :] = result
                for q, value in enumerate((dvy, dv, result.astype(F32))):
                    value = functools.reduce(
                        jnp.add, [value[s : s + 8] for s in range(0, 64, 8)]
                    )
                    totals[q] = value if totals[q] is None else totals[q] + value
            for q in range(3):
                small3[8 * q : 8 * q + 8, :] += totals[q]

        def back_in(i):
            pre[i][...] = nt(d3[tile_rows(i), :], wn[...])

        backward_two(0, back_in)
        serve(1)
        backward_one(slot_next, 0)
        for i in range(count):
            backward_inputs(i, slot_next)
            d_out[tile_rows(i), :] = dx[tile_rows(i), :latent].astype(BF16)

            @pl.when(section == 1)
            def _(i=i):
                pass_back(i).start()

        serve(2)
        put_hidden(slot_next)
        send_pieces(slot_next, range(hidden // PIECE))
        put_first(slot_next)
        third = latent // devices
        for n in range(0, hidden, PIECE):
            cols = slice(n, n + PIECE)
            at = lax.broadcasted_iota(jnp.int32, (PIECE, latent), 0) + n
            spot = (at // part) * third + (at % part) % third
            place = jnp.where(lax.broadcasted_iota(jnp.int32, (PIECE, latent), 1) == spot, 1.0, 0.0)
            side = nt(place.astype(BF16), small3[...].astype(BF16))
            side = side + tn(small[16:32, cols].astype(BF16), select)
            piece = HEAD_PIECES - 1
            put(slot_next, halving(piece, bits), n, piece, LANES, side)
            value = tn(h2[:, cols], d3[...])
            for q in range(latent // PIECE):
                piece = HEAD_PIECES + q
                put(slot_next, halving(piece, bits), n, piece, 0, value[:, q * PIECE : (q + 1) * PIECE])
        send_pieces(slot_next, range(hidden // PIECE, NEXT_PIECES))

    def turn(t, carry):
        pl.when(section == 1 - t)(dynamics_branch)
        return carry

    lax.fori_loop(0, 2, turn, 0)

    @pl.when(section == 1)
    def _():
        rest(heads_count + 1, heads_count + 2)

    table_rows = every.shape[1] - 16
    table = jnp.zeros((LANES, LANES), F32)
    for i in range(count):
        r = tile_rows(i)
        ids = cond[r, 5:6]
        hot = (lax.broadcasted_iota(jnp.int32, (TILE, LANES), 1).astype(F32) == ids).astype(F32)
        hot = hot.astype(BF16)
        value = dx[r, latent:]
        high = value.astype(BF16)
        middle = (value - high.astype(F32)).astype(BF16)
        table = table + (tn(hot, high) + tn(hot, middle))
    every[0, :table_rows, :] = table[:table_rows]
    every[0, table_rows : table_rows + 8, :] = head_bias[...]
    every[0, table_rows + 8 :, :] = jnp.broadcast_to(
        jnp.sum(loss[...], axis=0, keepdims=True), (8, LANES)
    )

    def exchange(step):
        to = partner(step) if step < bits else other
        return pltpu.make_async_remote_copy(
            src_ref=every.at[step], dst_ref=every_recv.at[step],
            send_sem=es_sem.at[step], recv_sem=er_sem.at[step],
            device_id=to, device_id_type=MESH,
        )

    exchange(0).start()
    swaps = 0

    def swap(step):
        exchange(step).wait_recv()
        every[step + 1] = every[step] + every_recv[step]
        if step < bits:
            exchange(step + 1).start()

    for turn_at in range(NEXT_PIECES + bits - 1):
        for stage in reversed(range(bits)):
            piece = turn_at - stage
            if 0 <= piece < NEXT_PIECES:
                take(slot_next, piece, stage, next_out.at[piece])
                if stage == bits - 1 and piece == HEAD_PIECES - 1:
                    first_layer_done(0, next_out)
        if turn_at % 2 == 1 and swaps <= bits:
            swap(swaps)
            swaps += 1
    for step in range(swaps, bits + 1):
        swap(step)
    all_out[:table_rows, :] = every[bits + 1, :table_rows, :]
    all_out[table_rows:, :] = every[bits, table_rows:, :]

    for slot in range(branches):
        source = lax.rem(device * branches + slot, devices)

        @pl.when(source != device)
        def _(slot=slot):
            pltpu.make_async_remote_copy(
                src_ref=one_send.at[0], dst_ref=one_recv.at[slot],
                send_sem=os_sem.at[0], recv_sem=or_sem.at[slot],
                device_id=other, device_id_type=MESH,
            ).wait_recv()

    for branch in range(branches):
        to, copy = send_one(branch)

        @pl.when(to != device)
        def _(copy=copy):
            copy.wait_send()

    one_out[...] = one_recv[...]
    for step in range(bits + 1):
        exchange(step).wait_send()

    @pl.when(section == 1)
    def _():
        for i in range(count):
            pass_back(i).wait_send()


def window(devices, bins, tasks_count, latents, ea, info, w_latent, w_task, w_act, g1, s1, w_hidden, g2, s2, w_head, bh, w_next, bn, g3, s3, goal):
    rows, latent = latents.shape
    hidden = w_hidden.shape[-1]
    heads_count = w_head.shape[0]
    branches = heads_count + 1
    part = hidden // devices
    bits = devices.bit_length() - 1
    count = rows // TILE
    table_rows = -(-tasks_count // 8) * 8
    vm, dma = pltpu.VMEM, pltpu.SemaphoreType.DMA
    inner = pl.BlockSpec(memory_space=pltpu.VMEM)
    outer = pl.BlockSpec(memory_space=pl.ANY)
    tall = (rows, hidden)
    scratch_shapes = (
        [
            vm((rows, latent), BF16),
            vm((2, latent, hidden), BF16),
            vm((2, LANES, hidden), BF16),
            vm((2, hidden, hidden), BF16),
            vm((2, hidden, bins), BF16),
            vm((hidden, LANES), BF16),
            vm((hidden, latent), BF16),
            vm((rows, latent), BF16),
            vm((rows, latent), BF16),
            vm((rows, LANES), F32),
            vm((LANES, rows), F32),
        ]
        + [vm((TILE, hidden), F32)] * 3
        + [vm(tall, BF16)] * 6
        + [vm((rows, 1), F32)] * 2
        + [
            vm((rows, LANES), BF16),
            vm((rows, latent), BF16),
            vm((rows, latent + LANES), F32),
            vm((rows, 1), F32),
            vm((8, LANES), F32),
            vm((32, hidden), F32),
            vm((LANES, latent), F32),
            vm((2, NEXT_PIECES, hidden, PIECE), BF16),
            vm((branches, part, latent + LANES), BF16),
            vm((branches, part, latent + LANES), BF16),
            vm((bits + 2, table_rows + 16, LANES), F32),
            vm((bits + 1, table_rows + 16, LANES), F32),
            [vm((2, NEXT_PIECES, hidden >> (s + 1), PIECE), BF16) for s in range(bits)],
            dma((2, 5)),
            dma((3,)),
            dma((bits, 2, NEXT_PIECES)),
            dma((bits, 2, NEXT_PIECES)),
        ]
        + [dma((count,))] * 4
        + [dma((branches,))] * 2
        + [dma((bits + 1,))] * 2
    )
    shapes = [
        ((rows, latent), BF16),
        ((rows, latent), BF16),
        ((heads_count, HEAD_PIECES, part, PIECE), F32),
        ((NEXT_PIECES, part, PIECE), F32),
        ((branches, part, latent + LANES), BF16),
        ((table_rows + 16, LANES), F32),
    ]
    return pl.pallas_call(
        functools.partial(window_kernel, devices, bins),
        out_shape=[jax.ShapeDtypeStruct(*s) for s in shapes],
        in_specs=[
            outer, inner, inner, outer, outer, outer, inner, inner, outer, inner, inner, outer,
            inner, outer, inner, inner, inner, outer,
        ],
        out_specs=[inner] * len(shapes),
        scratch_shapes=scratch_shapes,
        compiler_params=pltpu.CompilerParams(
            collective_id=0, has_side_effects=True, vmem_limit_bytes=WINDOW_BYTES
        ),
    )(latents, ea, info, w_latent, w_task, w_act, g1, s1, w_hidden, g2, s2, w_head, bh, w_next, bn, g3, s3, goal)


def on_device_window(
    latents, actions, tasks, masks, reward_bins, reward_frac, value_bins, value_frac, targets,
    task_table, w_latent, w_action, w_task, gain_one, shift_one, w_hidden, gain_two, shift_two,
    w_next, bias_next, gain_three, shift_three, w_head, bias_head,
):
    section = lax.axis_index("section")
    devices = lax.axis_size("batch")
    rows, latent = latents.shape
    branches, hidden = w_hidden.shape[1], w_hidden.shape[-1]
    heads_count, bins = w_head.shape[1], w_head.shape[-1]
    tasks_count, task_dim = task_table.shape
    act = actions.shape[-1]
    scale = 1.0 / (rows * devices)
    rho = jnp.where(section == 0, 1.0, RHO).astype(F32)
    spare = LANES - task_dim - act
    part = hidden // devices

    ids = lax.broadcasted_iota(jnp.int32, (1, tasks_count), 1)
    one_hot = (tasks[:, None] == ids).astype(BF16)
    embedded = nn(one_hot, task_table).astype(BF16)
    ea = jnp.concatenate([embedded, actions[0], jnp.zeros((rows, spare), BF16)], axis=1)
    w_act = jnp.pad(w_action[0], ((0, spare), (0, 0)))
    bh = jnp.pad(bias_head[0], ((0, 0), (0, LANES - bins)), constant_values=-1e30)[:, None, :]
    none = jnp.zeros((rows,), F32)
    info = jnp.stack(
        [
            reward_bins[0].astype(F32), reward_frac[0], value_bins[0].astype(F32), value_frac[0],
            rho * masks[0].astype(F32), tasks.astype(F32), none, none,
        ]
    )
    z_out, grads, of_heads, of_next, one, every = window(
        devices, bins, tasks_count, latents, ea, info, w_latent[0], w_task[0], w_act,
        gain_one[0].reshape(branches, 1, hidden), shift_one[0].reshape(branches, 1, hidden),
        w_hidden[0], gain_two[0][:, None, :], shift_two[0][:, None, :], w_head[0], bh,
        w_next[0], bias_next, gain_three, shift_three, targets[0],
    )

    hidden_pieces = hidden // PIECE
    w_two = jnp.concatenate([of_next[None, :hidden_pieces], of_heads[:, :hidden_pieces]])
    w_two = w_two.transpose(0, 1, 3, 2).reshape(branches, hidden, part) * scale
    w_one = one.astype(F32).reshape(branches * part, latent + LANES).T * scale
    last = HEAD_PIECES - 1
    small = jnp.concatenate([of_next[None, last, :, LANES:], of_heads[:, last, :, LANES:]])
    small = small[:, :, SMALL_AT : SMALL_AT + 16].reshape(branches, part, 2, 8).sum(-1) * scale
    extra = latent + SMALL_AT
    small_one = w_one[extra : extra + 16].reshape(2, 8, branches * part).sum(1)
    third = latent // devices
    small3 = of_next[last, :third, LANES : LANES + 24].reshape(third, 3, 8).sum(-1) * scale
    next_grad = jnp.concatenate([of_next[HEAD_PIECES], of_next[HEAD_PIECES + 1]], axis=1) * scale
    table_rows = every.shape[0] - 16
    return (
        z_out[None],
        grads[None],
        (every[table_rows + 8, 0] * scale).reshape(1),
        w_one[None, :latent],
        w_one[None, latent + task_dim : latent + task_dim + act],
        w_one[None, latent : latent + task_dim],
        small_one[0][None],
        small_one[1][None],
        w_two[None],
        small[None, :, :, 0],
        small[None, :, :, 1],
        next_grad[None],
        small3[None, :, 2],
        small3[None, :, 0],
        small3[None, :, 1],
        (of_heads[:, last, :, LANES : LANES + bins] * scale)[None],
        (every[table_rows : table_rows + heads_count, :bins] * scale)[None],
        every[:tasks_count, :task_dim] * scale,
    )


def solution(mesh):
    rows = P("section", "batch")
    wide = P("section", "batch", None)
    matrix = P("section", None, None)
    vector = P("section", None)
    in_specs = (
        P("batch", None), wide, P("batch"), rows, rows, rows, rows, rows, wide, P(),
        matrix, matrix, matrix, vector, vector, P("section", None, None, None), matrix, matrix,
        matrix, vector, vector, vector, P("section", None, None, None), matrix,
    )
    columns = P("section", None, "batch")
    out_specs = (
        wide, wide, P("section"), columns, columns, columns, rows, rows,
        P("section", None, None, "batch"), columns, columns, wide, rows, rows, rows,
        P("section", None, "batch", None), matrix, P(),
    )
    devices = mesh.shape["batch"]
    fits = mesh.shape["section"] == 2 and devices in (2, 4, 8, 16)
    body = on_device_window if fits else on_device
    return jax.shard_map(
        body, mesh=mesh, in_specs=in_specs, out_specs=out_specs, check_vma=False
    )
```

```python
import functools

import jax
import jax.numpy as jnp
from jax import lax
from jax.experimental import pallas as pl
from jax.experimental.pallas import tpu as pltpu
from jax.sharding import PartitionSpec as P

F32 = jnp.float32
BF16 = jnp.bfloat16
GROUP = 8
RHO = 0.5
CONSISTENCY = 20.0
EPSILON = 1e-05
HIGH = lax.Precision.HIGHEST
LANES = 128
TILE = 256
CHUNK = 16
CAP = 20.0
VMEM_BYTES = 58 * 2**20
WINDOW_BYTES = 62 * 2**20


def dot(left, right, contract):
    return lax.dot_general(
        left, right, ((contract[:1], contract[1:]), ((), ())), preferred_element_type=F32
    )


def nn(left, right):
    return dot(left, right, (1, 0))


def nt(left, right):
    return dot(left, right, (1, 1))


def tn(left, right):
    return dot(left, right, (0, 0))


def norm_forward(pre, gain, shift, hidden, slope, unit, inverse, row):
    width = pre.shape[1]
    for start in range(0, TILE, CHUNK):
        out = slice(row + start, row + start + CHUNK)
        x = pre[start : start + CHUNK, :]
        x = x - jnp.sum(x, axis=-1, keepdims=True) * (1.0 / width)
        r = lax.rsqrt(jnp.sum(x * x, axis=-1, keepdims=True) * (1.0 / width) + EPSILON)
        if inverse is not None:
            inverse[out, :] = r
        for q in range(0, width, 256):
            cols = slice(q, q + 256)
            y = x[:, cols] * r
            v = y * gain[:, cols] + shift[:, cols]
            e = jnp.exp(jnp.minimum(v, CAP))
            k = e * (e + 2.0)
            d = 1.0 / (k + 2.0)
            t = k * d
            hidden[out, cols] = (v * t).astype(BF16)
            if slope is not None:
                slope[out, cols] = (t + (4.0 * v * d) * ((k - e) * d)).astype(BF16)
                unit[out, cols] = y.astype(BF16)


def norm_backward(grad, gain, slope, unit, inverse, result, gain_sum, shift_sum, row):
    width = grad.shape[1]
    gains = shifts = None
    for start in range(0, TILE, CHUNK):
        out = slice(row + start, row + start + CHUNK)
        y = unit[out, :].astype(F32)
        dv = grad[start : start + CHUNK, :] * slope[out, :].astype(F32)
        dvy = dv * y
        g = dvy[:8] + dvy[8:]
        s = dv[:8] + dv[8:]
        gains = g if gains is None else gains + g
        shifts = s if shifts is None else shifts + s
        row_gain = gain[...]
        dx = dv * row_gain
        mean = jnp.sum(dx, axis=-1, keepdims=True) * (1.0 / width)
        along = jnp.sum(dvy * row_gain, axis=-1, keepdims=True) * (1.0 / width)
        result[out, :] = ((dx - mean - y * along) * inverse[out, :]).astype(BF16)
    gain_sum[...] += gains
    shift_sum[...] += shifts


def group_matrix():
    i = lax.broadcasted_iota(jnp.int32, (256, 256), 0) // GROUP
    j = lax.broadcasted_iota(jnp.int32, (256, 256), 1) // GROUP
    return jnp.where(i == j, 1.0, 0.0).astype(BF16)


def group_sum(values, ones):
    parts = []
    for q in range(0, values.shape[1], 256):
        v = values[:, q : q + 256]
        high = v.astype(BF16)
        low = (v - high.astype(F32)).astype(BF16)
        parts.append(nn(high, ones) + nn(low, ones))
    return jnp.concatenate(parts, axis=1)


def simplex_forward(pre, gain, shift, ones):
    width = pre.shape[1]
    x = pre - jnp.sum(pre, axis=-1, keepdims=True) * (1.0 / width)
    r = lax.rsqrt(jnp.sum(x * x, axis=-1, keepdims=True) * (1.0 / width) + EPSILON)
    y = x * r
    e = jnp.exp(y * gain + shift)
    return y, r, e / group_sum(e, ones)


def tile_rows(i):
    return slice(i * TILE, (i + 1) * TILE)


def staged(count, first, then):
    first(0)
    for i in range(count):
        if i + 1 < count:
            first(i + 1)
        then(i)


def forward_pair(x, wl, wta, g1, s1, w2, g2, s2, pre, h1, m1, x1, r1, h2, m2, x2, r2):
    count = x.shape[0] // TILE
    latent = wl.shape[0]

    def one(i):
        r = tile_rows(i)
        pre[i][...] = nn(x[r, :latent], wl[...]) + nn(x[r, latent:], wta[...])

    def two(i):
        pre[i][...] = nn(h1[tile_rows(i), :], w2[...])

    staged(count, one, lambda i: norm_forward(pre[i], g1, s1, h1, m1, x1, r1, i * TILE))
    staged(count, two, lambda i: norm_forward(pre[i], g2, s2, h2, m2, x2, r2, i * TILE))


def backward_pair(
    x, wl, wta, g1, w2, g2, pre, m1, x1, r1, m2, x2, r2, d1, d2, back_in,
    dx, add_dx, dg1, ds1, dg2, ds2,
):
    count = x.shape[0] // TILE
    latent = wl.shape[0]

    def one(i):
        pre[i][...] = nt(d2[tile_rows(i), :], w2[...])

    staged(
        count, back_in, lambda i: norm_backward(pre[i], g2, m2, x2, r2, d2, dg2, ds2, i * TILE)
    )
    staged(count, one, lambda i: norm_backward(pre[i], g1, m1, x1, r1, d1, dg1, ds1, i * TILE))
    for i in range(count):
        r = tile_rows(i)
        main, side = nt(d1[r, :], wl[...]), nt(d1[r, :], wta[...])
        if add_dx:
            dx[r, :latent] += main
            dx[r, latent:] += side
        else:
            dx[r, :latent] = main
            dx[r, latent:] = side


def weight_grads(x, h1, d1, d2, tail_left, tail_right, u):
    hidden = h1.shape[1]
    width = x.shape[1]
    for n in range(0, hidden, 256):
        cols = slice(n, n + 256)
        u[cols, :hidden] = tn(d2[:, cols], h1[...]).astype(BF16)
        u[cols, hidden : hidden + width] = tn(d1[:, cols], x[...]).astype(BF16)
        u[cols, hidden + width :] = tn(tail_left[:, cols], tail_right[...]).astype(BF16)


def heads_kernel(
    x, wl, wta, g1, s1, w2, g2, s2, wh, bh, cond,
    u, dx, head_bias, loss, small,
    p0, p1, p2, logits, h1, h2, m1, m2, x1, x2, r1, r2, d1, d2, dl,
):
    pre = (p0, p1, p2)
    w2, wh, g1, s1, g2, s2, bh, cond, u = (
        ref.at[0] for ref in (w2, wh, g1, s1, g2, s2, bh, cond, u)
    )
    sums = [small.at[0, pl.ds(8 * i, 8)] for i in range(4)]
    small[...] = jnp.zeros_like(small)
    head_bias[...] = jnp.zeros_like(head_bias)

    @pl.when(pl.program_id(0) == 0)
    def _():
        dx[...] = jnp.zeros_like(dx)
        loss[...] = jnp.zeros_like(loss)

    forward_pair(x, wl, wta, g1, s1, w2, g2, s2, pre, h1, m1, x1, r1, h2, m2, x2, r2)

    def tail(i):
        r = tile_rows(i)
        v = nn(h2[r, :], wh[...]) + bh[...]
        given = cond[r, :]
        lower, upper, weight = given[:, 0:1], given[:, 1:2], given[:, 2:3]
        v = v - jnp.max(v, axis=-1, keepdims=True)
        e = jnp.exp(v)
        total = jnp.sum(e, axis=-1, keepdims=True)
        at = lax.broadcasted_iota(jnp.int32, v.shape, 1).astype(F32)
        hot = jnp.where(at == lower, 1.0 - upper, 0.0) + jnp.where(at == lower + 1.0, upper, 0.0)
        loss[r, :] += weight * (jnp.log(total) - jnp.sum(hot * v, axis=-1, keepdims=True))
        grad = (weight * (e / total - hot)).astype(BF16)
        dl[r, :] = grad
        head_bias[0, 0:1, :] += jnp.sum(grad.astype(F32), axis=0, keepdims=True)

    for i in range(x.shape[0] // TILE):
        tail(i)

    def back_in(i):
        pre[i][...] = nt(dl[tile_rows(i), :], wh[...])

    backward_pair(
        x, wl, wta, g1, w2, g2, pre, m1, x1, r1, m2, x2, r2, d1, d2, back_in, dx, True, *sums
    )
    weight_grads(x, h1, d1, d2, h2, dl, u)


def scratch(rows, hidden, forward=False):
    def hold():
        return pltpu.VMEM((rows, hidden), BF16)

    if forward:
        return [pltpu.VMEM((TILE, hidden), F32)] * 3 + [hold(), hold()]
    return (
        [pltpu.VMEM((TILE, hidden), F32)] * 3
        + [hold() for _ in range(6)]
        + [pltpu.VMEM((rows, 1), F32)] * 2
        + [hold(), hold()]
    )


def heads(x, w_latent, wta, g1, s1, w_hidden, g2, s2, wh, bh, cond):
    rows, width = x.shape
    latent = w_latent.shape[0]
    count, hidden = wh.shape[0], w_hidden.shape[-1]
    held = scratch(rows, hidden)
    row = pl.BlockSpec((1, 1, hidden), lambda k: (k + 1, 0, 0))
    return pl.pallas_call(
        heads_kernel,
        grid=(count,),
        in_specs=[
            pl.BlockSpec((rows, width), lambda k: (0, 0)),
            pl.BlockSpec((latent, hidden), lambda k: (0, k + 1)),
            pl.BlockSpec((LANES, hidden), lambda k: (0, k + 1)),
            row,
            row,
            pl.BlockSpec((1, hidden, hidden), lambda k: (k + 1, 0, 0)),
            row,
            row,
            pl.BlockSpec((1, hidden, LANES), lambda k: (k, 0, 0)),
            pl.BlockSpec((1, 1, LANES), lambda k: (k, 0, 0)),
            pl.BlockSpec((1, rows, 8), lambda k: (jnp.minimum(k, 1), 0, 0)),
        ],
        out_shape=[
            jax.ShapeDtypeStruct((count, hidden, hidden + width + LANES), BF16),
            jax.ShapeDtypeStruct((rows, width), F32),
            jax.ShapeDtypeStruct((count, 8, LANES), F32),
            jax.ShapeDtypeStruct((rows, 1), F32),
            jax.ShapeDtypeStruct((count, 32, hidden), F32),
        ],
        out_specs=[
            pl.BlockSpec((1, hidden, hidden + width + LANES), lambda k: (k, 0, 0)),
            pl.BlockSpec((rows, width), lambda k: (0, 0)),
            pl.BlockSpec((1, 8, LANES), lambda k: (k, 0, 0)),
            pl.BlockSpec((rows, 1), lambda k: (0, 0)),
            pl.BlockSpec((1, 32, hidden), lambda k: (k, 0, 0)),
        ],
        scratch_shapes=held[:3]
        + [pltpu.VMEM((rows, LANES), F32)]
        + held[3:]
        + [pltpu.VMEM((rows, LANES), BF16)],
        compiler_params=pltpu.CompilerParams(vmem_limit_bytes=VMEM_BYTES),
    )(x, w_latent, wta, g1, s1, w_hidden, g2, s2, wh, bh, cond)


def dynamics_specs(rows, width, latent, hidden):
    row = pl.BlockSpec((1, 1, hidden), lambda k: (0, 0, 0))
    short = pl.BlockSpec((1, latent), lambda k: (0, 0))
    return [
        pl.BlockSpec((rows, width), lambda k: (0, 0)),
        pl.BlockSpec((latent, hidden), lambda k: (0, 0)),
        pl.BlockSpec((LANES, hidden), lambda k: (0, 0)),
        row,
        row,
        pl.BlockSpec((1, hidden, hidden), lambda k: (0, 0, 0)),
        row,
        row,
        pl.BlockSpec((hidden, latent), lambda k: (0, 0)),
        short,
        short,
        short,
    ]


def rollout_kernel(
    x, wl, wta, g1, s1, w2, g2, s2, wn, bn, g3, s3, z_out, p0, p1, p2, h1, h2
):
    pre = (p0, p1, p2)
    w2, g1, s1, g2, s2 = (ref.at[0] for ref in (w2, g1, s1, g2, s2))
    ones = group_matrix()
    none = (None, None, None)
    forward_pair(x, wl, wta, g1, s1, w2, g2, s2, pre, h1, *none, h2, *none)
    for i in range(x.shape[0] // TILE):
        for start in range(i * TILE, (i + 1) * TILE, 64):
            r = slice(start, start + 64)
            v = nn(h2[r, :], wn[...]) + bn[...]
            z_out[r, :] = simplex_forward(v, g3[...], s3[...], ones)[2].astype(BF16)


def rollout(x, w_latent, wta, g1, s1, w_hidden, g2, s2, wn, bn, g3, s3):
    rows, width = x.shape
    latent, hidden = w_latent.shape[0], w_hidden.shape[-1]
    return pl.pallas_call(
        rollout_kernel,
        grid=(1,),
        in_specs=dynamics_specs(rows, width, latent, hidden),
        out_shape=jax.ShapeDtypeStruct((rows, latent), BF16),
        out_specs=pl.BlockSpec((rows, latent), lambda k: (0, 0)),
        scratch_shapes=scratch(rows, hidden, True),
        compiler_params=pltpu.CompilerParams(vmem_limit_bytes=VMEM_BYTES),
    )(x, w_latent, wta, g1, s1, w_hidden, g2, s2, wn, bn, g3, s3)


def dynamics_kernel(
    x, wl, wta, g1, s1, w2, g2, s2, wn, bn, g3, s3, goal, weights, upstream,
    u, dx, z_out, loss, small, small3,
    p0, p1, p2, pre3, h1, h2, m1, m2, x1, x2, r1, r2, d1, d2, d3,
):
    pre = (p0, p1, p2)
    w2, g1, s1, g2, s2 = (ref.at[0] for ref in (w2, g1, s1, g2, s2))
    sums = [small.at[pl.ds(8 * i, 8)] for i in range(4)]
    small[...] = jnp.zeros_like(small)
    ones = group_matrix()
    width = wn.shape[1]
    forward_pair(x, wl, wta, g1, s1, w2, g2, s2, pre, h1, m1, x1, r1, h2, m2, x2, r2)
    totals = [None, None, None]
    count = x.shape[0] // TILE
    for i in range(count):
        r = tile_rows(i)
        pre3[r, :] = nn(h2[r, :], wn[...]) + bn[...]
    for start in range(0, x.shape[0], 64):
        r = slice(start, start + 64)
        y, inverse, z = simplex_forward(pre3[r, :], g3[...], s3[...], ones)
        z_out[r, :] = z.astype(BF16)
        differ = z - goal[r, :].astype(F32)
        weight = weights[r, :]
        loss[r, :] = weight * (
            CONSISTENCY / width * jnp.sum(differ * differ, axis=-1, keepdims=True)
        )
        grad = upstream[r, :].astype(F32) + weight * (2.0 * CONSISTENCY / width) * differ
        grad = grad * z
        dv = grad - z * group_sum(grad, ones)
        dvy = dv * y
        dy = dv * g3[...]
        mean = jnp.sum(dy, axis=-1, keepdims=True) * (1.0 / width)
        along = jnp.sum(dy * y, axis=-1, keepdims=True) * (1.0 / width)
        result = ((dy - mean - y * along) * inverse).astype(BF16)
        d3[r, :] = result
        for q, part in enumerate((dvy, dv, result.astype(F32))):
            part = functools.reduce(jnp.add, [part[s : s + 8] for s in range(0, 64, 8)])
            totals[q] = part if totals[q] is None else totals[q] + part
    for q in range(3):
        small3[8 * q : 8 * q + 8, :] = totals[q]

    def back_in(i):
        pre[i][...] = nt(d3[tile_rows(i), :], wn[...])

    backward_pair(
        x, wl, wta, g1, w2, g2, pre, m1, x1, r1, m2, x2, r2, d1, d2, back_in, dx, False, *sums
    )
    weight_grads(x, h1, d1, d2, h2, d3, u)


def dynamics(
    x, w_latent, wta, g1, s1, w_hidden, g2, s2, wn, bn, g3, s3, goal, weights, upstream
):
    rows, width = x.shape
    latent, hidden = w_latent.shape[0], w_hidden.shape[-1]
    held = scratch(rows, hidden)

    def whole(shape):
        return pl.BlockSpec(shape, lambda k: (0, 0))

    shapes = [
        ((hidden, hidden + width + latent), BF16),
        ((rows, width), F32),
        ((rows, latent), BF16),
        ((rows, 1), F32),
        ((32, hidden), F32),
        ((24, latent), F32),
    ]
    return pl.pallas_call(
        dynamics_kernel,
        grid=(1,),
        in_specs=dynamics_specs(rows, width, latent, hidden)
        + [whole((rows, latent)), whole((rows, 1)), whole((rows, latent))],
        out_shape=[jax.ShapeDtypeStruct(*s) for s in shapes],
        out_specs=[whole(s[0]) for s in shapes],
        scratch_shapes=held[:3]
        + [pltpu.VMEM((rows, latent), F32)]
        + held[3:]
        + [pltpu.VMEM((rows, latent), BF16)],
        compiler_params=pltpu.CompilerParams(vmem_limit_bytes=VMEM_BYTES),
    )(x, w_latent, wta, g1, s1, w_hidden, g2, s2, wn, bn, g3, s3, goal, weights, upstream)


def on_device(
    latents, actions, tasks, masks, reward_bins, reward_frac, value_bins, value_frac, targets,
    task_table, w_latent, w_action, w_task, gain_one, shift_one, w_hidden, gain_two, shift_two,
    w_next, bias_next, gain_three, shift_three, w_head, bias_head,
):
    section = lax.axis_index("section")
    device = lax.axis_index("batch")
    devices = lax.axis_size("batch")
    sections = lax.axis_size("section")
    rows, latent = latents.shape
    branches, hidden = w_hidden.shape[1], w_hidden.shape[-1]
    heads_count, bins = w_head.shape[1], w_head.shape[-1]
    tasks_count, task_dim = task_table.shape
    act = actions.shape[-1]
    scale = 1.0 / (rows * devices)
    rho = jnp.where(section == 0, 1.0, RHO).astype(F32)
    spare = LANES - task_dim - act

    ids = lax.broadcasted_iota(jnp.int32, (1, tasks_count), 1)
    one_hot = (tasks[:, None] == ids).astype(BF16)
    embedded = nn(one_hot, task_table).astype(BF16)
    extra = jnp.concatenate([embedded, actions[0], jnp.zeros((rows, spare), BF16)], axis=1)
    wta = jnp.concatenate(
        [w_task[0], w_action[0], jnp.zeros((spare, branches * hidden), BF16)], axis=0
    )
    weight = rho * masks[0].astype(F32)
    wide = LANES - bins
    wh = jnp.pad(w_head[0], ((0, 0), (0, 0), (0, wide)))
    bh = jnp.pad(bias_head[0], ((0, 0), (0, wide)), constant_values=-1e30)[:, None, :]
    none = jnp.zeros((2, rows), F32)
    cond = jnp.stack(
        [
            jnp.stack([reward_bins[0], value_bins[0]]).astype(F32),
            jnp.stack([reward_frac[0], value_frac[0]]),
            jnp.stack([weight, weight / (heads_count - 1)]),
        ]
        + [none] * 5,
        axis=-1,
    )
    g1 = gain_one[0].reshape(branches, 1, hidden)
    s1 = shift_one[0].reshape(branches, 1, hidden)
    g2 = gain_two[0][:, None, :]
    s2 = shift_two[0][:, None, :]
    shared = (w_latent[0], wta, g1, s1, w_hidden[0], g2, s2)
    last = (w_next[0], bias_next, gain_three, shift_three)

    first = rollout(jnp.concatenate([latents, extra], axis=1), *shared, *last)
    received = lax.ppermute(first, "section", [(i, i + 1) for i in range(sections - 1)])
    x = jnp.concatenate([jnp.where(section == 0, latents, received), extra], axis=1)
    u_heads, dx_heads, head_bias, loss, small = heads(x, *shared, wh, bh, cond)

    def run(upstream):
        return tuple(
            dynamics(x, *shared, *last, targets[0], weight[:, None], upstream)
        )

    empty = jnp.zeros((rows, latent), BF16)
    shapes = jax.eval_shape(run, empty)
    done = lax.cond(
        section == sections - 1,
        lambda: run(empty),
        lambda: tuple(jnp.zeros(s.shape, s.dtype) for s in shapes),
    )
    back = (dx_heads[:, :latent] + done[1][:, :latent]).astype(BF16)
    upstream = lax.ppermute(back, "section", [(i + 1, i) for i in range(sections - 1)])
    u_next, dx_next, z_out, loss_next, small_next, small3 = lax.cond(
        section == sections - 1, lambda: done, lambda: run(upstream)
    )

    dx = dx_heads + dx_next
    grads = dx[:, :latent].astype(BF16)
    table = jnp.einsum(
        "rt,re->te", one_hot.astype(F32), dx[:, latent : latent + task_dim], precision=HIGH
    )
    loss_sum = jnp.sum(loss) + jnp.sum(loss_next)

    width = x.shape[1]
    sum_heads = lax.psum_scatter(u_heads, "batch", scatter_dimension=1, tiled=True).astype(F32)
    sum_next = lax.psum_scatter(u_next, "batch", scatter_dimension=0, tiled=True).astype(F32)
    part = hidden // devices
    layer_one = jnp.concatenate(
        [sum_next[None, :, hidden : hidden + width], sum_heads[:, :, hidden : hidden + width]]
    )
    blocks = []
    inverse = pow(branches, -1, devices)
    for slot in range(branches):
        owner = lax.rem((device - slot + devices * branches) * inverse, devices)
        chosen = (branches * owner + slot) // devices
        piece = lax.dynamic_index_in_dim(layer_one, chosen, 0, keepdims=False)
        route = [((branches * e + slot) % devices, e) for e in range(devices)]
        blocks.append(lax.ppermute(piece.astype(BF16), "batch", route).astype(F32))
    w_one = jnp.concatenate(blocks, axis=0).T * scale

    small = jnp.concatenate([small_next[None], small]).reshape(branches, 4, 8, hidden).sum(2)
    small3 = small3.reshape(3, 8, latent).sum(1)
    packed = jnp.concatenate(
        [
            small[:, 0].reshape(devices, -1),
            small[:, 1].reshape(devices, -1),
            small[:, 2].reshape(branches, devices, part).swapaxes(0, 1).reshape(devices, -1),
            small[:, 3].reshape(branches, devices, part).swapaxes(0, 1).reshape(devices, -1),
            small3.reshape(3, devices, -1).swapaxes(0, 1).reshape(devices, -1),
        ],
        axis=1,
    )
    packed = lax.psum_scatter(packed, "batch", scatter_dimension=0, tiled=True)[0] * scale
    one = branches * hidden // devices
    two = branches * part
    three = latent // devices
    parts = jnp.split(packed, [one, 2 * one, 2 * one + two, 2 * one + 2 * two])
    third = parts[4].reshape(3, three)

    head_bias_total, loss_total = lax.psum((head_bias[:, 0, :bins], loss_sum), "batch")
    table_total = lax.psum(table, ("section", "batch"))
    w_two = jnp.concatenate([sum_next[None, :, :hidden], sum_heads[:, :, :hidden]])
    return (
        z_out[None],
        grads[None],
        (loss_total * scale).reshape(1),
        w_one[None, :latent],
        w_one[None, latent + task_dim : latent + task_dim + act],
        w_one[None, latent : latent + task_dim],
        parts[0][None],
        parts[1][None],
        (w_two.swapaxes(1, 2) * scale)[None],
        parts[2].reshape(1, branches, part),
        parts[3].reshape(1, branches, part),
        (sum_next[:, hidden + width :] * scale)[None],
        third[2][None],
        third[0][None],
        third[1][None],
        (sum_heads[:, :, hidden + width : hidden + width + bins] * scale)[None],
        (head_bias_total * scale)[None],
        table_total * scale,
    )


PIECE = 256
HEAD_PIECES = 7
NEXT_PIECES = 9
SMALL_AT = 104
POINTS = ((0, 1, 2), (3, 4), (5, 6))
LAGS = (7, 12, 15, 18)
SLOTS = 3
EXTRA = 16
EARLY = (7, 8, 0, 1, 2, 3)
MESH = pl.DeviceIdType.MESH


def halving(piece, bits):
    if piece in (1, HEAD_PIECES) and bits > 2:
        return (0,) + tuple(range(2, bits)) + (1,)
    return tuple(range(bits))


def held(slot, piece):
    if piece < HEAD_PIECES:
        return slot * HEAD_PIECES + piece
    return SLOTS * HEAD_PIECES + piece - HEAD_PIECES


def landing(slot, piece):
    if piece < HEAD_PIECES:
        return slot * HEAD_PIECES + piece
    return 2 * HEAD_PIECES + piece - HEAD_PIECES


def window_kernel(
    devices, task_dim,
    z_in, acts_in, tasks_in, masks_in, reward_in, reward_part, value_in, value_part, table_in, wl_in, wt_in, wa_in, g1, s1, w2_in, g2, s2, wh_in, bh, wn_in, bn, g3, s3, goal_in,
    z_out, d_out, heads_out, next_out, one_out, all_out,
    x, w1, w2, wh_raw, wh, wn, goal, upstream, cond, info_t, table_wide, acts, wa, bias,
    p0, p1, p2, h1, h2, m1, m2, x1, x2, r1, r2, dl, d3, dx, loss, head_bias, small, small3,
    u, one_send, one_recv, every, every_recv, rb,
    load_sem, once_sem, send_sem, recv_sem, zs_sem, zr_sem, ds_sem, dr_sem, os_sem, or_sem, es_sem, er_sem,
):
    section = lax.axis_index("section")
    device = lax.axis_index("batch")
    rows, latent = z_in.shape
    hidden = w2.shape[-1]
    heads_count, bins = bh.shape[0], bh.shape[-1]
    branches = heads_count + 1
    count = rows // TILE
    part = hidden // devices
    bits = devices.bit_length() - 1
    pre = (p0, p1, p2)
    bit = [lax.rem(lax.div(device, 1 << b), 2) for b in range(bits)]
    other = (1 - section, device)

    def partner(b):
        return (section, device + (1 - 2 * bit[b]) * (1 << b))

    barrier = pltpu.get_barrier_semaphore()
    for step in range(1, devices):
        to = (section, lax.rem(device + step, devices))
        pl.semaphore_signal(barrier, inc=1, device_id=to, device_id_type=MESH)
    pl.semaphore_signal(barrier, inc=1, device_id=other, device_id_type=MESH)

    def loads(branch, slot):
        cols = pl.ds(pl.multiple_of(branch * hidden, hidden), hidden)
        pairs = [
            (wl_in.at[:, cols], w1.at[slot, pl.ds(0, latent)]),
            (wt_in.at[:, cols], w1.at[slot, pl.ds(latent, task_dim)]),
            (w2_in.at[branch], w2.at[slot]),
        ]
        return [
            pltpu.make_async_copy(a, b, load_sem.at[slot, i]) for i, (a, b) in enumerate(pairs)
        ]

    def set_actions(branch, slot):
        cols = pl.ds(pl.multiple_of(branch * hidden, hidden), hidden)
        w1[slot, latent + task_dim :, :] = wa[:, cols]

    def load_head(head, slot):
        return pltpu.make_async_copy(wh_in.at[head], wh_raw.at[slot], load_sem.at[slot, 3])

    for copy in loads(0, 1):
        copy.start()
    first_z = pltpu.make_async_copy(
        z_in, x.at[pl.ds(0, rows), pl.ds(0, latent)], once_sem.at[0]
    )
    load_wn = pltpu.make_async_copy(wn_in, wn, once_sem.at[1])
    load_goal = pltpu.make_async_copy(goal_in, goal, once_sem.at[2])

    @pl.when(section == 0)
    def _():
        first_z.start()

    load_wn.start()
    load_goal.start()
    for copy in loads(1, 0):
        copy.start()
    load_head(0, 0).start()

    info_t[...] = jnp.zeros_like(info_t)
    rho = jnp.where(section == 0, 1.0, RHO)
    given = (
        reward_in[...].astype(F32), reward_part[...], value_in[...].astype(F32), value_part[...],
        rho * masks_in[...].astype(F32), tasks_in[...].astype(F32),
    )
    for i, value in enumerate(given):
        info_t[i : i + 1, :] = value
    cond[...] = info_t[...].T
    acts_count = acts_in.shape[0]
    wa[...] = jnp.zeros_like(wa)
    wa[:acts_count, :] = wa_in[...]
    set_actions(0, 1)
    acts[...] = jnp.zeros_like(acts)
    acts[:acts_count, :] = acts_in[...]
    table_wide[...] = jnp.zeros_like(table_wide)
    table_wide[: table_in.shape[0], :task_dim] = table_in[...]
    bias[...] = jnp.full_like(bias, -1e30)
    for i in range(heads_count):
        bias[i : i + 1, :bins] = bh[i]
    lanes = lax.broadcasted_iota(jnp.int32, (16, LANES), 1)
    lane_row = lax.broadcasted_iota(jnp.int32, (16, LANES), 0)
    act_place = jnp.where(lanes == lane_row + task_dim, 1.0, 0.0).astype(BF16)

    def task_hot(i):
        at = lax.broadcasted_iota(jnp.int32, (TILE, LANES), 1).astype(F32)
        return jnp.where(at == cond[tile_rows(i), 5:6], 1.0, 0.0).astype(BF16)

    for i in range(count):
        r = tile_rows(i)
        x[r, latent:] = (nn(task_hot(i), table_wide[...]) + tn(acts[:, r], act_place)).astype(BF16)
    x[rows:, :latent] = jnp.zeros((EXTRA, latent), BF16)
    select = jnp.where(lanes == lane_row + SMALL_AT, 1.0, 0.0).astype(BF16)
    x[rows:, latent:] = select
    dl[rows:, :] = select
    wh[...] = jnp.zeros_like(wh)
    dx[...] = jnp.zeros_like(dx)
    loss[...] = jnp.zeros_like(loss)
    head_bias[...] = jnp.zeros_like(head_bias)

    @pl.when(section == 1)
    def _():
        upstream[...] = jnp.zeros_like(upstream)

    def pass_on(i):
        r = pl.ds(i * TILE, TILE)
        return pltpu.make_async_remote_copy(
            src_ref=z_out.at[r], dst_ref=x.at[r, pl.ds(0, latent)], send_sem=zs_sem.at[i], recv_sem=zr_sem.at[i],
            device_id=other, device_id_type=MESH,
        )

    def pass_back(i):
        r = pl.ds(i * TILE, TILE)
        return pltpu.make_async_remote_copy(
            src_ref=d_out.at[r], dst_ref=upstream.at[r], send_sem=ds_sem.at[i], recv_sem=dr_sem.at[i],
            device_id=other, device_id_type=MESH,
        )

    ones = group_matrix()
    for copy in loads(0, 1):
        copy.wait()
    load_wn.wait()
    load_goal.wait()

    def layer_one(i, slot):
        r = tile_rows(i)
        pre[i][...] = nn(x[r, :], w1[slot])

    def layer_two(i, slot):
        pre[i][...] = nn(h1[tile_rows(i), :], w2[slot])

    def roll(i):
        layer_one(i, 1)
        norm_forward(pre[i], g1.at[0], s1.at[0], h1, None, None, None, i * TILE)
        layer_two(i, 1)
        norm_forward(pre[i], g2.at[0], s2.at[0], h2, None, None, None, i * TILE)
        pre[i][:, :latent] = nn(h2[tile_rows(i), :], wn[...]) + bn[...]
        for start in range(0, TILE, 64):
            v = pre[i][start : start + 64, :latent]
            result = simplex_forward(v, g3[...], s3[...], ones)[2]
            z_out[i * TILE + start : i * TILE + start + 64, :] = result.astype(BF16)

    @pl.when(section == 0)
    def _():
        first_z.wait()
        roll(0)

    pl.semaphore_wait(barrier, devices)

    @pl.when(section == 0)
    def _():
        pass_on(0).start()
        for i in range(1, count):
            roll(i)
            pass_on(i).start()

    def span(order, stage, take):
        half = hidden >> (stage + 1)
        at = sum(bit[order[i]] * (hidden >> (i + 1)) for i in range(stage)) + take * half
        return pl.ds(pl.multiple_of(at, half), half)

    def copy_of(unit, piece, stage):
        order = halving(piece, bits)
        at, to = held(lax.rem(unit, SLOTS), piece), landing(lax.rem(unit, 2), piece)
        return pltpu.make_async_remote_copy(
            src_ref=u.at[at, span(order, stage, 1 - bit[order[stage]])],
            dst_ref=rb[stage].at[to],
            send_sem=send_sem.at[stage, to],
            recv_sem=recv_sem.at[stage, to],
            device_id=partner(order[stage]),
            device_id_type=MESH,
        )

    def take(unit, piece, stage, result):
        copy = copy_of(unit, piece, stage)
        copy.wait_recv()
        copy.wait_send()
        order = halving(piece, bits)
        keep = span(order, stage, bit[order[stage]])
        at, to = held(lax.rem(unit, SLOTS), piece), landing(lax.rem(unit, 2), piece)
        if stage + 1 < bits:
            u[at, keep, :] = u[at, keep, :] + rb[stage][to]
            copy_of(unit, piece, stage + 1).start()
        else:
            result[...] = u[at, keep, :].astype(F32) + rb[stage][to].astype(F32)

    def owner_of(branch):
        block = branch * devices + device
        return lax.div(block, branches), lax.rem(block, branches)

    def send_one(branch):
        to, slot = owner_of(branch)
        return to, pltpu.make_async_remote_copy(
            src_ref=one_send.at[branch], dst_ref=one_recv.at[slot],
            send_sem=os_sem.at[branch], recv_sem=or_sem.at[slot],
            device_id=(section, to), device_id_type=MESH,
        )

    def first_layer_done(branch, result):
        one_send[branch, :, :PIECE] = result[4].astype(BF16)
        one_send[branch, :, PIECE:latent] = result[5].astype(BF16)
        one_send[branch, :, latent:] = result[6, :, :LANES].astype(BF16)
        to, copy = send_one(branch)

        @pl.when(to != device)
        def _():
            copy.start()

        @pl.when(to == device)
        def _():
            one_recv[owner_of(branch)[1]] = one_send[branch]

    def service(step, piece):
        for stage in range(bits):
            behind = step_lag[stage] - piece
            back = -(-behind // HEAD_PIECES)
            mine = back * HEAD_PIECES - behind
            unit = step - back

            def act(unit=unit, mine=mine, stage=stage):
                take(unit, mine, stage, heads_out.at[unit, mine])
                if stage == bits - 1 and mine == HEAD_PIECES - 1:
                    first_layer_done(unit + 1, heads_out.at[unit])

            pl.when((unit >= 0) & (unit < heads_count))(act)

    step_lag = LAGS if bits == len(LAGS) else tuple(7 + 4 * i for i in range(bits))

    def put(unit, n, piece, col, value):
        order = halving(piece, bits)
        each = PIECE // part
        slot = held(lax.rem(unit, SLOTS), piece)
        for q in range(each):
            block = n // part + q
            at = sum(((block >> order[i]) & 1) << (bits - 1 - i) for i in range(bits)) * part
            u[slot, at : at + part, col : col + value.shape[1]] = value[
                q * part : (q + 1) * part
            ].astype(BF16)

    def put_hidden(unit):
        for n in range(0, hidden, PIECE):
            value = tn(m2[:rows, n : n + PIECE], h1[...])
            for piece in range(hidden // PIECE):
                put(unit, n, piece, 0, value[:, piece * PIECE : (piece + 1) * PIECE])

    def put_first(unit):
        m1[rows:, :] = small[0:EXTRA, :].astype(BF16)
        for n in range(0, hidden, PIECE):
            value = tn(m1[:, n : n + PIECE], x[...])
            for q in range(latent // PIECE):
                put(unit, n, hidden // PIECE + q, 0, value[:, q * PIECE : (q + 1) * PIECE])
            put(unit, n, HEAD_PIECES - 1, 0, value[:, latent:])

    def send_pieces(unit, pieces):
        for piece in pieces:
            copy_of(unit, piece, 0).start()

    sums = [small.at[pl.ds(8 * i, 8)] for i in range(4)]

    def stages(slot, branch):
        one, two = (g1.at[branch], s1.at[branch]), (g2.at[branch], s2.at[branch])

        def back_one(i):
            pre[i][...] = nt(m2[tile_rows(i), :], w2[slot])

        def inputs(i):
            dx[tile_rows(i), :] += nt(m1[tile_rows(i), :], w1[slot])

        return dict(
            f1=lambda i: layer_one(i, slot),
            v1=lambda i: norm_forward(pre[i], *one, h1, m1, x1, r1, i * TILE),
            f2=lambda i: layer_two(i, slot),
            v2=lambda i: norm_forward(pre[i], *two, h2, m2, x2, r2, i * TILE),
            n2=lambda i: norm_backward(pre[i], two[0], m2, x2, r2, m2, sums[2], sums[3], i * TILE),
            b1=back_one,
            n1=lambda i: norm_backward(pre[i], one[0], m1, x1, r1, m1, sums[0], sums[1], i * TILE),
            dx=inputs,
        )

    def forward_stages(at):
        at["f1"](0)
        for i in range(count):
            if i + 1 < count:
                at["f1"](i + 1)
            else:
                at["f2"](0)
            at["v1"](i)
        for i in range(1, count):
            at["f2"](i)
            at["v2"](i - 1)
        at["v2"](count - 1)

    def head_tail(i, step):
        r = tile_rows(i)
        v = nt(h2[r, :], wh[...]) + bias[pl.ds(step, 1), :]
        given = cond[r, :]
        is_first = (step == 0).astype(F32)
        pick = lambda a, b: a * is_first + b * (1.0 - is_first)
        lower, upper = pick(given[:, 0:1], given[:, 2:3]), pick(given[:, 1:2], given[:, 3:4])
        weight = given[:, 4:5] * pick(1.0, 1.0 / (heads_count - 1))
        v = v - jnp.max(v, axis=-1, keepdims=True)
        e = jnp.exp(v)
        total = jnp.sum(e, axis=-1, keepdims=True)
        at = lax.broadcasted_iota(jnp.int32, v.shape, 1).astype(F32)
        hot = jnp.where(at == lower, 1.0 - upper, 0.0) + jnp.where(at == lower + 1.0, upper, 0.0)
        loss[r, :] += weight * (jnp.log(total) - jnp.sum(hot * v, axis=-1, keepdims=True))
        grad = (weight * (e / total - hot)).astype(BF16)
        dl[r, :] = grad
        return jnp.sum(grad.astype(F32), axis=0, keepdims=True)

    @pl.when(section == 1)
    def _():
        for i in range(count):
            pass_on(i).wait_recv()

    def head(step, carry):
        slot = lax.rem(step, 2)
        branch = step + 1
        for copy in loads(branch, slot):
            copy.wait()
        load_head(step, slot).wait()
        at = stages(slot, branch)
        wh[:bins, :] = wh_raw[slot]
        set_actions(branch, slot)
        for copy in loads(lax.rem(branch + 1, branches), 1 - slot):
            copy.start()

        @pl.when(step + 1 < heads_count)
        def _():
            load_head(step + 1, 1 - slot).start()

        small[...] = jnp.zeros_like(small)
        forward_stages(at)
        biases = [head_tail(i, step) for i in range(count)]
        head_bias[pl.ds(step, 1), :] = functools.reduce(jnp.add, biases)
        for piece in POINTS[0]:
            service(step, piece)

        def back_in(i):
            pre[i][...] = nn(dl[tile_rows(i), :], wh[...])

        back_in(0)
        for i in range(count):
            if i + 1 < count:
                back_in(i + 1)
            else:
                at["b1"](0)
            at["n2"](i)
        for i in range(1, count):
            at["b1"](i)
            at["n1"](i - 1)
        at["dx"](0)
        at["n1"](count - 1)
        for i in range(1, count):
            at["dx"](i)
        for piece in POINTS[1]:
            service(step, piece)
        put_hidden(step)
        send_pieces(step, range(hidden // PIECE))
        put_first(step)
        h2[rows:, :] = small[EXTRA : 2 * EXTRA, :].astype(BF16)
        for n in range(0, hidden, PIECE):
            put(step, n, HEAD_PIECES - 1, LANES, tn(h2[:, n : n + PIECE], dl[...]))
        for piece in POINTS[2]:
            service(step, piece)
        send_pieces(step, range(hidden // PIECE, HEAD_PIECES))
        return carry

    lax.fori_loop(0, heads_count, head, 0)

    def rest(start, stop):
        def body(step, carry):
            for piece in range(HEAD_PIECES):
                service(step, piece)
            return carry

        lax.fori_loop(start, stop, body, 0)

    @pl.when(section == 0)
    def _():
        for i in range(count):
            pass_on(i).wait_send()
        rest(heads_count, heads_count + 3)

    slot_next = heads_count % 2
    last_unit = SLOTS * -(-heads_count // SLOTS)
    assert last_unit == heads_count

    def dynamics_branch():
        for copy in loads(0, slot_next):
            copy.wait()
        set_actions(0, slot_next)
        small[...] = jnp.zeros_like(small)
        at = stages(slot_next, 0)
        forward_stages(at)

        def serve(point):
            @pl.when(section == 1)
            def _():
                for piece in POINTS[point]:
                    service(heads_count, piece)

        serve(0)
        width = latent
        for i in range(count):
            pre[i][:, :latent] = nn(h2[tile_rows(i), :], wn[...]) + bn[...]
        small3[...] = jnp.zeros_like(small3)
        for i in range(count):

            @pl.when(section == 0)
            def _(i=i):
                pass_back(i).wait_recv()

            totals = [None, None, None]
            for start in range(0, TILE, 64):
                r = slice(i * TILE + start, i * TILE + start + 64)
                v = pre[i][start : start + 64, :latent]
                y, inverse, zz = simplex_forward(v, g3[...], s3[...], ones)
                z_out[r, :] = zz.astype(BF16)
                differ = zz - goal[r, :].astype(F32)
                weight = cond[r, 4:5]
                loss[r, :] += weight * (
                    CONSISTENCY / width * jnp.sum(differ * differ, axis=-1, keepdims=True)
                )
                grad = upstream[r, :].astype(F32) + weight * (2.0 * CONSISTENCY / width) * differ
                grad = grad * zz
                dv = grad - zz * group_sum(grad, ones)
                dvy = dv * y
                dy = dv * g3[...]
                mean = jnp.sum(dy, axis=-1, keepdims=True) * (1.0 / width)
                along = jnp.sum(dy * y, axis=-1, keepdims=True) * (1.0 / width)
                result = ((dy - mean - y * along) * inverse).astype(BF16)
                d3[r, :] = result
                for q, value in enumerate((dvy, dv, result.astype(F32))):
                    value = functools.reduce(
                        jnp.add, [value[s : s + 8] for s in range(0, 64, 8)]
                    )
                    totals[q] = value if totals[q] is None else totals[q] + value
            for q in range(3):
                small3[8 * q : 8 * q + 8, :] += totals[q]

        def back_in(i):
            pre[i][...] = nt(d3[tile_rows(i), :], wn[...])

        back_in(0)
        for i in range(count):
            if i + 1 < count:
                back_in(i + 1)
            at["n2"](i)

        def put_next():
            for n in range(0, hidden, PIECE):
                value = tn(h2[:rows, n : n + PIECE], d3[...])
                for q in range(latent // PIECE):
                    put(last_unit, n, HEAD_PIECES + q, 0, value[:, q * PIECE : (q + 1) * PIECE])
            send_pieces(last_unit, range(HEAD_PIECES, NEXT_PIECES))
            put_hidden(last_unit)
            send_pieces(last_unit, range(hidden // PIECE))

        pl.when(section == 0)(put_next)
        serve(1)
        at["b1"](0)
        for i in range(count):
            if i + 1 < count:
                at["b1"](i + 1)
            at["n1"](i)
        for i in range(count):
            at["dx"](i)
            d_out[tile_rows(i), :] = dx[tile_rows(i), :latent].astype(BF16)

            @pl.when(section == 1)
            def _(i=i):
                pass_back(i).start()

        serve(2)
        pl.when(section == 1)(put_next)

        @pl.when(section == 0)
        def _():
            for piece in EARLY:
                take(last_unit, piece, 0, None)

        put_first(last_unit)
        third = latent // devices
        h2[rows:, :] = small[EXTRA : 2 * EXTRA, :].astype(BF16)
        for n in range(0, hidden, PIECE):
            at_row = lax.broadcasted_iota(jnp.int32, (PIECE, latent), 0) + n
            spot = (at_row // part) * third + (at_row % part) % third
            place = jnp.where(lax.broadcasted_iota(jnp.int32, (PIECE, latent), 1) == spot, 1.0, 0.0)
            side = nt(place.astype(BF16), small3[...].astype(BF16))
            side = side + tn(h2[rows:, n : n + PIECE], dl[rows:, :])
            put(last_unit, n, HEAD_PIECES - 1, LANES, side)
        send_pieces(last_unit, range(hidden // PIECE, HEAD_PIECES))

    def turn(t, carry):
        pl.when(section == 1 - t)(dynamics_branch)
        return carry

    lax.fori_loop(0, 2, turn, 0)

    @pl.when(section == 1)
    def _():
        rest(heads_count + 1, heads_count + 3)
        for piece in EARLY:
            take(last_unit, piece, 0, None)

    table_rows = every.shape[1] - 16
    table = jnp.zeros((LANES, LANES), F32)
    for i in range(count):
        r = tile_rows(i)
        hot = task_hot(i)
        value = dx[r, latent:]
        high = value.astype(BF16)
        middle = (value - high.astype(F32)).astype(BF16)
        table = table + (tn(hot, high) + tn(hot, middle))
    every[0, :table_rows, :] = table[:table_rows]
    every[0, table_rows : table_rows + 8, :] = head_bias[...]
    every[0, table_rows + 8 :, :] = jnp.broadcast_to(
        jnp.sum(loss[...], axis=0, keepdims=True), (8, LANES)
    )

    def exchange(step):
        to = partner(step) if step < bits else other
        return pltpu.make_async_remote_copy(
            src_ref=every.at[step], dst_ref=every_recv.at[step],
            send_sem=es_sem.at[step], recv_sem=er_sem.at[step],
            device_id=to, device_id_type=MESH,
        )

    exchange(0).start()
    swaps = 0

    def swap(step):
        exchange(step).wait_recv()
        every[step + 1] = every[step] + every_recv[step]
        if step < bits:
            exchange(step + 1).start()

    late = [piece for piece in range(NEXT_PIECES) if piece not in EARLY]
    for piece in late:
        take(last_unit, piece, 0, None)
    order = list(EARLY) + late
    for turn_at in range(NEXT_PIECES + bits - 2):
        for stage in reversed(range(1, bits)):
            if 0 <= turn_at - stage + 1 < NEXT_PIECES:
                piece = order[turn_at - stage + 1]
                take(last_unit, piece, stage, next_out.at[piece])
                if stage == bits - 1 and piece == HEAD_PIECES - 1:
                    first_layer_done(0, next_out)
        if turn_at % 2 == 1 and swaps <= bits:
            swap(swaps)
            swaps += 1
    for step in range(swaps, bits + 1):
        swap(step)
    all_out[:table_rows, :] = every[bits + 1, :table_rows, :]
    all_out[table_rows:, :] = every[bits, table_rows:, :]

    for slot in range(branches):
        source = lax.rem(device * branches + slot, devices)

        @pl.when(source != device)
        def _(slot=slot):
            pltpu.make_async_remote_copy(
                src_ref=one_send.at[0], dst_ref=one_recv.at[slot],
                send_sem=os_sem.at[0], recv_sem=or_sem.at[slot],
                device_id=other, device_id_type=MESH,
            ).wait_recv()

    for branch in range(branches):
        to, copy = send_one(branch)

        @pl.when(to != device)
        def _(copy=copy):
            copy.wait_send()

    one_out[...] = one_recv[...]
    for step in range(bits + 1):
        exchange(step).wait_send()

    @pl.when(section == 1)
    def _():
        for i in range(count):
            pass_back(i).wait_send()


def window(devices, latents, acts, *given):
    (tasks, masks, reward, reward_part, value, value_part, table, w_latent, w_task, w_act,
     g1, s1, w_hidden, g2, s2, w_head, bh, w_next, bn, g3, s3, goal) = given
    rows, latent = latents.shape
    hidden = w_hidden.shape[-1]
    heads_count, bins = bh.shape[0], bh.shape[-1]
    branches = heads_count + 1
    part = hidden // devices
    bits = devices.bit_length() - 1
    count = rows // TILE
    task_dim = table.shape[1]
    table_rows = -(-table.shape[0] // 8) * 8
    landings = 2 * HEAD_PIECES + NEXT_PIECES - HEAD_PIECES
    vm, dma = pltpu.VMEM, pltpu.SemaphoreType.DMA
    inner = pl.BlockSpec(memory_space=pltpu.VMEM)
    outer = pl.BlockSpec(memory_space=pl.ANY)
    tall = (rows + EXTRA, hidden)
    scratch_shapes = (
        [
            vm((rows + EXTRA, latent + LANES), BF16),
            vm((2, latent + LANES, hidden), BF16),
            vm((2, hidden, hidden), BF16),
            vm((2, bins, hidden), BF16),
            vm((LANES, hidden), BF16),
            vm((hidden, latent), BF16),
            vm((rows, latent), BF16),
            vm((rows, latent), BF16),
            vm((rows, LANES), F32),
            vm((LANES, rows), F32),
            vm((LANES, LANES), BF16),
            vm((16, rows), BF16),
            vm((LANES - task_dim, branches * hidden), BF16),
            vm((8, LANES), F32),
        ]
        + [vm((TILE, hidden), F32)] * 3
        + [vm((rows, hidden), BF16), vm(tall, BF16), vm(tall, BF16)]
        + [vm((rows, hidden), BF16)] * 3
        + [vm((rows, 1), F32)] * 2
        + [
            vm((rows + EXTRA, LANES), BF16),
            vm((rows, latent), BF16),
            vm((rows, latent + LANES), F32),
            vm((rows, 1), F32),
            vm((8, LANES), F32),
            vm((32, hidden), F32),
            vm((LANES, latent), F32),
            vm((SLOTS * HEAD_PIECES + NEXT_PIECES - HEAD_PIECES, hidden, PIECE), BF16),
            vm((branches, part, latent + LANES), BF16),
            vm((branches, part, latent + LANES), BF16),
            vm((bits + 2, table_rows + 16, LANES), F32),
            vm((bits + 1, table_rows + 16, LANES), F32),
            [vm((landings, hidden >> (s + 1), PIECE), BF16) for s in range(bits)],
            dma((2, 4)),
            dma((3,)),
            dma((bits, landings)),
            dma((bits, landings)),
        ]
        + [dma((count,))] * 4
        + [dma((branches,))] * 2
        + [dma((bits + 1,))] * 2
    )
    shapes = [
        ((rows, latent), BF16),
        ((rows, latent), BF16),
        ((heads_count, HEAD_PIECES, part, PIECE), F32),
        ((NEXT_PIECES, part, PIECE), F32),
        ((branches, part, latent + LANES), BF16),
        ((table_rows + 16, LANES), F32),
    ]
    return pl.pallas_call(
        functools.partial(window_kernel, devices, task_dim),
        out_shape=[jax.ShapeDtypeStruct(*s) for s in shapes],
        in_specs=[
            outer, inner, inner, inner, inner, inner, inner, inner, inner, outer, outer, inner,
            inner, inner, outer, inner, inner, outer, inner, outer, inner, inner, inner, outer,
        ],
        out_specs=[inner] * len(shapes),
        scratch_shapes=scratch_shapes,
        compiler_params=pltpu.CompilerParams(
            collective_id=0, has_side_effects=True, vmem_limit_bytes=WINDOW_BYTES
        ),
    )(latents, acts, *given)


def finish_kernel(
    scale, task_dim,
    z_in, d_in, heads_in, next_in, one_in, every,
    z_out, d_out, loss, w_latent, w_action, w_task, gain_one, shift_one, w_hidden, gain_two, shift_two,
    w_next, bias_next, gain_three, shift_three, w_head, bias_head, table,
    flip_one, flip_two,
):
    branches, part, width = one_in.shape
    latent = width - LANES
    acts, bins = w_action.shape[0], w_head.shape[-1]
    all_rows = branches * part
    heads_count = branches - 1
    pieces = w_hidden.shape[-1] // PIECE
    table_rows = every.shape[0] - 16
    last = HEAD_PIECES - 1
    z_out[...] = z_in[...]
    d_out[...] = d_in[...]
    flip_one[...] = jnp.zeros_like(flip_one)
    flip_two[...] = jnp.zeros_like(flip_two)
    for k in range(branches):
        rows = slice(k * part, (k + 1) * part)
        source = next_in if k == 0 else heads_in.at[k - 1]
        for p in range(pieces):
            w_hidden[k, :, p * PIECE : (p + 1) * PIECE] = source[p] * scale
        w_latent[rows, :] = one_in[k, :, :latent].astype(F32) * scale
        flip_one[rows, :] = one_in[k, :, latent:].astype(F32) * scale
        flip_two[rows, :] = source[last, :, LANES:] * scale
        if k > 0:
            w_head[k - 1] = source[last, :, LANES : LANES + bins] * scale
            bias_head[k - 1] = every[table_rows + k - 1 : table_rows + k, :bins] * scale
    one = flip_one[...].T
    w_task[...] = one[:task_dim, :all_rows]
    for a in range(acts):
        w_action[a] = one[task_dim + a : task_dim + a + 1, :all_rows]

    def total(value, start):
        return jnp.sum(value[start : start + 8], axis=0, keepdims=True)

    gain_one[...] = total(one, SMALL_AT)[:, :all_rows]
    shift_one[...] = total(one, SMALL_AT + 8)[:, :all_rows]
    two = flip_two[...].T
    gains, shifts = total(two, SMALL_AT), total(two, SMALL_AT + 8)
    for k in range(branches):
        gain_two[k] = gains[:, k * part : (k + 1) * part]
        shift_two[k] = shifts[:, k * part : (k + 1) * part]
    third = gain_three.shape[1]
    gain_three[...] = total(two, 0)[:, :third]
    shift_three[...] = total(two, 8)[:, :third]
    bias_next[...] = total(two, 16)[:, :third]
    for q in range(latent // PIECE):
        w_next[:, q * PIECE : (q + 1) * PIECE] = next_in[HEAD_PIECES + q] * scale
    loss[...] = every[table_rows + 8 : table_rows + 9, 0:1] * scale
    table[...] = every[: table.shape[0], :task_dim] * scale


def on_device_window(
    latents, actions, tasks, masks, reward_bins, reward_frac, value_bins, value_frac, targets,
    task_table, w_latent, w_action, w_task, gain_one, shift_one, w_hidden, gain_two, shift_two,
    w_next, bias_next, gain_three, shift_three, w_head, bias_head,
):
    devices = lax.axis_size("batch")
    rows, latent = latents.shape
    branches, hidden = w_hidden.shape[1], w_hidden.shape[-1]
    heads_count, bins = w_head.shape[1], w_head.shape[-1]
    tasks_count, task_dim = task_table.shape
    act = actions.shape[-1]
    part = hidden // devices
    raw = window(
        devices, latents, actions[0].T, tasks[None], masks, reward_bins, reward_frac, value_bins,
        value_frac, task_table, w_latent[0], w_task[0], w_action[0],
        gain_one[0].reshape(branches, 1, hidden), shift_one[0].reshape(branches, 1, hidden),
        w_hidden[0], gain_two[0][:, None, :], shift_two[0][:, None, :],
        w_head[0].swapaxes(1, 2), bias_head[0][:, None, :],
        w_next[0], bias_next, gain_three, shift_three, targets[0],
    )
    one = branches * part
    third = latent // devices
    shapes = [
        ((rows, latent), BF16), ((rows, latent), BF16), ((1, 1), F32), ((one, latent), F32),
        ((act, 1, one), F32), ((task_dim, one), F32), ((1, one), F32), ((1, one), F32),
        ((branches, part, hidden), F32), ((branches, 1, part), F32), ((branches, 1, part), F32),
        ((part, latent), F32), ((1, third), F32), ((1, third), F32), ((1, third), F32),
        ((heads_count, part, bins), F32), ((heads_count, 1, bins), F32), ((tasks_count, task_dim), F32),
    ]
    inner = pl.BlockSpec(memory_space=pltpu.VMEM)
    flipped = pltpu.VMEM((-(-one // LANES) * LANES, LANES), F32)
    (z_out, grads, loss, d_latent, d_action, d_task, d_gain_one, d_shift_one, d_hidden,
     d_gain_two, d_shift_two, d_next, d_bias_next, d_gain_three, d_shift_three, d_head,
     d_bias_head, d_table) = pl.pallas_call(
        functools.partial(finish_kernel, 1.0 / (rows * devices), task_dim),
        out_shape=[jax.ShapeDtypeStruct(*s) for s in shapes],
        in_specs=[inner] * len(raw),
        out_specs=[inner] * len(shapes),
        scratch_shapes=[flipped, flipped],
        compiler_params=pltpu.CompilerParams(vmem_limit_bytes=VMEM_BYTES),
    )(*raw)
    return (
        z_out[None], grads[None], loss.reshape(1), d_latent.T[None], d_action.swapaxes(0, 1),
        d_task[None], d_gain_one, d_shift_one, d_hidden.swapaxes(1, 2)[None],
        d_gain_two.swapaxes(0, 1), d_shift_two.swapaxes(0, 1), d_next[None], d_bias_next,
        d_gain_three, d_shift_three, d_head[None], d_bias_head.swapaxes(0, 1), d_table,
    )


def solution(mesh):
    rows = P("section", "batch")
    wide = P("section", "batch", None)
    matrix = P("section", None, None)
    vector = P("section", None)
    in_specs = (
        P("batch", None), wide, P("batch"), rows, rows, rows, rows, rows, wide, P(),
        matrix, matrix, matrix, vector, vector, P("section", None, None, None), matrix, matrix,
        matrix, vector, vector, vector, P("section", None, None, None), matrix,
    )
    columns = P("section", None, "batch")
    out_specs = (
        wide, wide, P("section"), columns, columns, columns, rows, rows,
        P("section", None, None, "batch"), columns, columns, wide, rows, rows, rows,
        P("section", None, "batch", None), matrix, P(),
    )
    devices = mesh.shape["batch"]
    fits = mesh.shape["section"] == 2 and devices in (2, 4, 8, 16)
    body = on_device_window if fits else on_device
    return jax.shard_map(
        body, mesh=mesh, in_specs=in_specs, out_specs=out_specs, check_vma=False
    )
```

```python
import functools

import jax
import jax.numpy as jnp
from jax import lax
from jax.experimental import pallas as pl
from jax.experimental.pallas import tpu as pltpu
from jax.sharding import PartitionSpec as P

F32 = jnp.float32
BF16 = jnp.bfloat16
GROUP = 8
RHO = 0.5
CONSISTENCY = 20.0
EPSILON = 1e-05
HIGH = lax.Precision.HIGHEST
LANES = 128
TILE = 256
CHUNK = 16
CAP = 20.0
VMEM_BYTES = 58 * 2**20
WINDOW_BYTES = 62 * 2**20


def dot(left, right, contract):
    return lax.dot_general(
        left, right, ((contract[:1], contract[1:]), ((), ())), preferred_element_type=F32
    )


def nn(left, right):
    return dot(left, right, (1, 0))


def nt(left, right):
    return dot(left, right, (1, 1))


def tn(left, right):
    return dot(left, right, (0, 0))


def norm_forward(pre, gain, shift, hidden, slope, unit, inverse, row):
    width = pre.shape[1]
    for start in range(0, TILE, CHUNK):
        out = slice(row + start, row + start + CHUNK)
        x = pre[start : start + CHUNK, :]
        x = x - jnp.sum(x, axis=-1, keepdims=True) * (1.0 / width)
        r = lax.rsqrt(jnp.sum(x * x, axis=-1, keepdims=True) * (1.0 / width) + EPSILON)
        if inverse is not None:
            inverse[out, :] = r
        for q in range(0, width, 256):
            cols = slice(q, q + 256)
            y = x[:, cols] * r
            v = y * gain[:, cols] + shift[:, cols]
            e = jnp.exp(jnp.minimum(v, CAP))
            k = e * (e + 2.0)
            d = 1.0 / (k + 2.0)
            t = k * d
            hidden[out, cols] = (v * t).astype(BF16)
            if slope is not None:
                slope[out, cols] = (t + (4.0 * v * d) * ((k - e) * d)).astype(BF16)
                unit[out, cols] = y.astype(BF16)


def norm_backward(grad, gain, slope, unit, inverse, result, gain_sum, shift_sum, row):
    width = grad.shape[1]
    gains = shifts = None
    for start in range(0, TILE, CHUNK):
        out = slice(row + start, row + start + CHUNK)
        y = unit[out, :].astype(F32)
        dv = grad[start : start + CHUNK, :] * slope[out, :].astype(F32)
        dvy = dv * y
        g = dvy[:8] + dvy[8:]
        s = dv[:8] + dv[8:]
        gains = g if gains is None else gains + g
        shifts = s if shifts is None else shifts + s
        row_gain = gain[...]
        dx = dv * row_gain
        mean = jnp.sum(dx, axis=-1, keepdims=True) * (1.0 / width)
        along = jnp.sum(dvy * row_gain, axis=-1, keepdims=True) * (1.0 / width)
        result[out, :] = ((dx - mean - y * along) * inverse[out, :]).astype(BF16)
    gain_sum[...] += gains
    shift_sum[...] += shifts


def group_matrix():
    i = lax.broadcasted_iota(jnp.int32, (256, 256), 0) // GROUP
    j = lax.broadcasted_iota(jnp.int32, (256, 256), 1) // GROUP
    return jnp.where(i == j, 1.0, 0.0).astype(BF16)


def group_sum(values, ones):
    parts = []
    for q in range(0, values.shape[1], 256):
        v = values[:, q : q + 256]
        high = v.astype(BF16)
        low = (v - high.astype(F32)).astype(BF16)
        parts.append(nn(high, ones) + nn(low, ones))
    return jnp.concatenate(parts, axis=1)


def simplex_forward(pre, gain, shift, ones):
    width = pre.shape[1]
    x = pre - jnp.sum(pre, axis=-1, keepdims=True) * (1.0 / width)
    r = lax.rsqrt(jnp.sum(x * x, axis=-1, keepdims=True) * (1.0 / width) + EPSILON)
    y = x * r
    e = jnp.exp(y * gain + shift)
    return y, r, e / group_sum(e, ones)


def tile_rows(i):
    return slice(i * TILE, (i + 1) * TILE)


def staged(count, first, then):
    first(0)
    for i in range(count):
        if i + 1 < count:
            first(i + 1)
        then(i)


def forward_pair(x, wl, wta, g1, s1, w2, g2, s2, pre, h1, m1, x1, r1, h2, m2, x2, r2):
    count = x.shape[0] // TILE
    latent = wl.shape[0]

    def one(i):
        r = tile_rows(i)
        pre[i][...] = nn(x[r, :latent], wl[...]) + nn(x[r, latent:], wta[...])

    def two(i):
        pre[i][...] = nn(h1[tile_rows(i), :], w2[...])

    staged(count, one, lambda i: norm_forward(pre[i], g1, s1, h1, m1, x1, r1, i * TILE))
    staged(count, two, lambda i: norm_forward(pre[i], g2, s2, h2, m2, x2, r2, i * TILE))


def backward_pair(
    x, wl, wta, g1, w2, g2, pre, m1, x1, r1, m2, x2, r2, d1, d2, back_in,
    dx, add_dx, dg1, ds1, dg2, ds2,
):
    count = x.shape[0] // TILE
    latent = wl.shape[0]

    def one(i):
        pre[i][...] = nt(d2[tile_rows(i), :], w2[...])

    staged(
        count, back_in, lambda i: norm_backward(pre[i], g2, m2, x2, r2, d2, dg2, ds2, i * TILE)
    )
    staged(count, one, lambda i: norm_backward(pre[i], g1, m1, x1, r1, d1, dg1, ds1, i * TILE))
    for i in range(count):
        r = tile_rows(i)
        main, side = nt(d1[r, :], wl[...]), nt(d1[r, :], wta[...])
        if add_dx:
            dx[r, :latent] += main
            dx[r, latent:] += side
        else:
            dx[r, :latent] = main
            dx[r, latent:] = side


def weight_grads(x, h1, d1, d2, tail_left, tail_right, u):
    hidden = h1.shape[1]
    width = x.shape[1]
    for n in range(0, hidden, 256):
        cols = slice(n, n + 256)
        u[cols, :hidden] = tn(d2[:, cols], h1[...]).astype(BF16)
        u[cols, hidden : hidden + width] = tn(d1[:, cols], x[...]).astype(BF16)
        u[cols, hidden + width :] = tn(tail_left[:, cols], tail_right[...]).astype(BF16)


def heads_kernel(
    x, wl, wta, g1, s1, w2, g2, s2, wh, bh, cond,
    u, dx, head_bias, loss, small,
    p0, p1, p2, logits, h1, h2, m1, m2, x1, x2, r1, r2, d1, d2, dl,
):
    pre = (p0, p1, p2)
    w2, wh, g1, s1, g2, s2, bh, cond, u = (
        ref.at[0] for ref in (w2, wh, g1, s1, g2, s2, bh, cond, u)
    )
    sums = [small.at[0, pl.ds(8 * i, 8)] for i in range(4)]
    small[...] = jnp.zeros_like(small)
    head_bias[...] = jnp.zeros_like(head_bias)

    @pl.when(pl.program_id(0) == 0)
    def _():
        dx[...] = jnp.zeros_like(dx)
        loss[...] = jnp.zeros_like(loss)

    forward_pair(x, wl, wta, g1, s1, w2, g2, s2, pre, h1, m1, x1, r1, h2, m2, x2, r2)

    def tail(i):
        r = tile_rows(i)
        v = nn(h2[r, :], wh[...]) + bh[...]
        given = cond[r, :]
        lower, upper, weight = given[:, 0:1], given[:, 1:2], given[:, 2:3]
        v = v - jnp.max(v, axis=-1, keepdims=True)
        e = jnp.exp(v)
        total = jnp.sum(e, axis=-1, keepdims=True)
        at = lax.broadcasted_iota(jnp.int32, v.shape, 1).astype(F32)
        hot = jnp.where(at == lower, 1.0 - upper, 0.0) + jnp.where(at == lower + 1.0, upper, 0.0)
        loss[r, :] += weight * (jnp.log(total) - jnp.sum(hot * v, axis=-1, keepdims=True))
        grad = (weight * (e / total - hot)).astype(BF16)
        dl[r, :] = grad
        head_bias[0, 0:1, :] += jnp.sum(grad.astype(F32), axis=0, keepdims=True)

    for i in range(x.shape[0] // TILE):
        tail(i)

    def back_in(i):
        pre[i][...] = nt(dl[tile_rows(i), :], wh[...])

    backward_pair(
        x, wl, wta, g1, w2, g2, pre, m1, x1, r1, m2, x2, r2, d1, d2, back_in, dx, True, *sums
    )
    weight_grads(x, h1, d1, d2, h2, dl, u)


def scratch(rows, hidden, forward=False):
    def hold():
        return pltpu.VMEM((rows, hidden), BF16)

    if forward:
        return [pltpu.VMEM((TILE, hidden), F32)] * 3 + [hold(), hold()]
    return (
        [pltpu.VMEM((TILE, hidden), F32)] * 3
        + [hold() for _ in range(6)]
        + [pltpu.VMEM((rows, 1), F32)] * 2
        + [hold(), hold()]
    )


def heads(x, w_latent, wta, g1, s1, w_hidden, g2, s2, wh, bh, cond):
    rows, width = x.shape
    latent = w_latent.shape[0]
    count, hidden = wh.shape[0], w_hidden.shape[-1]
    held = scratch(rows, hidden)
    row = pl.BlockSpec((1, 1, hidden), lambda k: (k + 1, 0, 0))
    return pl.pallas_call(
        heads_kernel,
        grid=(count,),
        in_specs=[
            pl.BlockSpec((rows, width), lambda k: (0, 0)),
            pl.BlockSpec((latent, hidden), lambda k: (0, k + 1)),
            pl.BlockSpec((LANES, hidden), lambda k: (0, k + 1)),
            row,
            row,
            pl.BlockSpec((1, hidden, hidden), lambda k: (k + 1, 0, 0)),
            row,
            row,
            pl.BlockSpec((1, hidden, LANES), lambda k: (k, 0, 0)),
            pl.BlockSpec((1, 1, LANES), lambda k: (k, 0, 0)),
            pl.BlockSpec((1, rows, 8), lambda k: (jnp.minimum(k, 1), 0, 0)),
        ],
        out_shape=[
            jax.ShapeDtypeStruct((count, hidden, hidden + width + LANES), BF16),
            jax.ShapeDtypeStruct((rows, width), F32),
            jax.ShapeDtypeStruct((count, 8, LANES), F32),
            jax.ShapeDtypeStruct((rows, 1), F32),
            jax.ShapeDtypeStruct((count, 32, hidden), F32),
        ],
        out_specs=[
            pl.BlockSpec((1, hidden, hidden + width + LANES), lambda k: (k, 0, 0)),
            pl.BlockSpec((rows, width), lambda k: (0, 0)),
            pl.BlockSpec((1, 8, LANES), lambda k: (k, 0, 0)),
            pl.BlockSpec((rows, 1), lambda k: (0, 0)),
            pl.BlockSpec((1, 32, hidden), lambda k: (k, 0, 0)),
        ],
        scratch_shapes=held[:3]
        + [pltpu.VMEM((rows, LANES), F32)]
        + held[3:]
        + [pltpu.VMEM((rows, LANES), BF16)],
        compiler_params=pltpu.CompilerParams(vmem_limit_bytes=VMEM_BYTES),
    )(x, w_latent, wta, g1, s1, w_hidden, g2, s2, wh, bh, cond)


def dynamics_specs(rows, width, latent, hidden):
    row = pl.BlockSpec((1, 1, hidden), lambda k: (0, 0, 0))
    short = pl.BlockSpec((1, latent), lambda k: (0, 0))
    return [
        pl.BlockSpec((rows, width), lambda k: (0, 0)),
        pl.BlockSpec((latent, hidden), lambda k: (0, 0)),
        pl.BlockSpec((LANES, hidden), lambda k: (0, 0)),
        row,
        row,
        pl.BlockSpec((1, hidden, hidden), lambda k: (0, 0, 0)),
        row,
        row,
        pl.BlockSpec((hidden, latent), lambda k: (0, 0)),
        short,
        short,
        short,
    ]


def rollout_kernel(
    x, wl, wta, g1, s1, w2, g2, s2, wn, bn, g3, s3, z_out, p0, p1, p2, h1, h2
):
    pre = (p0, p1, p2)
    w2, g1, s1, g2, s2 = (ref.at[0] for ref in (w2, g1, s1, g2, s2))
    ones = group_matrix()
    none = (None, None, None)
    forward_pair(x, wl, wta, g1, s1, w2, g2, s2, pre, h1, *none, h2, *none)
    for i in range(x.shape[0] // TILE):
        for start in range(i * TILE, (i + 1) * TILE, 64):
            r = slice(start, start + 64)
            v = nn(h2[r, :], wn[...]) + bn[...]
            z_out[r, :] = simplex_forward(v, g3[...], s3[...], ones)[2].astype(BF16)


def rollout(x, w_latent, wta, g1, s1, w_hidden, g2, s2, wn, bn, g3, s3):
    rows, width = x.shape
    latent, hidden = w_latent.shape[0], w_hidden.shape[-1]
    return pl.pallas_call(
        rollout_kernel,
        grid=(1,),
        in_specs=dynamics_specs(rows, width, latent, hidden),
        out_shape=jax.ShapeDtypeStruct((rows, latent), BF16),
        out_specs=pl.BlockSpec((rows, latent), lambda k: (0, 0)),
        scratch_shapes=scratch(rows, hidden, True),
        compiler_params=pltpu.CompilerParams(vmem_limit_bytes=VMEM_BYTES),
    )(x, w_latent, wta, g1, s1, w_hidden, g2, s2, wn, bn, g3, s3)


def dynamics_kernel(
    x, wl, wta, g1, s1, w2, g2, s2, wn, bn, g3, s3, goal, weights, upstream,
    u, dx, z_out, loss, small, small3,
    p0, p1, p2, pre3, h1, h2, m1, m2, x1, x2, r1, r2, d1, d2, d3,
):
    pre = (p0, p1, p2)
    w2, g1, s1, g2, s2 = (ref.at[0] for ref in (w2, g1, s1, g2, s2))
    sums = [small.at[pl.ds(8 * i, 8)] for i in range(4)]
    small[...] = jnp.zeros_like(small)
    ones = group_matrix()
    width = wn.shape[1]
    forward_pair(x, wl, wta, g1, s1, w2, g2, s2, pre, h1, m1, x1, r1, h2, m2, x2, r2)
    totals = [None, None, None]
    count = x.shape[0] // TILE
    for i in range(count):
        r = tile_rows(i)
        pre3[r, :] = nn(h2[r, :], wn[...]) + bn[...]
    for start in range(0, x.shape[0], 64):
        r = slice(start, start + 64)
        y, inverse, z = simplex_forward(pre3[r, :], g3[...], s3[...], ones)
        z_out[r, :] = z.astype(BF16)
        differ = z - goal[r, :].astype(F32)
        weight = weights[r, :]
        loss[r, :] = weight * (
            CONSISTENCY / width * jnp.sum(differ * differ, axis=-1, keepdims=True)
        )
        grad = upstream[r, :].astype(F32) + weight * (2.0 * CONSISTENCY / width) * differ
        grad = grad * z
        dv = grad - z * group_sum(grad, ones)
        dvy = dv * y
        dy = dv * g3[...]
        mean = jnp.sum(dy, axis=-1, keepdims=True) * (1.0 / width)
        along = jnp.sum(dy * y, axis=-1, keepdims=True) * (1.0 / width)
        result = ((dy - mean - y * along) * inverse).astype(BF16)
        d3[r, :] = result
        for q, part in enumerate((dvy, dv, result.astype(F32))):
            part = functools.reduce(jnp.add, [part[s : s + 8] for s in range(0, 64, 8)])
            totals[q] = part if totals[q] is None else totals[q] + part
    for q in range(3):
        small3[8 * q : 8 * q + 8, :] = totals[q]

    def back_in(i):
        pre[i][...] = nt(d3[tile_rows(i), :], wn[...])

    backward_pair(
        x, wl, wta, g1, w2, g2, pre, m1, x1, r1, m2, x2, r2, d1, d2, back_in, dx, False, *sums
    )
    weight_grads(x, h1, d1, d2, h2, d3, u)


def dynamics(
    x, w_latent, wta, g1, s1, w_hidden, g2, s2, wn, bn, g3, s3, goal, weights, upstream
):
    rows, width = x.shape
    latent, hidden = w_latent.shape[0], w_hidden.shape[-1]
    held = scratch(rows, hidden)

    def whole(shape):
        return pl.BlockSpec(shape, lambda k: (0, 0))

    shapes = [
        ((hidden, hidden + width + latent), BF16),
        ((rows, width), F32),
        ((rows, latent), BF16),
        ((rows, 1), F32),
        ((32, hidden), F32),
        ((24, latent), F32),
    ]
    return pl.pallas_call(
        dynamics_kernel,
        grid=(1,),
        in_specs=dynamics_specs(rows, width, latent, hidden)
        + [whole((rows, latent)), whole((rows, 1)), whole((rows, latent))],
        out_shape=[jax.ShapeDtypeStruct(*s) for s in shapes],
        out_specs=[whole(s[0]) for s in shapes],
        scratch_shapes=held[:3]
        + [pltpu.VMEM((rows, latent), F32)]
        + held[3:]
        + [pltpu.VMEM((rows, latent), BF16)],
        compiler_params=pltpu.CompilerParams(vmem_limit_bytes=VMEM_BYTES),
    )(x, w_latent, wta, g1, s1, w_hidden, g2, s2, wn, bn, g3, s3, goal, weights, upstream)


def on_device(
    latents, actions, tasks, masks, reward_bins, reward_frac, value_bins, value_frac, targets,
    task_table, w_latent, w_action, w_task, gain_one, shift_one, w_hidden, gain_two, shift_two,
    w_next, bias_next, gain_three, shift_three, w_head, bias_head,
):
    section = lax.axis_index("section")
    device = lax.axis_index("batch")
    devices = lax.axis_size("batch")
    sections = lax.axis_size("section")
    rows, latent = latents.shape
    branches, hidden = w_hidden.shape[1], w_hidden.shape[-1]
    heads_count, bins = w_head.shape[1], w_head.shape[-1]
    tasks_count, task_dim = task_table.shape
    act = actions.shape[-1]
    scale = 1.0 / (rows * devices)
    rho = jnp.where(section == 0, 1.0, RHO).astype(F32)
    spare = LANES - task_dim - act

    ids = lax.broadcasted_iota(jnp.int32, (1, tasks_count), 1)
    one_hot = (tasks[:, None] == ids).astype(BF16)
    embedded = nn(one_hot, task_table).astype(BF16)
    extra = jnp.concatenate([embedded, actions[0], jnp.zeros((rows, spare), BF16)], axis=1)
    wta = jnp.concatenate(
        [w_task[0], w_action[0], jnp.zeros((spare, branches * hidden), BF16)], axis=0
    )
    weight = rho * masks[0].astype(F32)
    wide = LANES - bins
    wh = jnp.pad(w_head[0], ((0, 0), (0, 0), (0, wide)))
    bh = jnp.pad(bias_head[0], ((0, 0), (0, wide)), constant_values=-1e30)[:, None, :]
    none = jnp.zeros((2, rows), F32)
    cond = jnp.stack(
        [
            jnp.stack([reward_bins[0], value_bins[0]]).astype(F32),
            jnp.stack([reward_frac[0], value_frac[0]]),
            jnp.stack([weight, weight / (heads_count - 1)]),
        ]
        + [none] * 5,
        axis=-1,
    )
    g1 = gain_one[0].reshape(branches, 1, hidden)
    s1 = shift_one[0].reshape(branches, 1, hidden)
    g2 = gain_two[0][:, None, :]
    s2 = shift_two[0][:, None, :]
    shared = (w_latent[0], wta, g1, s1, w_hidden[0], g2, s2)
    last = (w_next[0], bias_next, gain_three, shift_three)

    first = rollout(jnp.concatenate([latents, extra], axis=1), *shared, *last)
    received = lax.ppermute(first, "section", [(i, i + 1) for i in range(sections - 1)])
    x = jnp.concatenate([jnp.where(section == 0, latents, received), extra], axis=1)
    u_heads, dx_heads, head_bias, loss, small = heads(x, *shared, wh, bh, cond)

    def run(upstream):
        return tuple(
            dynamics(x, *shared, *last, targets[0], weight[:, None], upstream)
        )

    empty = jnp.zeros((rows, latent), BF16)
    shapes = jax.eval_shape(run, empty)
    done = lax.cond(
        section == sections - 1,
        lambda: run(empty),
        lambda: tuple(jnp.zeros(s.shape, s.dtype) for s in shapes),
    )
    back = (dx_heads[:, :latent] + done[1][:, :latent]).astype(BF16)
    upstream = lax.ppermute(back, "section", [(i + 1, i) for i in range(sections - 1)])
    u_next, dx_next, z_out, loss_next, small_next, small3 = lax.cond(
        section == sections - 1, lambda: done, lambda: run(upstream)
    )

    dx = dx_heads + dx_next
    grads = dx[:, :latent].astype(BF16)
    table = jnp.einsum(
        "rt,re->te", one_hot.astype(F32), dx[:, latent : latent + task_dim], precision=HIGH
    )
    loss_sum = jnp.sum(loss) + jnp.sum(loss_next)

    width = x.shape[1]
    sum_heads = lax.psum_scatter(u_heads, "batch", scatter_dimension=1, tiled=True).astype(F32)
    sum_next = lax.psum_scatter(u_next, "batch", scatter_dimension=0, tiled=True).astype(F32)
    part = hidden // devices
    layer_one = jnp.concatenate(
        [sum_next[None, :, hidden : hidden + width], sum_heads[:, :, hidden : hidden + width]]
    )
    blocks = []
    inverse = pow(branches, -1, devices)
    for slot in range(branches):
        owner = lax.rem((device - slot + devices * branches) * inverse, devices)
        chosen = (branches * owner + slot) // devices
        piece = lax.dynamic_index_in_dim(layer_one, chosen, 0, keepdims=False)
        route = [((branches * e + slot) % devices, e) for e in range(devices)]
        blocks.append(lax.ppermute(piece.astype(BF16), "batch", route).astype(F32))
    w_one = jnp.concatenate(blocks, axis=0).T * scale

    small = jnp.concatenate([small_next[None], small]).reshape(branches, 4, 8, hidden).sum(2)
    small3 = small3.reshape(3, 8, latent).sum(1)
    packed = jnp.concatenate(
        [
            small[:, 0].reshape(devices, -1),
            small[:, 1].reshape(devices, -1),
            small[:, 2].reshape(branches, devices, part).swapaxes(0, 1).reshape(devices, -1),
            small[:, 3].reshape(branches, devices, part).swapaxes(0, 1).reshape(devices, -1),
            small3.reshape(3, devices, -1).swapaxes(0, 1).reshape(devices, -1),
        ],
        axis=1,
    )
    packed = lax.psum_scatter(packed, "batch", scatter_dimension=0, tiled=True)[0] * scale
    one = branches * hidden // devices
    two = branches * part
    three = latent // devices
    parts = jnp.split(packed, [one, 2 * one, 2 * one + two, 2 * one + 2 * two])
    third = parts[4].reshape(3, three)

    head_bias_total, loss_total = lax.psum((head_bias[:, 0, :bins], loss_sum), "batch")
    table_total = lax.psum(table, ("section", "batch"))
    w_two = jnp.concatenate([sum_next[None, :, :hidden], sum_heads[:, :, :hidden]])
    return (
        z_out[None],
        grads[None],
        (loss_total * scale).reshape(1),
        w_one[None, :latent],
        w_one[None, latent + task_dim : latent + task_dim + act],
        w_one[None, latent : latent + task_dim],
        parts[0][None],
        parts[1][None],
        (w_two.swapaxes(1, 2) * scale)[None],
        parts[2].reshape(1, branches, part),
        parts[3].reshape(1, branches, part),
        (sum_next[:, hidden + width :] * scale)[None],
        third[2][None],
        third[0][None],
        third[1][None],
        (sum_heads[:, :, hidden + width : hidden + width + bins] * scale)[None],
        (head_bias_total * scale)[None],
        table_total * scale,
    )


PIECE = 256
GROUPS = ((0, 768), (768, 1024), (1024, 1792), (1792, 2304))
HEAD_GROUPS = 3
ALONG_Z = 1
EARLY = (0, 1)
LATE = (2, 3)
SMALL_AT = 104
LAGS = ((3, 5, 6, 9), (3, 5, 7, 9), (1, 4, 6, 8))
SLOTS = 3
EXTRA = 16
MESH = pl.DeviceIdType.MESH


def halving(group, bits):
    if group == ALONG_Z and bits > 2:
        return (0,) + tuple(range(2, bits)) + (1,)
    return tuple(range(bits))


def group_slots(group, slots):
    return slots if group < HEAD_GROUPS else 1


def window_kernel(
    devices, task_dim,
    z_in, acts_in, tasks_in, masks_in, reward_in, reward_part, value_in, value_part, table_in, wl_in, wt_in, wa_in, g1, s1, w2_in, g2, s2, wh_in, bh, wn_in, bn, g3, s3, goal_in,
    z_out, d_out, heads_out, next_out, one_out, all_out,
    x, w1, w2, wh_raw, wh, wn, goal, upstream, cond, table_wide, acts, wa, bias,
    p0, p1, p2, h1, h2, m1, m2, x1, x2, r1, r2, dl, dx, loss, head_bias, small, small3,
    group_ones, parts, r3, u, one_send, one_recv, every, every_recv, rb,
    load_sem, once_sem, send_sem, recv_sem, zs_sem, zr_sem, ds_sem, dr_sem, os_sem, or_sem, es_sem, er_sem,
):
    section = lax.axis_index("section")
    device = lax.axis_index("batch")
    rows, latent = z_in.shape
    hidden = w2.shape[-1]
    heads_count, bins = bh.shape[0], bh.shape[-1]
    branches = heads_count + 1
    count = rows // TILE
    part = hidden // devices
    bits = devices.bit_length() - 1
    pre = (p0, p1, p2)
    bit = [lax.rem(lax.div(device, 1 << b), 2) for b in range(bits)]
    other = (1 - section, device)

    def partner(b):
        return (section, device + (1 - 2 * bit[b]) * (1 << b))

    d3 = upstream
    barrier = pltpu.get_barrier_semaphore()
    for step in range(1, devices):
        to = (section, lax.rem(device + step, devices))
        pl.semaphore_signal(barrier, inc=1, device_id=to, device_id_type=MESH)
    pl.semaphore_signal(barrier, inc=1, device_id=other, device_id_type=MESH)

    def loads(branch, slot):
        cols = pl.ds(pl.multiple_of(branch * hidden, hidden), hidden)
        pairs = [
            (wl_in.at[:, cols], w1.at[slot, pl.ds(0, latent)]),
            (wt_in.at[:, cols], w1.at[slot, pl.ds(latent, task_dim)]),
            (w2_in.at[branch], w2.at[slot]),
        ]
        return [
            pltpu.make_async_copy(a, b, load_sem.at[slot, i]) for i, (a, b) in enumerate(pairs)
        ]

    def set_actions(branch, slot):
        cols = pl.ds(pl.multiple_of(branch * hidden, hidden), hidden)
        w1[slot, latent + task_dim :, :] = wa[:, cols]

    def load_head(head, slot):
        return pltpu.make_async_copy(wh_in.at[head], wh_raw.at[slot], load_sem.at[slot, 3])

    for copy in loads(0, 1):
        copy.start()
    first_z = pltpu.make_async_copy(
        z_in, x.at[pl.ds(0, rows), pl.ds(0, latent)], once_sem.at[0]
    )
    load_wn = pltpu.make_async_copy(wn_in, wn, once_sem.at[1])
    load_goal = pltpu.make_async_copy(goal_in, goal, once_sem.at[2])

    @pl.when(section == 0)
    def _():
        first_z.start()

    load_wn.start()
    load_goal.start()
    for copy in loads(1, 0):
        copy.start()
    load_head(0, 0).start()

    p0[...] = jnp.zeros_like(p0)
    rho = jnp.where(section == 0, 1.0, RHO)
    given = (
        reward_in[...].astype(F32), reward_part[...], value_in[...].astype(F32), value_part[...],
        rho * masks_in[...].astype(F32), tasks_in[...].astype(F32),
    )
    for i, value in enumerate(given):
        p0[i : i + 1, :rows] = value
    cond[...] = p0[:LANES, :rows].T
    acts_count = acts_in.shape[0]
    wa[...] = jnp.zeros_like(wa)
    wa[:acts_count, :] = wa_in[...]
    set_actions(0, 1)
    acts[...] = jnp.zeros_like(acts)
    acts[:acts_count, :] = acts_in[...]
    table_wide[...] = jnp.zeros_like(table_wide)
    table_wide[: table_in.shape[0], :task_dim] = table_in[...]
    bias[...] = jnp.full_like(bias, -1e30)
    for i in range(heads_count):
        bias[i : i + 1, :bins] = bh[i]
    lanes = lax.broadcasted_iota(jnp.int32, (16, LANES), 1)
    lane_row = lax.broadcasted_iota(jnp.int32, (16, LANES), 0)
    act_place = jnp.where(lanes == lane_row + task_dim, 1.0, 0.0).astype(BF16)

    def task_hot(i):
        at = lax.broadcasted_iota(jnp.int32, (TILE, LANES), 1).astype(F32)
        return jnp.where(at == cond[tile_rows(i), 5:6], 1.0, 0.0).astype(BF16)

    for i in range(count):
        r = tile_rows(i)
        x[r, latent:] = (nn(task_hot(i), table_wide[...]) + tn(acts[:, r], act_place)).astype(BF16)
    x[rows:, :latent] = jnp.zeros((EXTRA, latent), BF16)
    select = jnp.where(lanes == lane_row + SMALL_AT, 1.0, 0.0).astype(BF16)
    x[rows:, latent:] = select
    dl[rows:, :] = select
    wh[...] = jnp.zeros_like(wh)
    dx[...] = jnp.zeros_like(dx)
    loss[...] = jnp.zeros_like(loss)
    head_bias[...] = jnp.zeros_like(head_bias)

    @pl.when(section == 1)
    def _():
        upstream[...] = jnp.zeros_like(upstream)

    def pass_on(i):
        r = pl.ds(i * TILE, TILE)
        return pltpu.make_async_remote_copy(
            src_ref=z_out.at[r], dst_ref=x.at[r, pl.ds(0, latent)], send_sem=zs_sem.at[i], recv_sem=zr_sem.at[i],
            device_id=other, device_id_type=MESH,
        )

    def pass_back(i):
        r = pl.ds(i * TILE, TILE)
        return pltpu.make_async_remote_copy(
            src_ref=d_out.at[r], dst_ref=upstream.at[r], send_sem=ds_sem.at[i], recv_sem=dr_sem.at[i],
            device_id=other, device_id_type=MESH,
        )

    group_ones[:PIECE, :] = group_matrix()
    group_ones[PIECE:, :] = group_matrix()
    for copy in loads(0, 1):
        copy.wait()
    load_wn.wait()
    load_goal.wait()

    def layer_one(i, slot):
        r = tile_rows(i)
        pre[i][...] = nn(x[r, :], w1[slot])

    def layer_two(i, slot):
        pre[i][...] = nn(h1[tile_rows(i), :], w2[slot])

    def split(c, value):
        high = value.astype(BF16)
        low = (value - high.astype(F32)).astype(BF16)
        for q in range(latent // PIECE):
            cols = slice(q * PIECE, (q + 1) * PIECE)
            parts[c, 2 * q * PIECE : (2 * q + 1) * PIECE] = high[:, cols]
            parts[c, (2 * q + 1) * PIECE : (2 * q + 2) * PIECE] = low[:, cols]

    def group_sums(result):
        for q in range(latent // PIECE):
            cols = slice(2 * q * PIECE, 2 * (q + 1) * PIECE)
            result[:, q * PIECE : (q + 1) * PIECE] = nn(parts[:, cols], group_ones[...])

    def beside(i):
        other_pre = pre[(i + 1) % len(pre)]
        return other_pre.at[:, pl.ds(0, latent)], other_pre.at[:, pl.ds(latent, latent)]

    def simplex_start(i):
        unit3 = beside(i)[0]
        for start in range(0, TILE, CHUNK):
            c = slice(start, start + CHUNK)
            v = pre[i][c, :latent]
            v = v - jnp.sum(v, axis=-1, keepdims=True) * (1.0 / latent)
            r = lax.rsqrt(jnp.sum(v * v, axis=-1, keepdims=True) * (1.0 / latent) + EPSILON)
            y = v * r
            e = jnp.exp(y * g3[...] + s3[...])
            unit3[c, :] = y
            r3[c, :] = r
            pre[i][c, latent:] = e
            split(c, e)
        group_sums(pre[i].at[:, pl.ds(0, latent)])

    def roll(i):
        layer_one(i, 1)
        norm_forward(pre[i], g1.at[0], s1.at[0], h1, None, None, None, i * TILE)
        layer_two(i, 1)
        norm_forward(pre[i], g2.at[0], s2.at[0], h2, None, None, None, i * TILE)
        pre[i][:, :latent] = nn(h2[tile_rows(i), :], wn[...]) + bn[...]
        simplex_start(i)
        for start in range(0, TILE, CHUNK):
            c = slice(start, start + CHUNK)
            result = pre[i][c, latent:] / pre[i][c, :latent]
            z_out[i * TILE + start : i * TILE + start + CHUNK, :] = result.astype(BF16)

    @pl.when(section == 0)
    def _():
        first_z.wait()
        roll(0)

    pl.semaphore_wait(barrier, devices)

    @pl.when(section == 0)
    def _():
        pass_on(0).start()
        for i in range(1, count):
            roll(i)
            pass_on(i).start()

    def span(order, stage, take):
        half = hidden >> (stage + 1)
        at = sum(bit[order[i]] * (hidden >> (i + 1)) for i in range(stage)) + take * half
        return pl.ds(pl.multiple_of(at, half), half)

    def places(unit, group):
        if group < HEAD_GROUPS:
            return lax.rem(unit, SLOTS), lax.rem(unit, 2)
        return 0, 0

    def copy_of(unit, group, stage):
        order = halving(group, bits)
        at, to = places(unit, group)
        return pltpu.make_async_remote_copy(
            src_ref=u[group].at[at, span(order, stage, 1 - bit[order[stage]])],
            dst_ref=rb[group][stage].at[to],
            send_sem=send_sem.at[group, stage, to],
            recv_sem=recv_sem.at[group, stage, to],
            device_id=partner(order[stage]),
            device_id_type=MESH,
        )

    def take(unit, group, stage, result):
        copy = copy_of(unit, group, stage)
        copy.wait_recv()
        copy.wait_send()
        order = halving(group, bits)
        keep = span(order, stage, bit[order[stage]])
        at, to = places(unit, group)
        if stage + 1 < bits:
            u[group][at, keep, :] = u[group][at, keep, :] + rb[group][stage][to]
            copy_of(unit, group, stage + 1).start()
        else:
            value = u[group][at, keep, :].astype(F32) + rb[group][stage][to].astype(F32)
            result[:, GROUPS[group][0] : GROUPS[group][1]] = value

    def owner_of(branch):
        block = branch * devices + device
        return lax.div(block, branches), lax.rem(block, branches)

    def send_one(branch):
        to, slot = owner_of(branch)
        return to, pltpu.make_async_remote_copy(
            src_ref=one_send.at[branch], dst_ref=one_recv.at[slot],
            send_sem=os_sem.at[branch], recv_sem=or_sem.at[slot],
            device_id=(section, to), device_id_type=MESH,
        )

    def first_layer_done(branch, result):
        one_send[branch] = result[:, hidden : hidden + latent + LANES].astype(BF16)
        to, copy = send_one(branch)

        @pl.when(to != device)
        def _():
            copy.start()

        @pl.when(to == device)
        def _():
            one_recv[owner_of(branch)[1]] = one_send[branch]

    def service(step, group):
        for mine in range(HEAD_GROUPS):
            for stage in reversed(range(bits)):
                behind = LAGS[mine][stage] + mine - group
                if behind % HEAD_GROUPS:
                    continue
                unit = step - behind // HEAD_GROUPS

                def act(unit=unit, mine=mine, stage=stage):
                    take(unit, mine, stage, heads_out.at[unit])
                    if stage == bits - 1 and mine == HEAD_GROUPS - 1:
                        first_layer_done(unit + 1, heads_out.at[unit])

                pl.when((unit >= 0) & (unit < heads_count))(act)

    def put(unit, n, col, value):
        for group, (low, high) in enumerate(GROUPS):
            start, stop = max(col, low), min(col + value.shape[1], high)
            if start >= stop:
                continue
            order = halving(group, bits)
            slot = places(unit, group)[0]
            for q in range(PIECE // part):
                block = n // part + q
                at = sum(((block >> order[i]) & 1) << (bits - 1 - i) for i in range(bits)) * part
                u[group][slot, at : at + part, start - low : stop - low] = value[
                    q * part : (q + 1) * part, start - col : stop - col
                ].astype(BF16)

    def put_hidden(unit):
        for n in range(0, hidden, PIECE):
            put(unit, n, 0, tn(m2[:rows, n : n + PIECE], h1[...]))

    def put_first(unit):
        m1[rows:, :] = small[0:EXTRA, :].astype(BF16)
        for n in range(0, hidden, PIECE):
            put(unit, n, hidden, tn(m1[:, n : n + PIECE], x[...]))

    def send_groups(unit, groups):
        for group in groups:
            copy_of(unit, group, 0).start()

    sums = [small.at[pl.ds(8 * i, 8)] for i in range(4)]

    def stages(slot, branch):
        one, two = (g1.at[branch], s1.at[branch]), (g2.at[branch], s2.at[branch])

        def back_one(i):
            pre[i][...] = nt(m2[tile_rows(i), :], w2[slot])

        def inputs(i):
            dx[tile_rows(i), :] += nt(m1[tile_rows(i), :], w1[slot])

        return dict(
            f1=lambda i: layer_one(i, slot),
            v1=lambda i: norm_forward(pre[i], *one, h1, m1, x1, r1, i * TILE),
            f2=lambda i: layer_two(i, slot),
            v2=lambda i: norm_forward(pre[i], *two, h2, m2, x2, r2, i * TILE),
            n2=lambda i: norm_backward(pre[i], two[0], m2, x2, r2, m2, sums[2], sums[3], i * TILE),
            b1=back_one,
            n1=lambda i: norm_backward(pre[i], one[0], m1, x1, r1, m1, sums[0], sums[1], i * TILE),
            dx=inputs,
        )

    def forward_stages(at):
        at["f1"](0)
        for i in range(count):
            if i + 1 < count:
                at["f1"](i + 1)
            else:
                at["f2"](0)
            at["v1"](i)
        for i in range(1, count):
            at["f2"](i)
            at["v2"](i - 1)
        at["v2"](count - 1)

    def head_tail(r, step):
        v = nt(h2[r, :], wh[...]) + bias[pl.ds(step, 1), :]
        given = cond[r, :]
        is_first = (step == 0).astype(F32)
        pick = lambda a, b: a * is_first + b * (1.0 - is_first)
        lower, upper = pick(given[:, 0:1], given[:, 2:3]), pick(given[:, 1:2], given[:, 3:4])
        weight = given[:, 4:5] * pick(1.0, 1.0 / (heads_count - 1))
        v = v - jnp.max(v, axis=-1, keepdims=True)
        e = jnp.exp(v)
        total = jnp.sum(e, axis=-1, keepdims=True)
        at = lax.broadcasted_iota(jnp.int32, v.shape, 1).astype(F32)
        hot = jnp.where(at == lower, 1.0 - upper, 0.0) + jnp.where(at == lower + 1.0, upper, 0.0)
        lost = weight * (jnp.log(total) - jnp.sum(hot * v, axis=-1, keepdims=True))
        loss[0:1, :] += jnp.sum(lost, axis=0, keepdims=True)
        grad = (weight * (e / total - hot)).astype(BF16)
        dl[r, :] = grad
        return jnp.sum(grad.astype(F32), axis=0, keepdims=True)

    @pl.when(section == 1)
    def _():
        for i in range(count):
            pass_on(i).wait_recv()

    def head(step, carry):
        slot = lax.rem(step, 2)
        branch = step + 1
        for copy in loads(branch, slot):
            copy.wait()
        load_head(step, slot).wait()
        at = stages(slot, branch)
        wh[:bins, :] = wh_raw[slot]
        set_actions(branch, slot)
        for copy in loads(lax.rem(branch + 1, branches), 1 - slot):
            copy.start()

        @pl.when(step + 1 < heads_count)
        def _():
            load_head(step + 1, 1 - slot).start()

        small[...] = jnp.zeros_like(small)
        forward_stages(at)
        biases = [head_tail(tile_rows(i), step) for i in range(count)]
        head_bias[pl.ds(step, 1), :] = functools.reduce(jnp.add, biases)
        service(step, 0)

        def back_in(i):
            pre[i][...] = nn(dl[tile_rows(i), :], wh[...])

        back_in(0)
        for i in range(count):
            if i + 1 < count:
                back_in(i + 1)
            else:
                at["b1"](0)
            at["n2"](i)
        for i in range(1, count):
            at["b1"](i)
            at["n1"](i - 1)
        at["dx"](0)
        at["n1"](count - 1)
        for i in range(1, count):
            at["dx"](i)
        service(step, 1)
        put_hidden(step)
        send_groups(step, (0, 1))
        put_first(step)
        h2[rows:, :] = small[EXTRA : 2 * EXTRA, :].astype(BF16)
        for n in range(0, hidden, PIECE):
            put(step, n, hidden + latent + LANES, tn(h2[:, n : n + PIECE], dl[...]))
        service(step, 2)
        send_groups(step, (2,))
        return carry

    lax.fori_loop(0, heads_count, head, 0)

    def rest(start, stop):
        def body(step, carry):
            for group in range(HEAD_GROUPS):
                service(step, group)
            return carry

        lax.fori_loop(start, stop, body, 0)

    @pl.when(section == 0)
    def _():
        for i in range(count):
            pass_on(i).wait_send()
        rest(heads_count, heads_count + 3)

    slot_next = heads_count % 2
    last_unit = SLOTS * -(-heads_count // SLOTS)
    assert last_unit == heads_count

    def dynamics_branch():
        for copy in loads(0, slot_next):
            copy.wait()
        set_actions(0, slot_next)
        small[...] = jnp.zeros_like(small)
        at = stages(slot_next, 0)
        forward_stages(at)

        width = latent
        small3[...] = jnp.zeros_like(small3)
        for i in range(count):

            @pl.when(section == 0)
            def _(i=i):
                pass_back(i).wait_recv()

            unit3, sums3 = beside(i)
            pre[i][:, :latent] = nn(h2[tile_rows(i), :], wn[...]) + bn[...]
            simplex_start(i)
            for start in range(0, TILE, CHUNK):
                c = slice(start, start + CHUNK)
                r = slice(i * TILE + start, i * TILE + start + CHUNK)
                zz = pre[i][c, latent:] / pre[i][c, :latent]
                z_out[r, :] = zz.astype(BF16)
                differ = zz - goal[r, :].astype(F32)
                weight = cond[r, 4:5]
                loss[...] += weight * (
                    CONSISTENCY / width * jnp.sum(differ * differ, axis=-1, keepdims=True)
                )
                grad = upstream[r, :].astype(F32) + weight * (2.0 * CONSISTENCY / width) * differ
                grad = grad * zz
                pre[i][c, latent:] = zz
                pre[i][c, :latent] = grad
                split(c, grad)
            group_sums(sums3)
            totals = [None, None, None]
            for start in range(0, TILE, CHUNK):
                c = slice(start, start + CHUNK)
                r = slice(i * TILE + start, i * TILE + start + CHUNK)
                y = unit3[c, :]
                dv = pre[i][c, :latent] - pre[i][c, latent:] * sums3[c, :]
                dvy = dv * y
                dy = dv * g3[...]
                mean = jnp.sum(dy, axis=-1, keepdims=True) * (1.0 / width)
                along = jnp.sum(dy * y, axis=-1, keepdims=True) * (1.0 / width)
                result = ((dy - mean - y * along) * r3[c, :]).astype(BF16)
                d3[r, :] = result
                for q, value in enumerate((dvy, dv, result.astype(F32))):
                    value = value[:8] + value[8:]
                    totals[q] = value if totals[q] is None else totals[q] + value
            for q in range(3):
                small3[8 * q : 8 * q + 8, :] += totals[q]

        def back_in(i):
            pre[i][...] = nt(d3[tile_rows(i), :], wn[...])

        back_in(0)
        for i in range(count):
            if i + 1 < count:
                back_in(i + 1)
            at["n2"](i)

        def put_next():
            for n in range(0, hidden, PIECE):
                put(last_unit, n, GROUPS[3][0], tn(h2[:rows, n : n + PIECE], d3[...]))
            send_groups(last_unit, (3,))
            put_hidden(last_unit)
            send_groups(last_unit, (0, 1))

        def input_grads():
            for i in range(count):
                at["dx"](i)
                d_out[tile_rows(i), :] = dx[tile_rows(i), :latent].astype(BF16)

                @pl.when(section == 1)
                def _(i=i):
                    pass_back(i).start()

        pl.when(section == 0)(put_next)
        at["b1"](0)
        for i in range(count):
            if i + 1 < count:
                at["b1"](i + 1)
            at["n1"](i)

        @pl.when(section == 0)
        def _():
            for group in EARLY:
                take(last_unit, group, 0, None)

        @pl.when(section == 1)
        def _():
            input_grads()
            for point in range(HEAD_GROUPS):
                service(heads_count, point)
            put_next()

        put_first(last_unit)
        third = latent // devices
        h2[rows:, :] = small[EXTRA : 2 * EXTRA, :].astype(BF16)
        for n in range(0, hidden, PIECE):
            at_row = lax.broadcasted_iota(jnp.int32, (PIECE, latent), 0) + n
            spot = (at_row // part) * third + (at_row % part) % third
            place = jnp.where(lax.broadcasted_iota(jnp.int32, (PIECE, latent), 1) == spot, 1.0, 0.0)
            side = nt(place.astype(BF16), small3[...].astype(BF16))
            side = side + tn(h2[rows:, n : n + PIECE], dl[rows:, :])
            put(last_unit, n, hidden + latent + LANES, side)
        send_groups(last_unit, (2,))
        pl.when(section == 0)(input_grads)

    def turn(t, carry):
        pl.when(section == 1 - t)(dynamics_branch)
        return carry

    lax.fori_loop(0, 2, turn, 0)

    @pl.when(section == 1)
    def _():
        rest(heads_count + 1, heads_count + 3)
        for group in EARLY:
            take(last_unit, group, 0, None)

    table_rows = every.shape[1] - 16
    table = jnp.zeros((LANES, LANES), F32)
    for i in range(count):
        r = tile_rows(i)
        hot = task_hot(i)
        value = dx[r, latent:]
        high = value.astype(BF16)
        middle = (value - high.astype(F32)).astype(BF16)
        table = table + (tn(hot, high) + tn(hot, middle))
    every[0, :table_rows, :] = table[:table_rows]
    every[0, table_rows : table_rows + 8, :] = head_bias[...]
    every[0, table_rows + 8 :, :] = jnp.broadcast_to(
        jnp.sum(loss[...], axis=0, keepdims=True), (8, LANES)
    )

    def exchange(step):
        to = partner(step) if step < bits else other
        return pltpu.make_async_remote_copy(
            src_ref=every.at[step], dst_ref=every_recv.at[step],
            send_sem=es_sem.at[step], recv_sem=er_sem.at[step],
            device_id=to, device_id_type=MESH,
        )

    exchange(0).start()
    swaps = 0

    def swap(step):
        exchange(step).wait_recv()
        every[step + 1] = every[step] + every_recv[step]
        if step < bits:
            exchange(step + 1).start()

    for group in LATE:
        take(last_unit, group, 0, None)
    order = EARLY + LATE
    for turn_at in range(len(order) + bits - 2):
        for stage in reversed(range(1, bits)):
            if 0 <= turn_at - stage + 1 < len(order):
                group = order[turn_at - stage + 1]
                take(last_unit, group, stage, next_out)
                if stage == bits - 1 and group == HEAD_GROUPS - 1:
                    first_layer_done(0, next_out)
        if swaps <= bits:
            swap(swaps)
            swaps += 1
    for step in range(swaps, bits + 1):
        swap(step)
    all_out[:table_rows, :] = every[bits + 1, :table_rows, :]
    all_out[table_rows:, :] = every[bits, table_rows:, :]

    for slot in range(branches):
        source = lax.rem(device * branches + slot, devices)

        @pl.when(source != device)
        def _(slot=slot):
            pltpu.make_async_remote_copy(
                src_ref=one_send.at[0], dst_ref=one_recv.at[slot],
                send_sem=os_sem.at[0], recv_sem=or_sem.at[slot],
                device_id=other, device_id_type=MESH,
            ).wait_recv()

    for branch in range(branches):
        to, copy = send_one(branch)

        @pl.when(to != device)
        def _(copy=copy):
            copy.wait_send()

    take_out = pltpu.make_async_copy(one_recv, one_out, once_sem.at[0])
    take_out.start()
    take_out.wait()
    for step in range(bits + 1):
        exchange(step).wait_send()

    @pl.when(section == 1)
    def _():
        for i in range(count):
            pass_back(i).wait_send()


def window(devices, latents, acts, *given):
    (tasks, masks, reward, reward_part, value, value_part, table, w_latent, w_task, w_act,
     g1, s1, w_hidden, g2, s2, w_head, bh, w_next, bn, g3, s3, goal) = given
    rows, latent = latents.shape
    hidden = w_hidden.shape[-1]
    heads_count, bins = bh.shape[0], bh.shape[-1]
    branches = heads_count + 1
    part = hidden // devices
    bits = devices.bit_length() - 1
    count = rows // TILE
    task_dim = table.shape[1]
    table_rows = -(-table.shape[0] // 8) * 8
    vm, dma = pltpu.VMEM, pltpu.SemaphoreType.DMA
    inner = pl.BlockSpec(memory_space=pltpu.VMEM)
    outer = pl.BlockSpec(memory_space=pl.ANY)
    tall = (rows + EXTRA, hidden)
    scratch_shapes = (
        [
            vm((rows + EXTRA, latent + LANES), BF16),
            vm((2, latent + LANES, hidden), BF16),
            vm((2, hidden, hidden), BF16),
            vm((2, bins, hidden), BF16),
            vm((LANES, hidden), BF16),
            vm((hidden, latent), BF16),
            vm((rows, latent), BF16),
            vm((rows, latent), BF16),
            vm((rows, LANES), F32),
            vm((LANES, LANES), BF16),
            vm((16, rows), BF16),
            vm((LANES - task_dim, branches * hidden), BF16),
            vm((8, LANES), F32),
        ]
        + [vm((TILE, hidden), F32)] * 3
        + [vm((rows, hidden), BF16), vm(tall, BF16), vm(tall, BF16)]
        + [vm((rows, hidden), BF16)] * 3
        + [vm((rows, 1), F32)] * 2
        + [
            vm((rows + EXTRA, LANES), BF16),
            vm((rows, latent + LANES), F32),
            vm((CHUNK, 1), F32),
            vm((8, LANES), F32),
            vm((32, hidden), F32),
            vm((LANES, latent), F32),
            vm((2 * PIECE, PIECE), BF16),
            vm((TILE, 2 * latent), BF16),
            vm((TILE, 1), F32),
            [
                vm((group_slots(g, SLOTS), hidden, high - low), BF16)
                for g, (low, high) in enumerate(GROUPS)
            ],
            vm((branches, part, latent + LANES), BF16),
            vm((branches, part, latent + LANES), BF16),
            vm((bits + 2, table_rows + 16, LANES), F32),
            vm((bits + 1, table_rows + 16, LANES), F32),
            [
                [
                    vm((group_slots(g, 2), hidden >> (s + 1), high - low), BF16)
                    for s in range(bits)
                ]
                for g, (low, high) in enumerate(GROUPS)
            ],
            dma((2, 4)),
            dma((3,)),
            dma((len(GROUPS), bits, 2)),
            dma((len(GROUPS), bits, 2)),
        ]
        + [dma((count,))] * 4
        + [dma((branches,))] * 2
        + [dma((bits + 1,))] * 2
    )
    shapes = [
        ((rows, latent), BF16),
        ((rows, latent), BF16),
        ((heads_count, part, GROUPS[HEAD_GROUPS - 1][1]), F32),
        ((part, GROUPS[-1][1]), F32),
        ((branches, part, latent + LANES), BF16),
        ((table_rows + 16, LANES), F32),
    ]
    return pl.pallas_call(
        functools.partial(window_kernel, devices, task_dim),
        out_shape=[jax.ShapeDtypeStruct(*s) for s in shapes],
        in_specs=[
            outer, inner, inner, inner, inner, inner, inner, inner, inner, outer, outer, inner,
            inner, inner, outer, inner, inner, outer, inner, outer, inner, inner, inner, outer,
        ],
        out_specs=[inner] * 4 + [outer, inner],
        scratch_shapes=scratch_shapes,
        compiler_params=pltpu.CompilerParams(
            collective_id=0, has_side_effects=True, vmem_limit_bytes=WINDOW_BYTES
        ),
    )(latents, acts, *given)


def finish_kernel(
    scale, task_dim,
    z_in, d_in, heads_in, next_in, one_in, every,
    z_out, d_out, loss, w_latent, w_action, w_task, gain_one, shift_one, w_hidden, gain_two, shift_two,
    w_next, bias_next, gain_three, shift_three, w_head, bias_head, table,
    flip_one, flip_two,
):
    branches, part, width = one_in.shape
    latent = width - LANES
    acts, bins = w_action.shape[0], w_head.shape[-1]
    all_rows = branches * part
    heads_count = branches - 1
    hidden = w_hidden.shape[-1]
    side = hidden + width
    table_rows = every.shape[0] - 16
    z_out[...] = z_in[...]
    d_out[...] = d_in[...]
    flip_one[...] = jnp.zeros_like(flip_one)
    flip_two[...] = jnp.zeros_like(flip_two)
    for k in range(branches):
        rows = slice(k * part, (k + 1) * part)
        source = next_in if k == 0 else heads_in.at[k - 1]
        w_hidden[k] = source[:, :hidden] * scale
        w_latent[rows, :] = one_in[k, :, :latent].astype(F32) * scale
        flip_one[rows, :] = one_in[k, :, latent:].astype(F32) * scale
        flip_two[rows, :] = source[:, side : side + LANES] * scale
        if k > 0:
            w_head[k - 1] = source[:, side : side + bins] * scale
            bias_head[k - 1] = every[table_rows + k - 1 : table_rows + k, :bins] * scale
    one = flip_one[...].T
    w_task[...] = one[:task_dim, :all_rows]
    for a in range(acts):
        w_action[a] = one[task_dim + a : task_dim + a + 1, :all_rows]

    def total(value, start):
        return jnp.sum(value[start : start + 8], axis=0, keepdims=True)

    gain_one[...] = total(one, SMALL_AT)[:, :all_rows]
    shift_one[...] = total(one, SMALL_AT + 8)[:, :all_rows]
    two = flip_two[...].T
    gains, shifts = total(two, SMALL_AT), total(two, SMALL_AT + 8)
    for k in range(branches):
        gain_two[k] = gains[:, k * part : (k + 1) * part]
        shift_two[k] = shifts[:, k * part : (k + 1) * part]
    third = gain_three.shape[1]
    gain_three[...] = total(two, 0)[:, :third]
    shift_three[...] = total(two, 8)[:, :third]
    bias_next[...] = total(two, 16)[:, :third]
    w_next[...] = next_in[:, side + LANES :] * scale
    loss[...] = every[table_rows + 8 : table_rows + 9, 0:1] * scale
    table[...] = every[: table.shape[0], :task_dim] * scale


def on_device_window(
    latents, actions, tasks, masks, reward_bins, reward_frac, value_bins, value_frac, targets,
    task_table, w_latent, w_action, w_task, gain_one, shift_one, w_hidden, gain_two, shift_two,
    w_next, bias_next, gain_three, shift_three, w_head, bias_head,
):
    devices = lax.axis_size("batch")
    rows, latent = latents.shape
    branches, hidden = w_hidden.shape[1], w_hidden.shape[-1]
    heads_count, bins = w_head.shape[1], w_head.shape[-1]
    tasks_count, task_dim = task_table.shape
    act = actions.shape[-1]
    part = hidden // devices
    raw = window(
        devices, latents, actions[0].T, tasks[None], masks, reward_bins, reward_frac, value_bins,
        value_frac, task_table, w_latent[0], w_task[0], w_action[0],
        gain_one[0].reshape(branches, 1, hidden), shift_one[0].reshape(branches, 1, hidden),
        w_hidden[0], gain_two[0][:, None, :], shift_two[0][:, None, :],
        w_head[0].swapaxes(1, 2), bias_head[0][:, None, :],
        w_next[0], bias_next, gain_three, shift_three, targets[0],
    )
    one = branches * part
    third = latent // devices
    shapes = [
        ((rows, latent), BF16), ((rows, latent), BF16), ((1, 1), F32), ((one, latent), F32),
        ((act, 1, one), F32), ((task_dim, one), F32), ((1, one), F32), ((1, one), F32),
        ((branches, part, hidden), F32), ((branches, 1, part), F32), ((branches, 1, part), F32),
        ((part, latent), F32), ((1, third), F32), ((1, third), F32), ((1, third), F32),
        ((heads_count, part, bins), F32), ((heads_count, 1, bins), F32), ((tasks_count, task_dim), F32),
    ]
    inner = pl.BlockSpec(memory_space=pltpu.VMEM)
    flipped = pltpu.VMEM((-(-one // LANES) * LANES, LANES), F32)
    (z_out, grads, loss, d_latent, d_action, d_task, d_gain_one, d_shift_one, d_hidden,
     d_gain_two, d_shift_two, d_next, d_bias_next, d_gain_three, d_shift_three, d_head,
     d_bias_head, d_table) = pl.pallas_call(
        functools.partial(finish_kernel, 1.0 / (rows * devices), task_dim),
        out_shape=[jax.ShapeDtypeStruct(*s) for s in shapes],
        in_specs=[inner] * len(raw),
        out_specs=[inner] * len(shapes),
        scratch_shapes=[flipped, flipped],
        compiler_params=pltpu.CompilerParams(vmem_limit_bytes=VMEM_BYTES),
    )(*raw)
    return (
        z_out[None], grads[None], loss.reshape(1), d_latent.T[None], d_action.swapaxes(0, 1),
        d_task[None], d_gain_one, d_shift_one, d_hidden.swapaxes(1, 2)[None],
        d_gain_two.swapaxes(0, 1), d_shift_two.swapaxes(0, 1), d_next[None], d_bias_next,
        d_gain_three, d_shift_three, d_head[None], d_bias_head.swapaxes(0, 1), d_table,
    )


def solution(mesh):
    rows = P("section", "batch")
    wide = P("section", "batch", None)
    matrix = P("section", None, None)
    vector = P("section", None)
    in_specs = (
        P("batch", None), wide, P("batch"), rows, rows, rows, rows, rows, wide, P(),
        matrix, matrix, matrix, vector, vector, P("section", None, None, None), matrix, matrix,
        matrix, vector, vector, vector, P("section", None, None, None), matrix,
    )
    columns = P("section", None, "batch")
    out_specs = (
        wide, wide, P("section"), columns, columns, columns, rows, rows,
        P("section", None, None, "batch"), columns, columns, wide, rows, rows, rows,
        P("section", None, "batch", None), matrix, P(),
    )
    devices = mesh.shape["batch"]
    fits = mesh.shape["section"] == 2 and devices in (2, 4, 8, 16)
    body = on_device_window if fits else on_device
    return jax.shard_map(
        body, mesh=mesh, in_specs=in_specs, out_specs=out_specs, check_vma=False
    )
```
